32 devices in a mesh: grp: 4 (over y, x), tile: 8 (over z, core).
Axes of the slice: x: 2, y: 2, z: 4, core: 2. Of those that a mesh axis runs over, the one named last changes fastest.
Arguments:
- base_velocity: float32 [2, 256, 1024], P(None, 'grp', 'tile'), may hold values from -6 to 6
- viscosity: float32 [256, 1024], P('grp', 'tile'), may hold values from 0.5 to 2
- friction: float32 [256, 1024], P('grp', 'tile'), may hold values from 2 to 8
- friction_probe: float32 [256, 1024], P('grp', 'tile'), may hold values from -6 to 6
- pixel_los: float32 [4, 8, 2, 512], P('grp', 'tile'), may hold values from -6 to 6
- pixel_weight: float32 [4, 8, 1, 512], P('grp', 'tile'), may hold values from 2 to 20
- pixel_cell: int32 [4, 8, 1, 512], P('grp', 'tile'), may hold values from 0 to 8191
- pixel_count: int32 [4, 8, 1, 8], P('grp', 'tile'), may hold values from 8 to 64, as said below
- panels: bfloat16 [128, 256, 1024], P('grp', None, 'tile'), may hold values from -0.015625 to 0.015625
Outputs:
- increment: float32 [2, 256, 1024], P(None, 'grp', 'tile')
- hessian_probe: float32 [256, 1024], P('grp', 'tile')
- coefficients: float32 [128], replicated
The draws below stay inside these ranges and needn't reach their ends.
Inputs may be any that keep to these rules, and one draw needn't show every extreme that they name: In group g, tile s uses the first pixel_count[g, s, 0, o] of its 64 slots toward owner tile o; in every group some owner receives 64 from every tile, and such owners are a few times busier than the mean. `pixel_cell`: cells are numbered row by row within the owner's block of 64 x 128 cells.
All inputs are finite; a program needn't handle non-finite values.
Results may differ from the reference program's by a relative error of at most 0.0036.
Values may be sent and summed in bfloat16 or wider, within the bound.
No kernel may reach another device: no remote copies, remote signals or barrier semaphores. Data moves between devices by JAX's collectives and lax.ppermute only.
A program may use at most 64 MiB of HBM per device.

```python
import math
import jax
import jax.numpy as jnp

CX = 64
CY = 128
CAP = 64
K = 128
SWEEPS = 8
NX = 256
NY = 1024
SLOTS = 512
N_GRP = 4
N_TILE = 8


def draw_pixel_count(key, part):
    key = jax.random.fold_in(key, 7)
    key_base, key_hot, key_forced = jax.random.split(key, 3)
    base = jax.random.randint(key_base, (N_GRP, N_TILE, 1, N_TILE), CAP // 8, CAP // 2 + 1)
    busy = jax.random.randint(key_hot, (N_GRP, 1, 1, N_TILE), 0, 8) == 0
    forced = jax.random.randint(key_forced, (N_GRP, 1, 1, 1), 0, N_TILE)
    busy = busy | (jnp.arange(N_TILE)[None, None, None, :] == forced)
    return jnp.where(busy, CAP, base).astype(jnp.int32)


def plant(entries, own_key, smallest, top_value):
    longest = entries.shape.index(max(entries.shape))
    spots = []
    for shift in (0, 1):
        where = [jax.random.randint(jax.random.fold_in(own_key, axis), (), 0, length) for axis, length in enumerate(entries.shape)]
        where[longest] = (where[longest] + shift) % entries.shape[longest]
        spots.append(tuple(where))
    return entries.at[spots[0]].set(smallest).at[spots[1]].set(top_value)


def strengthened(entries, stream_key, source, target, blocks, factor):
    def block_of(position):
        return (jnp.arange(entries.shape[position]) // (entries.shape[position] // blocks)).reshape((-1,) + (1,) * (entries.ndim - 1 - position))

    near = jax.random.permutation(stream_key, blocks)[block_of(target)]
    far = (block_of(target) + blocks // 2) % blocks
    return jnp.where((block_of(source) == near) | (block_of(source) == far), factor * entries, entries)


def level_of(key, extent, cuts, low, high):
    gain = 1.0
    for dim, blocks in cuts:
        draws = jax.random.uniform(jax.random.fold_in(jax.random.fold_in(key, 6), dim), (blocks,), jnp.float32, low / len(cuts), high / len(cuts))
        gain = gain * jnp.repeat(jnp.exp(draws), extent[dim] // blocks).reshape((-1,) + (1,) * (len(extent) - 1 - dim))
    return gain


def gaussian(rng, shape, width, limit, cuts=(), kind=jnp.bfloat16):
    result = width * jax.random.normal(rng, shape, jnp.float32)
    if cuts:
        result = result * level_of(rng, shape, cuts, -0.22, 0.18)
    return jnp.clip(result, -limit, limit).astype(kind)


def bell_draw_with(stream_key, shape, width, most, pieces, heavy, kind=jnp.bfloat16):
    values = width * jax.random.normal(stream_key, shape, jnp.float32)
    if pieces:
        values = values * level_of(stream_key, shape, pieces, -0.22, 0.18)
    return jnp.clip(strengthened(values, jax.random.fold_in(stream_key, 3), *heavy), -most, most).astype(kind)


def setup_inputs(seed: int = 0) -> dict:
    splits = jax.random.split(jax.random.key(seed), 10)
    return {
        "base_velocity": gaussian(splits[0], (2, NX, NY), 1.0, 6.0, ((1, 4), (2, 8)), jnp.float32),
        "viscosity": jnp.clip(jnp.exp(math.log(2.0) - 1.3862944 * jax.random.uniform(splits[1], (NX, NY), jnp.float32) ** level_of(splits[1], (NX, NY), ((0, 4), (1, 8)), -0.2, 0.2)), 0.5, 2.0),
        "friction": jnp.clip(jnp.exp(math.log(8.0) - 1.3862944 * jax.random.uniform(splits[2], (NX, NY), jnp.float32) ** level_of(splits[2], (NX, NY), ((0, 4), (1, 8)), -0.2, 0.2)), 2.0, 8.0),
        "friction_probe": gaussian(splits[3], (NX, NY), 1.0, 6.0, ((0, 4), (1, 8)), jnp.float32),
        "pixel_los": gaussian(splits[4], (N_GRP, N_TILE, 2, SLOTS), 1.0, 6.0, ((0, 4), (1, 8)), jnp.float32),
        "pixel_weight": jnp.clip(jnp.exp(math.log(20.0) - 2.3025851 * jax.random.uniform(splits[5], (N_GRP, N_TILE, 1, SLOTS), jnp.float32) ** level_of(splits[5], (N_GRP, N_TILE, 1, SLOTS), ((0, 4), (1, 8)), -0.2, 0.2)), 2.0, 20.0),
        "pixel_cell": plant(jax.random.randint(splits[6], (N_GRP, N_TILE, 1, SLOTS), 0, CX * CY), jax.random.fold_in(splits[6], 1), 0, (CX * CY) - 1).astype(jnp.int32),
        "pixel_count": draw_pixel_count(jax.random.fold_in(splits[9], 71), 0),
        "panels": bell_draw_with(splits[8], (K, NX, NY), (NX * NY) ** -0.5, 0.015625, ((0, 4), (2, 8)), (1, 0, 4, 2.0)),
    }


relax_weight = 0.8


def face_terms(visc_ext, fric_inner):
    centre = visc_ext[1:-1, 1:-1]
    east = 0.5 * (centre + visc_ext[2:, 1:-1])
    west = 0.5 * (centre + visc_ext[:-2, 1:-1])
    north = 0.5 * (centre + visc_ext[1:-1, 2:])
    south = 0.5 * (centre + visc_ext[1:-1, :-2])
    node_pp = 0.25 * (centre + visc_ext[2:, 1:-1] + visc_ext[1:-1, 2:] + visc_ext[2:, 2:])
    node_mm = 0.25 * (centre + visc_ext[:-2, 1:-1] + visc_ext[1:-1, :-2] + visc_ext[:-2, :-2])
    node_pm = 0.25 * (centre + visc_ext[2:, 1:-1] + visc_ext[1:-1, :-2] + visc_ext[2:, :-2])
    node_mp = 0.25 * (centre + visc_ext[:-2, 1:-1] + visc_ext[1:-1, 2:] + visc_ext[:-2, 2:])
    diag_x = fric_inner + 2.0 * (east + west) + (north + south)
    diag_y = fric_inner + (east + west) + 2.0 * (north + south)
    return jnp.stack([east, west, north, south, node_pp, node_mm, node_pm, node_mp, diag_x, diag_y])


def operate(field_ext, terms):
    east, west, north, south = terms[0], terms[1], terms[2], terms[3]
    node_pp, node_mm, node_pm, node_mp = terms[4], terms[5], terms[6], terms[7]
    first = field_ext[0]
    second = field_ext[1]

    def axial(comp, along_one, along_two):
        return along_one * (east * comp[2:, 1:-1] + west * comp[:-2, 1:-1]) + along_two * (north * comp[1:-1, 2:] + south * comp[1:-1, :-2])

    def cross(comp):
        return node_pp * comp[2:, 2:] + node_mm * comp[:-2, :-2] - node_pm * comp[2:, :-2] - node_mp * comp[:-2, 2:]

    out_first = terms[8] * first[1:-1, 1:-1] - axial(first, 2.0, 1.0) - 0.25 * cross(second)
    out_second = terms[9] * second[1:-1, 1:-1] - axial(second, 1.0, 2.0) - 0.25 * cross(first)
    return jnp.stack([out_first, out_second])


def relax(source, terms):
    field = jnp.zeros(source.shape, jnp.float32)
    diagonal = terms[8:10]
    for sweep in range(SWEEPS):
        padded = jnp.pad(field, ((0, 0), (1, 1), (1, 1)))
        field = field + relax_weight * (source - operate(padded, terms)) / diagonal
    return field


def reference(base_velocity, viscosity, friction, friction_probe, pixel_los, pixel_weight, pixel_cell, pixel_count, panels):
    terms = face_terms(jnp.pad(viscosity, 1), friction)
    source = -(friction_probe[None] * base_velocity)
    increment = relax(source, terms)
    los = pixel_los.reshape(N_GRP, N_TILE, 2, N_TILE, CAP)
    weight = pixel_weight.reshape(N_GRP, N_TILE, N_TILE, CAP)
    cell = pixel_cell.reshape(N_GRP, N_TILE, N_TILE, CAP)
    count = pixel_count.reshape(N_GRP, N_TILE, N_TILE)
    live = jnp.arange(CAP, dtype=jnp.int32)[None, None, None, :] < count[..., None]
    group = jnp.arange(N_GRP, dtype=jnp.int32)[:, None, None, None]
    owner = jnp.arange(N_TILE, dtype=jnp.int32)[None, None, :, None]
    row_ids = group * CX + cell // CY
    col_ids = owner * CY + cell % CY
    spot = (row_ids * NY + col_ids).reshape(-1).astype(jnp.int32)
    flat = increment.reshape(2, -1)
    los_x = los[:, :, 0].reshape(-1)
    los_y = los[:, :, 1].reshape(-1)
    predicted = los_x * flat[0][spot] + los_y * flat[1][spot]
    amount = jnp.where(live.reshape(-1), weight.reshape(-1) * predicted, 0.0)
    adjoint_source = jnp.zeros((2, NX * NY), jnp.float32).at[:, spot].add(jnp.stack([amount * los_x, amount * los_y])).reshape(2, NX, NY)
    multiplier = relax(adjoint_source, terms)
    hessian_probe = -(base_velocity[0] * multiplier[0] + base_velocity[1] * multiplier[1])
    probe_low = hessian_probe.astype(jnp.bfloat16)
    coefficients = jnp.dot(panels.reshape(K, -1), probe_low.reshape(-1), preferred_element_type=jnp.float32)
    return increment, hessian_probe, coefficients
```

```python
import functools

import jax
import jax.numpy as jnp
from jax import lax
from jax.experimental import pallas as pl
from jax.experimental.pallas import tpu as pltpu
from jax.sharding import PartitionSpec as P

SWEEPS = 8
RELAX = 0.8
CAP = 64
CHUNK = 6
HALO = 16
FIELDS = 4
STRIPS = 8
F32 = jnp.float32
BF16 = jnp.bfloat16


def lanes(shape=(8, 128)):
    return lax.broadcasted_iota(jnp.int32, shape, len(shape) - 1)


def fetch(sources, targets, sems):
    copies = [pltpu.make_async_copy(s, d, sems.at[i]) for i, (s, d) in enumerate(zip(sources, targets))]
    for copy in copies:
        copy.start()
    return copies


def pack_tiles_kernel(n_tile, *refs):
    sources, (out_ref, fields_ref), targets, sems = refs[:8], refs[8:10], refs[10:18], refs[18]
    copies = fetch(sources, targets, sems)
    bv_ref, visc_ref, fric_ref, fp_ref, los_ref, weight_ref, cell_ref, count_ref = targets
    t = lax.axis_index("tile")
    parity = lax.rem(t, 2)
    rows = visc_ref.shape[0]
    half = rows // 2
    for copy in copies:
        copy.wait()
    probe = fp_ref[...]
    fields = [-(probe * bv_ref[0]), -(probe * bv_ref[1]), visc_ref[...], fric_ref[...]]
    for f, field in enumerate(fields):
        fields_ref[f] = field
    lane = lanes((half, 128))

    def fold(first_lane):
        packed = jnp.zeros((half, 128), F32)
        for part in range(2):
            for f, field in enumerate(fields):
                start = part * 64 + f * HALO
                piece = field[part * half : (part + 1) * half]
                piece = pltpu.roll(piece, (start - first_lane) % 128, 1)
                packed = jnp.where((lane >= start) & (lane < start + HALO), piece, packed)
        return packed

    @pl.when(t < n_tile - 1)
    def _():
        out_ref[t + 1, 0:half, :] = fold(128 - HALO)

    @pl.when(t > 0)
    def _():
        out_ref[t - 1, 0:half, :] = fold(0)

    row_lane = lanes((1, 128))
    low = lanes((4, 128)) < CAP
    straight, turned = [], []
    for j in range(n_tile // 2):
        at = pl.ds(j * 128, 128)
        count = jnp.where(
            row_lane < CAP, count_ref[0, 0, :, 2 * j : 2 * j + 1], count_ref[0, 0, :, 2 * j + 1 : 2 * j + 2]
        )
        live = (row_lane & (CAP - 1)) < count
        weight = jnp.where(live, weight_ref[0, 0, :, at], 0.0)
        cell = cell_ref[0, 0, :, at].astype(F32)
        block = jnp.concatenate([los_ref[0, 0, :, at], weight, cell], axis=0)
        straight.append(block)
        turned.append(pltpu.roll(block, CAP, 1))
    nothing = jnp.zeros((4, 128), F32)
    in_half = (lanes((4, 128)) // CAP) == parity

    def placed(owner, side):
        if owner < 0 or owner >= n_tile:
            return nothing
        return (straight if owner % 2 == side else turned)[owner // 2]

    for d in range(n_tile):
        solo = jnp.where(parity == d % 2, straight[d // 2], turned[d // 2])
        solo = jnp.where(in_half, solo, 0.0)
        pair = jnp.where(low, placed(d - 1, 0), placed(d + 1, 1))
        out_ref[d, half : half + 8, :] = jnp.concatenate([solo, pair], axis=0)


def pack_rows_kernel(n_tile, fields_ref, got_ref, ext_ref, pix_ref, up_ref, down_ref):
    t = lax.axis_index("tile")
    rows = fields_ref.shape[1]
    half = rows // 2
    fields = [fields_ref[f] for f in range(FIELDS)]
    lane = lanes((half, 128))
    right = jnp.where(t < n_tile - 1, got_ref[jnp.minimum(t + 1, n_tile - 1), 0:half, :], 0.0)
    left = jnp.where(t > 0, got_ref[jnp.maximum(t - 1, 0), 0:half, :], 0.0)
    band = lanes((HALO, 128))
    edge_up = jnp.zeros((HALO, 128), F32)
    edge_down = jnp.zeros((HALO, 128), F32)
    for f, field in enumerate(fields):
        ext_ref[f, :, 0:128] = field
        up_ref[f * HALO : (f + 1) * HALO, :] = field[0:HALO]
        down_ref[f * HALO : (f + 1) * HALO, :] = field[rows - HALO :]
        edges = []
        for part in range(2):
            start = part * 64 + f * HALO
            edge = jnp.where(
                lane < HALO,
                pltpu.roll(right, (0 - start) % 128, 1),
                jnp.where(lane >= 128 - HALO, pltpu.roll(left, (128 - HALO - start) % 128, 1), 0.0),
            )
            ext_ref[f, part * half : (part + 1) * half, 128:256] = edge
            edges.append(edge)
        here = (band >= 2 * f * HALO) & (band < 2 * (f + 1) * HALO)
        turn = (2 * f + 1) * HALO % 128
        edge_up = jnp.where(here, pltpu.roll(edges[0][0:HALO], turn, 1), edge_up)
        edge_down = jnp.where(here, pltpu.roll(edges[1][half - HALO :], turn, 1), edge_down)
    base = FIELDS * HALO
    up_ref[base : base + HALO, :] = edge_up
    down_ref[base : base + HALO, :] = edge_down
    base = base + HALO
    for s in range(n_tile):
        block = got_ref[s, half : half + 8, :]
        pix_ref[8 * s : 8 * s + 8, :] = block
        up_ref[base + 8 * s : base + 8 * s + 8, :] = block
        down_ref[base + 8 * s : base + 8 * s + 8, :] = block


def solve_kernel(
    n_grp, n_tile, ext_ref, pix_ref, above_ref, below_ref, bv_hbm, panels_hbm,
    inc_ref, hess_ref, low_ref, panels_ref,
    plane_ref, coef_ref, src_ref, w_ref, table_ref, hot_ref, acc_ref, out_ref, bv_ref, sems,
):
    copies = fetch((bv_hbm, panels_hbm), (bv_ref, panels_ref), sems)
    g = lax.axis_index("grp")
    t = lax.axis_index("tile")
    rows = ext_ref.shape[1]
    span = rows + 2 * HALO
    groups = span // STRIPS
    lane = lanes()
    first_lane = lane == 0
    last_lane = lane == 127

    band = lanes((HALO, 128))
    for f in range(FIELDS):
        for h in range(2):
            plane_ref[f, h, HALO : HALO + rows, :] = ext_ref[f, :, h * 128 : (h + 1) * 128]
        for ref, at in ((above_ref, 0), (below_ref, HALO + rows)):
            plane_ref[f, 0, at : at + HALO, :] = ref[f * HALO : (f + 1) * HALO, :]
            edge = pltpu.roll(ref[FIELDS * HALO : (FIELDS + 1) * HALO, :], (0 - (2 * f + 1) * HALO) % 128, 1)
            plane_ref[f, 1, at : at + HALO, :] = jnp.where((band < HALO) | (band >= 128 - HALO), edge, 0.0)

    def strided(f, h, v):
        return plane_ref[f, h, pl.ds(v, STRIPS, stride=groups), :]

    def beside(pair):
        a, b = pair
        ra, rb = pltpu.roll(a, 1, 1), pltpu.roll(b, 1, 1)
        before = (jnp.where(first_lane, rb, ra), jnp.where(first_lane, ra, rb))
        ra, rb = pltpu.roll(a, 127, 1), pltpu.roll(b, 127, 1)
        after = (jnp.where(last_lane, rb, ra), jnp.where(last_lane, ra, rb))
        return before, pair, after

    def row(load, v):
        if v < 0:
            return beside(tuple(pltpu.roll(load(h, groups - 1), 1, 0) for h in range(2)))
        if v == groups:
            return beside(tuple(pltpu.roll(load(h, 0), STRIPS - 1, 0) for h in range(2)))
        return beside(tuple(load(h, v) for h in range(2)))

    strip = lax.broadcasted_iota(jnp.int32, (8, 128), 0)
    col_in = [
        None,
        ((lane < HALO) & (t < n_tile - 1)) | ((lane >= 128 - HALO) & (t > 0)),
    ]
    load_visc = functools.partial(strided, 2)
    prev, cur = row(load_visc, -1), row(load_visc, 0)
    for v in range(groups):
        nxt = row(load_visc, v + 1)
        place = g * rows - HALO + strip * groups + v
        row_in = (place >= 0) & (place < n_grp * rows)
        at = pl.ds(v * 8, 8)
        for h in range(2):
            centre = cur[1][h]
            east = 0.5 * (centre + nxt[1][h])
            west = 0.5 * (centre + prev[1][h])
            north = 0.5 * (centre + cur[2][h])
            south = 0.5 * (centre + cur[0][h])
            node_pp = 0.25 * (centre + nxt[1][h] + cur[2][h] + nxt[2][h])
            node_mm = 0.25 * (centre + prev[1][h] + cur[0][h] + prev[0][h])
            node_pm = 0.25 * (centre + nxt[1][h] + cur[0][h] + nxt[0][h])
            node_mp = 0.25 * (centre + prev[1][h] + cur[2][h] + prev[2][h])
            fric = strided(3, h, v)
            diag_x = fric + 2.0 * (east + west) + (north + south)
            diag_y = fric + (east + west) + 2.0 * (north + south)
            inside = row_in if col_in[h] is None else row_in & col_in[h]
            inv_x = jnp.where(inside, RELAX / jnp.where(inside, diag_x, 1.0), 0.0)
            inv_y = jnp.where(inside, RELAX / jnp.where(inside, diag_y, 1.0), 0.0)
            cols = pl.ds(h * 128, 128)
            for i, plane in enumerate(
                (east, west, north, south, 0.25 * node_pp, 0.25 * node_mm, 0.25 * node_pm, 0.25 * node_mp, inv_x, inv_y)
            ):
                coef_ref[i, at, cols] = plane
            src_ref[0, at, cols] = inv_x * strided(0, h, v)
            src_ref[1, at, cols] = inv_y * strided(1, h, v)
        prev, cur = cur, nxt

    def relax():
        w_ref[0] = src_ref[...]

        def sweep(i, _):
            now = lax.rem(i, 2)
            later = 1 - now

            def load(c, h, v):
                return w_ref[now, c, pl.ds(v * 8, 8), pl.ds(h * 128, 128)]

            def both(v):
                return tuple(row(functools.partial(load, c), v) for c in range(2))

            prev, cur = both(-1), both(0)
            for v in range(groups):
                nxt = both(v + 1)
                at = pl.ds(v * 8, 8)
                for h in range(2):
                    cols = pl.ds(h * 128, 128)
                    east, west, north, south, pp, mm, pm, mp, inv_x, inv_y = (
                        coef_ref[i, at, cols] for i in range(10)
                    )

                    def along(c):
                        return (
                            east * nxt[c][1][h] + west * prev[c][1][h],
                            north * cur[c][2][h] + south * cur[c][0][h],
                        )

                    def cross(c):
                        return (
                            pp * nxt[c][2][h] + mm * prev[c][0][h] - pm * nxt[c][0][h] - mp * prev[c][2][h]
                        )

                    one, two = along(0)
                    sum_x = 2.0 * one + two + cross(1)
                    one, two = along(1)
                    sum_y = one + 2.0 * two + cross(0)
                    w_ref[later, 0, at, cols] = (
                        (1.0 - RELAX) * cur[0][1][h] + src_ref[0, at, cols] + inv_x * sum_x
                    )
                    w_ref[later, 1, at, cols] = (
                        (1.0 - RELAX) * cur[1][1][h] + src_ref[1, at, cols] + inv_y * sum_y
                    )
                prev, cur = cur, nxt
            return 0

        lax.fori_loop(0, SWEEPS - 1, sweep, 0)

    relax()
    last = (SWEEPS - 1) % 2
    for c in range(2):
        for v in range(groups):
            out_ref[c, pl.ds(v, STRIPS, stride=groups), :] = w_ref[last, c, pl.ds(v * 8, 8), 0:128]
        inc_ref[c] = out_ref[c, HALO : HALO + rows, :]

    low = lanes((1, 128)) < 64

    def tabulate(slot, block, delta, beyond):
        cell = block[3:4].astype(jnp.int32)
        r = lax.shift_right_logical(cell, 7)
        c = cell & 127
        place = r + HALO + rows * delta
        s = lax.shift_right_arithmetic(place * ((1 << 16) // groups + 1), 16)
        m = (place - s * groups) * 8 + s
        if beyond:
            col_ok = (c < HALO) & (~low) | (c >= 128 - HALO) & low
        else:
            col_ok = c >= 0
        ok = (place >= 0) & (place < span) & col_ok
        weight = jnp.where(ok, block[2:3], 0.0)
        table_ref[slot, 0:8, :] = jnp.concatenate(
            [block[0:2], weight, m.astype(F32), c.astype(F32), jnp.zeros((3, 128), F32)], axis=0
        )

    base = (FIELDS + 1) * HALO
    near, far = 0, 3 * n_tile // 2
    for ref, start, delta in ((pix_ref, 0, 0), (above_ref, base, -1), (below_ref, base, 1)):
        for s in range(0, n_tile, 2):
            one = ref[start + 8 * s : start + 8 * s + 8, :]
            two = ref[start + 8 * s + 8 : start + 8 * s + 16, :]
            tabulate(near, jnp.where(low, one[0:4], two[0:4]), delta, False)
            tabulate(far, one[4:8], delta, True)
            tabulate(far + 1, two[4:8], delta, True)
            near, far = near + 1, far + 2

    acc_ref[...] = jnp.zeros_like(acc_ref)
    for h in range(2):
        field = jnp.concatenate([w_ref[last, c, :, h * 128 : (h + 1) * 128] for c in range(2)], axis=0)
        high = field.astype(BF16)
        hot_ref[h] = jnp.concatenate([high, (field - high.astype(F32)).astype(BF16)], axis=1)
    wide = CHUNK * 128
    row_id = lax.broadcasted_iota(jnp.int32, (span, wide), 0).astype(F32)
    lane_id = lax.broadcasted_iota(jnp.int32, (128, wide), 0).astype(F32)

    def pixels(h, first, j, _):
        data = jnp.concatenate([table_ref[first + j * CHUNK + i] for i in range(CHUNK)], axis=1)
        los_x, los_y, weight = data[0:1], data[1:2], data[2:3]
        hot = jnp.where(lane_id == data[4:5], 1.0, 0.0).astype(BF16)
        got = jnp.dot(hot_ref[h], jnp.concatenate([hot, hot], axis=0), preferred_element_type=F32)
        here = row_id == data[3:4]
        got_x = jnp.sum(jnp.where(here, got[0:span], 0.0), axis=0, keepdims=True)
        got_y = jnp.sum(jnp.where(here, got[span:], 0.0), axis=0, keepdims=True)
        amount = weight * (los_x * got_x + los_y * got_y)
        total = acc_ref[h]
        parts = [amount * los_x, amount * los_y]
        highs = [p.astype(BF16).astype(F32) for p in parts]
        for terms in (highs, [p - q for p, q in zip(parts, highs)]):
            spread = jnp.concatenate([jnp.where(here, p, 0.0).astype(BF16) for p in terms], axis=0)
            total = total + lax.dot_general(
                spread, hot, (((1,), (1,)), ((), ())), preferred_element_type=F32
            )
        acc_ref[h] = total
        return 0

    split = 3 * n_tile // 2
    lax.fori_loop(0, split // CHUNK, functools.partial(pixels, 0, 0), 0)
    lax.fori_loop(0, 2 * split // CHUNK, functools.partial(pixels, 1, split), 0)

    for h in range(2):
        cols = pl.ds(h * 128, 128)
        for c in range(2):
            src_ref[c, :, cols] = coef_ref[8 + c, :, cols] * acc_ref[h, c * span : (c + 1) * span, :]
    relax()
    for c in range(2):
        for v in range(groups):
            out_ref[c, pl.ds(v, STRIPS, stride=groups), :] = w_ref[last, c, pl.ds(v * 8, 8), 0:128]
    for copy in copies:
        copy.wait()
    hess = -(bv_ref[0] * out_ref[0, HALO : HALO + rows, :] + bv_ref[1] * out_ref[1, HALO : HALO + rows, :])
    hess_ref[...] = hess
    low_ref[...] = hess.astype(BF16)


def project_kernel(panels_ref, probe_ref, out_ref):
    count = panels_ref.shape[0]
    probe = probe_ref[...].astype(F32)
    sums = []
    for k in range(count):
        product = panels_ref[k].astype(F32) * probe
        sums.append(jnp.sum(product, axis=0, keepdims=True))
    sums.append(jnp.zeros((128 - count, 128), F32))
    table = jnp.concatenate(sums, axis=0)
    line = lax.dot_general(
        jnp.ones((8, 128), F32), table, (((1,), (1,)), ((), ())),
        precision=lax.Precision.HIGHEST, preferred_element_type=F32,
    )
    line = pltpu.roll(line, lax.axis_index("grp") * count, 1)[0:1]
    out_ref[...] = jnp.broadcast_to(line[None], out_ref.shape)


def add_lines_kernel(lines_ref, out_ref):
    out_ref[...] = jnp.sum(lines_ref[...], axis=0)


def vmem(n):
    return [pl.BlockSpec(memory_space=pltpu.VMEM)] * n


def on_device(
    base_velocity, viscosity, friction, friction_probe, pixel_los, pixel_weight, pixel_cell, pixel_count, panels
):
    n_grp, n_tile = lax.axis_size("grp"), lax.axis_size("tile")
    rows, columns = viscosity.shape
    half = rows // 2
    span = rows + 2 * HALO
    params = pltpu.CompilerParams(vmem_limit_bytes=32 * 2**20)

    inputs = [
        pltpu.with_memory_space_constraint(x, pltpu.HBM)
        for x in (
            base_velocity, viscosity, friction, friction_probe, pixel_los, pixel_weight, pixel_cell, pixel_count
        )
    ]
    slots, fields = pl.pallas_call(
        functools.partial(pack_tiles_kernel, n_tile),
        out_shape=(
            jax.ShapeDtypeStruct((n_tile, half + 8, 128), F32),
            jax.ShapeDtypeStruct((FIELDS, rows, columns), F32),
        ),
        in_specs=[pl.BlockSpec(memory_space=pltpu.HBM)] * len(inputs),
        out_specs=tuple(vmem(2)),
        scratch_shapes=[pltpu.VMEM(x.shape, x.dtype) for x in inputs] + [pltpu.SemaphoreType.DMA((len(inputs),))],
        compiler_params=params,
        name="pack_tiles",
    )(*inputs)
    got = lax.all_to_all(slots, "tile", split_axis=0, concat_axis=0, tiled=True)

    packet = (FIELDS + 1) * HALO + 8 * n_tile
    ext, pix, up, down = pl.pallas_call(
        functools.partial(pack_rows_kernel, n_tile),
        out_shape=(
            jax.ShapeDtypeStruct((FIELDS, rows, 256), F32),
            jax.ShapeDtypeStruct((8 * n_tile, 128), F32),
            jax.ShapeDtypeStruct((packet, 128), F32),
            jax.ShapeDtypeStruct((packet, 128), F32),
        ),
        in_specs=vmem(2),
        out_specs=tuple(vmem(4)),
        compiler_params=params,
        name="pack_rows",
    )(fields, got)
    above = lax.ppermute(down, "grp", [(i, i + 1) for i in range(n_grp - 1)])
    below = lax.ppermute(up, "grp", [(i + 1, i) for i in range(n_grp - 1)])

    tiles = 9 * n_tile // 2
    increment, hessian_probe, probe_low, panels_near = pl.pallas_call(
        functools.partial(solve_kernel, n_grp, n_tile),
        out_shape=(
            jax.ShapeDtypeStruct((2, rows, columns), F32),
            jax.ShapeDtypeStruct((rows, columns), F32),
            jax.ShapeDtypeStruct((rows, columns), BF16),
            jax.ShapeDtypeStruct(panels.shape, BF16),
        ),
        in_specs=vmem(4) + [pl.BlockSpec(memory_space=pltpu.HBM)] * 2,
        out_specs=tuple(vmem(4)),
        scratch_shapes=[
            pltpu.VMEM((FIELDS, 2, span, 128), F32),
            pltpu.VMEM((10, span, 256), F32),
            pltpu.VMEM((2, span, 256), F32),
            pltpu.VMEM((2, 2, span, 256), F32),
            pltpu.VMEM((tiles, 8, 128), F32),
            pltpu.VMEM((2, 2 * span, 256), BF16),
            pltpu.VMEM((2, 2 * span, 128), F32),
            pltpu.VMEM((2, span, 128), F32),
            pltpu.VMEM(base_velocity.shape, F32),
            pltpu.SemaphoreType.DMA((2,)),
        ],
        compiler_params=params,
        name="solve",
    )(ext, pix, above, below, inputs[0], pltpu.with_memory_space_constraint(panels, pltpu.HBM))

    column = lax.all_gather(probe_low, "grp", axis=0, tiled=True)
    partial = pl.pallas_call(
        project_kernel,
        out_shape=jax.ShapeDtypeStruct((n_grp * n_tile, 1, 128), F32),
        in_specs=vmem(2),
        out_specs=pl.BlockSpec(memory_space=pltpu.VMEM),
        compiler_params=params,
        name="project",
    )(panels_near, column)
    everyone = lax.all_to_all(partial, ("grp", "tile"), split_axis=0, concat_axis=0, tiled=True)
    coefficients = pl.pallas_call(
        add_lines_kernel,
        out_shape=jax.ShapeDtypeStruct((1, 128), F32),
        in_specs=vmem(1),
        out_specs=pl.BlockSpec(memory_space=pltpu.VMEM),
        compiler_params=params,
        name="add_lines",
    )(everyone)
    return increment, hessian_probe, coefficients.reshape(128)


def solution(mesh):
    in_specs = (
        P(None, "grp", "tile"),
        P("grp", "tile"),
        P("grp", "tile"),
        P("grp", "tile"),
        P("grp", "tile", None, None),
        P("grp", "tile", None, None),
        P("grp", "tile", None, None),
        P("grp", "tile", None, None),
        P("grp", None, "tile"),
    )
    out_specs = (P(None, "grp", "tile"), P("grp", "tile"), P())
    return jax.shard_map(
        on_device, mesh=mesh, in_specs=in_specs, out_specs=out_specs, check_vma=False
    )
```

```python
import functools

import jax
import jax.numpy as jnp
from jax import lax
from jax.experimental import pallas as pl
from jax.experimental.pallas import tpu as pltpu
from jax.sharding import PartitionSpec as P

SWEEPS = 8
RELAX = 0.8
CAP = 64
HALO = 16
EDGE = 8
FIELDS = 4
STRIPS = 8
F32 = jnp.float32
BF16 = jnp.bfloat16


def lanes(shape=(8, 128)):
    return lax.broadcasted_iota(jnp.int32, shape, len(shape) - 1)


def fetch(sources, targets, sems):
    copies = [pltpu.make_async_copy(s, d, sems.at[i]) for i, (s, d) in enumerate(zip(sources, targets))]
    for copy in copies:
        copy.start()
    return copies


def pack_tiles_kernel(n_tile, *refs):
    sources, (out_ref, fields_ref), targets, sems = refs[:8], refs[8:10], refs[10:18], refs[18]
    copies = fetch(sources, targets, sems)
    bv_ref, visc_ref, fric_ref, fp_ref, los_ref, weight_ref, cell_ref, count_ref = targets
    t = lax.axis_index("tile")
    parity = lax.rem(t, 2)
    rows = visc_ref.shape[0]
    half = rows // 2
    for copy in copies[4:]:
        copy.wait()
    row_lane = lanes((1, 128))
    low = lanes() < CAP
    straight, turned = [], []
    for j in range(n_tile // 2):
        at = pl.ds(j * 128, 128)
        count = jnp.where(
            row_lane < CAP, count_ref[0, 0, :, 2 * j : 2 * j + 1], count_ref[0, 0, :, 2 * j + 1 : 2 * j + 2]
        )
        live = (row_lane & (CAP - 1)) < count
        weight = jnp.where(live, weight_ref[0, 0, :, at], 0.0)
        scaled = jnp.sqrt(weight) * los_ref[0, 0, :, at]
        high = scaled.astype(BF16).astype(F32)
        cell = cell_ref[0, 0, :, at]
        block = jnp.concatenate(
            [
                high, scaled - high,
                lax.shift_right_logical(cell, 7).astype(F32), (cell & 127).astype(F32), jnp.zeros((2, 128), F32),
            ],
            axis=0,
        )
        straight.append(block)
        turned.append(pltpu.roll(block, CAP, 1))
    nothing = jnp.zeros((8, 128), F32)
    in_half = (lanes() // CAP) == parity

    def placed(owner, side):
        if owner < 0 or owner >= n_tile:
            return nothing
        return (straight if owner % 2 == side else turned)[owner // 2]

    for d in range(n_tile):
        solo = jnp.where(parity == d % 2, straight[d // 2], turned[d // 2])
        solo = jnp.where(in_half, solo, 0.0)
        pair = jnp.where(low, placed(d - 1, 0), placed(d + 1, 1))
        out_ref[d, half : half + 16, :] = jnp.concatenate([solo, pair], axis=0).astype(BF16)

    for copy in copies[:4]:
        copy.wait()
    probe = fp_ref[...]
    fields = [-(probe * bv_ref[0]), -(probe * bv_ref[1]), visc_ref[...], fric_ref[...]]
    for f, field in enumerate(fields):
        fields_ref[f] = field
    lane = lanes((half, 128))

    def fold(first_lane):
        packed = jnp.zeros((half, 128), F32)
        for part in range(2):
            for f, field in enumerate(fields):
                start = part * 64 + f * HALO
                piece = field[part * half : (part + 1) * half]
                piece = pltpu.roll(piece, (start - first_lane) % 128, 1)
                packed = jnp.where((lane >= start) & (lane < start + HALO), piece, packed)
        return packed

    @pl.when(t < n_tile - 1)
    def _():
        out_ref[t + 1, 0:half, :] = fold(128 - HALO).astype(BF16)

    @pl.when(t > 0)
    def _():
        out_ref[t - 1, 0:half, :] = fold(0).astype(BF16)


def pack_rows_kernel(n_grp, n_tile, fields_ref, got_ref, ext_ref, pix_ref, out_ref):
    g = lax.axis_index("grp")
    t = lax.axis_index("tile")
    rows = fields_ref.shape[1]
    half = rows // 2
    fields = [fields_ref[f] for f in range(FIELDS)]
    lane = lanes((half, 128))
    right = jnp.where(t < n_tile - 1, got_ref[jnp.minimum(t + 1, n_tile - 1), 0:half, :].astype(F32), 0.0)
    left = jnp.where(t > 0, got_ref[jnp.maximum(t - 1, 0), 0:half, :].astype(F32), 0.0)
    band = lanes((HALO, 128))
    edge_up = jnp.zeros((HALO, 128), F32)
    edge_down = jnp.zeros((HALO, 128), F32)
    for f, field in enumerate(fields):
        ext_ref[f, :, 0:128] = field
        edges = []
        for part in range(2):
            start = part * 64 + f * HALO
            edge = jnp.where(
                lane < HALO,
                pltpu.roll(right, (0 - start) % 128, 1),
                jnp.where(lane >= 128 - HALO, pltpu.roll(left, (128 - HALO - start) % 128, 1), 0.0),
            )
            ext_ref[f, part * half : (part + 1) * half, 128:256] = edge
            edges.append(edge)
        here = (band >= 2 * f * HALO) & (band < 2 * (f + 1) * HALO)
        turn = (2 * f + 1) * HALO % 128
        edge_up = jnp.where(here, pltpu.roll(edges[0][0:HALO], turn, 1), edge_up)
        edge_down = jnp.where(here, pltpu.roll(edges[1][half - HALO :], turn, 1), edge_down)
    low = lanes() < CAP
    near, far = [], []
    for s in range(0, n_tile, 2):
        one = got_ref[s, half : half + 16, :].astype(F32)
        two = got_ref[s + 1, half : half + 16, :].astype(F32)
        near.append(jnp.where(low, one[0:8], two[0:8]))
        far += [one[8:16], two[8:16]]
    blocks = near + far
    pixels = jnp.concatenate(
        [b[0:1] + b[2:3] for b in blocks]
        + [b[1:2] + b[3:4] for b in blocks]
        + [b[4:5] for b in blocks]
        + [b[5:6] for b in blocks],
        axis=0,
    )
    pix_ref[...] = pixels
    pixels = pixels.astype(BF16)

    def send(slot, first, edge):
        for f, field in enumerate(fields):
            out_ref[slot, f * HALO : (f + 1) * HALO, :] = field[first : first + HALO].astype(BF16)
        base = FIELDS * HALO
        out_ref[slot, base : base + HALO, :] = edge.astype(BF16)
        base = base + HALO
        out_ref[slot, base:, :] = pixels

    @pl.when(g > 0)
    def _():
        send(g - 1, 0, edge_up)

    @pl.when(g < n_grp - 1)
    def _():
        send(g + 1, rows - HALO, edge_down)


def solve_kernel(
    n_grp, n_tile, ext_ref, pix_ref, got_ref, bv_hbm, panels_hbm,
    inc_ref, hess_ref, low_ref, panels_ref,
    plane_ref, coef_ref, src_ref, w_ref, nat_ref, bv_ref, sems,
):
    copies = fetch((bv_hbm, panels_hbm), (bv_ref, panels_ref), sems)
    g = lax.axis_index("grp")
    t = lax.axis_index("tile")
    rows = ext_ref.shape[1]
    span = rows + 2 * HALO
    groups = span // STRIPS
    lane = lanes()

    def above(first, size):
        return jnp.where(g > 0, got_ref[jnp.maximum(g - 1, 0), first : first + size, :].astype(F32), 0.0)

    def below(first, size):
        return jnp.where(g < n_grp - 1, got_ref[jnp.minimum(g + 1, n_grp - 1), first : first + size, :].astype(F32), 0.0)

    first_lane = lane == 0
    last_lane = lane == 127

    band = lanes((HALO, 128))
    for f in range(FIELDS):
        for h in range(2):
            plane_ref[f, h, HALO : HALO + rows, :] = ext_ref[f, :, h * 128 : (h + 1) * 128]
        for load, at in ((above, 0), (below, HALO + rows)):
            plane_ref[f, 0, at : at + HALO, :] = load(f * HALO, HALO)
            edge = pltpu.roll(load(FIELDS * HALO, HALO), (0 - (2 * f + 1) * HALO) % 128, 1)
            plane_ref[f, 1, at : at + HALO, :] = jnp.where((band < HALO) | (band >= 128 - HALO), edge, 0.0)

    def strided(f, h, v):
        return plane_ref[f, h, pl.ds(v, STRIPS, stride=groups), :]

    def beside(pair):
        a, b = pair
        ra, rb = pltpu.roll(a, 1, 1), pltpu.roll(b, 1, 1)
        before = (jnp.where(first_lane, rb, ra), jnp.where(first_lane, ra, rb))
        ra, rb = pltpu.roll(a, 127, 1), pltpu.roll(b, 127, 1)
        after = (jnp.where(last_lane, rb, ra), jnp.where(last_lane, ra, rb))
        return before, pair, after

    def row(load, v):
        if v < 0:
            return beside(tuple(pltpu.roll(load(h, groups - 1), 1, 0) for h in range(2)))
        if v == groups:
            return beside(tuple(pltpu.roll(load(h, 0), STRIPS - 1, 0) for h in range(2)))
        return beside(tuple(load(h, v) for h in range(2)))

    strip = lax.broadcasted_iota(jnp.int32, (8, 128), 0)
    col_in = [
        None,
        ((lane < HALO) & (t < n_tile - 1)) | ((lane >= 128 - HALO) & (t > 0)),
    ]
    load_visc = functools.partial(strided, 2)
    prev, cur = row(load_visc, -1), row(load_visc, 0)
    for v in range(groups):
        nxt = row(load_visc, v + 1)
        place = g * rows - HALO + strip * groups + v
        row_in = (place >= 0) & (place < n_grp * rows)
        at = pl.ds(v * 8, 8)
        for h in range(2):
            centre = cur[1][h]
            east = 0.5 * (centre + nxt[1][h])
            west = 0.5 * (centre + prev[1][h])
            north = 0.5 * (centre + cur[2][h])
            south = 0.5 * (centre + cur[0][h])
            node_pp = 0.25 * (centre + nxt[1][h] + cur[2][h] + nxt[2][h])
            node_mm = 0.25 * (centre + prev[1][h] + cur[0][h] + prev[0][h])
            node_pm = 0.25 * (centre + nxt[1][h] + cur[0][h] + nxt[0][h])
            node_mp = 0.25 * (centre + prev[1][h] + cur[2][h] + prev[2][h])
            fric = strided(3, h, v)
            diag_x = fric + 2.0 * (east + west) + (north + south)
            diag_y = fric + (east + west) + 2.0 * (north + south)
            inside = row_in if col_in[h] is None else row_in & col_in[h]
            inv_x = jnp.where(inside, RELAX / jnp.where(inside, diag_x, 1.0), 0.0)
            inv_y = jnp.where(inside, RELAX / jnp.where(inside, diag_y, 1.0), 0.0)
            cols = pl.ds(h * 128, 128)
            for i, plane in enumerate(
                (east, west, north, south, 0.25 * node_pp, 0.25 * node_mm, 0.25 * node_pm, 0.25 * node_mp, inv_x, inv_y)
            ):
                coef_ref[i, at, cols] = plane
            src_ref[0, at, cols] = inv_x * strided(0, h, v)
            src_ref[1, at, cols] = inv_y * strided(1, h, v)
        prev, cur = cur, nxt

    def natural(h, v):
        return (h, pl.ds(v, STRIPS, stride=groups), slice(None))

    def sweep(i, carry):
        now, later = w_ref.at[i & 1], w_ref.at[1 - (i & 1)]

        def both(v):
            return tuple(row(lambda h, u, c=c: now[c, pl.ds(u * 8, 8), pl.ds(h * 128, 128)], v) for c in range(2))

        prev, cur = both(-1), both(0)
        for v in range(groups):
            nxt = both(v + 1)
            at = pl.ds(v * 8, 8)
            for h in range(2):
                cols = pl.ds(h * 128, 128)
                east, west, north, south, pp, mm, pm, mp, inv_x, inv_y = (coef_ref[k, at, cols] for k in range(10))

                def along(c):
                    return (
                        east * nxt[c][1][h] + west * prev[c][1][h],
                        north * cur[c][2][h] + south * cur[c][0][h],
                    )

                def cross(c):
                    return pp * nxt[c][2][h] + mm * prev[c][0][h] - pm * nxt[c][0][h] - mp * prev[c][2][h]

                one, two = along(0)
                sum_x = 2.0 * one + two + cross(1)
                one, two = along(1)
                sum_y = one + 2.0 * two + cross(0)
                for c, new in ((0, inv_x * sum_x), (1, inv_y * sum_y)):
                    later[c, at, cols] = (1.0 - RELAX) * cur[c][1][h] + src_ref[c, at, cols] + new
            prev, cur = cur, nxt
        return carry

    def solve(phase, carry):
        w_ref[0] = src_ref[...]
        lax.fori_loop(0, SWEEPS - 1, sweep, 0)
        for v in range(groups):
            for h in range(2):
                for c in range(2):
                    nat_ref[(c,) + natural(h, v)] = w_ref[
                        (SWEEPS - 1) % 2, c, pl.ds(v * 8, 8), pl.ds(h * 128, 128)
                    ]

        @pl.when(phase == 0)
        def _():
            for c in range(2):
                inc_ref[c] = nat_ref[c, 0, HALO : HALO + rows, :]
            misfit()

        return carry

    def misfit():
        n_near, n_all = n_tile // 2, 3 * n_tile // 2
        low = lanes((n_tile, 128)) < CAP
        spans = ((0, HALO, rows), (-1, HALO - EDGE, EDGE), (1, HALO + rows, EDGE))
        rim_lane = lanes((2 * rows, 128))
        jobs = []
        for delta, first, size in spans:
            if delta == 0:
                values = pix_ref[...]
            else:
                base = (FIELDS + 1) * HALO
                values = (above if delta < 0 else below)(base, 4 * n_all)
            los_x, los_y, r, c = (values[q * n_all : (q + 1) * n_all] for q in range(4))
            if delta < 0:
                r = r - (rows - EDGE)
            in_rim = c[n_near:] + jnp.where(low, float(EDGE) - 128.0, float(EDGE))
            for h, begin, count, lane_of in ((0, 0, n_near, c[0:n_near]), (1, n_near, n_tile, in_rim)):
                parts = []
                for comp in range(2):
                    part = nat_ref[comp, h, first : first + size, :]
                    parts.append(part if h == 0 else pltpu.roll(part, EDGE, 1))
                field = jnp.concatenate(parts, axis=0)
                high = field.astype(BF16).astype(F32)
                rest = field - high
                if h == 0:
                    stacked = jnp.concatenate([high.astype(BF16), rest.astype(BF16)], axis=1)
                else:
                    lane_here = rim_lane[0 : 2 * size]
                    stacked = jnp.where(lane_here < 2 * EDGE, high, pltpu.roll(rest, 2 * EDGE, 1))
                    stacked = jnp.where(lane_here < 4 * EDGE, stacked, 0.0).astype(BF16)
                jobs.append((h, first, size, begin, count, lane_of, los_x, los_y, r, stacked))

        nat_ref[...] = jnp.zeros_like(nat_ref)
        for h, first, size, begin, count, lane_of, los_x, los_y, r, stacked in jobs:
            chunk = 4 if h == 0 else 8
            depth = 128 if h == 0 else 2 * EDGE
            wide = chunk * 128
            row_id = lax.broadcasted_iota(jnp.int32, (size, wide), 0).astype(F32)
            lane_id = lax.broadcasted_iota(jnp.int32, (depth, wide), 0).astype(F32)
            total = jnp.zeros((4 * size, 128), F32)
            for j in range(0, count, chunk):

                def line(table, offset):
                    return jnp.concatenate([table[offset + i : offset + i + 1] for i in range(j, j + chunk)], axis=1)

                line_x, line_y = line(los_x, begin), line(los_y, begin)
                hot = jnp.where(lane_id == line(lane_of, 0), 1.0, 0.0).astype(BF16)
                here = row_id == line(r, begin)
                twice = [hot, hot]
                if h == 1:
                    twice.append(jnp.zeros((128 - 2 * depth, wide), BF16))
                    hot = jnp.concatenate([hot, jnp.zeros((128 - depth, wide), BF16)], axis=0)
                got = jnp.dot(stacked, jnp.concatenate(twice, axis=0), preferred_element_type=F32)
                got_x = jnp.sum(jnp.where(here, got[0:size], 0.0), axis=0, keepdims=True)
                got_y = jnp.sum(jnp.where(here, got[size:], 0.0), axis=0, keepdims=True)
                amount = line_x * got_x + line_y * got_y
                terms = [amount * line_x, amount * line_y]
                highs = [p.astype(BF16).astype(F32) for p in terms]
                terms = highs + [p - q for p, q in zip(terms, highs)]
                spread = jnp.concatenate([jnp.where(here, p, 0.0) for p in terms], axis=0).astype(BF16)
                total = total + lax.dot_general(spread, hot, (((1,), (1,)), ((), ())), preferred_element_type=F32)
            total = total[0 : 2 * size] + total[2 * size :]
            if h == 1:
                total = pltpu.roll(total, 128 - EDGE, 1)
            for c in range(2):
                nat_ref[c, h, first : first + size, :] = total[c * size : (c + 1) * size]

        for v in range(groups):
            at = pl.ds(v * 8, 8)
            for h in range(2):
                cols = pl.ds(h * 128, 128)
                for c in range(2):
                    src_ref[c, at, cols] = coef_ref[8 + c, at, cols] * nat_ref[(c,) + natural(h, v)]

    lax.fori_loop(0, 2, solve, 0)
    for copy in copies:
        copy.wait()
    hess = -(bv_ref[0] * nat_ref[0, 0, HALO : HALO + rows, :] + bv_ref[1] * nat_ref[1, 0, HALO : HALO + rows, :])
    hess_ref[...] = hess
    low_ref[...] = jnp.broadcast_to(hess.astype(BF16)[None], low_ref.shape)


def project_kernel(panels_ref, probe_ref, out_ref, sums_ref):
    count = panels_ref.shape[0]
    probe = probe_ref[...].reshape(panels_ref.shape[1:])

    def some(i, carry):
        for k in range(4):
            product = panels_ref[4 * i + k].astype(F32) * probe.astype(F32)
            sums_ref[4 * i + k] = jnp.sum(product.reshape(-1, 8, 128), axis=0)
        return carry

    lax.fori_loop(0, count // 4, some, 0)
    table = jnp.sum(sums_ref[...], axis=1)
    table = jnp.concatenate([table, jnp.zeros((128 - count, 128), F32)], axis=0)
    line = lax.dot_general(
        jnp.ones((8, 128), F32), table, (((1,), (1,)), ((), ())),
        precision=lax.Precision.HIGHEST, preferred_element_type=F32,
    )
    line = pltpu.roll(line, lax.axis_index("grp") * count, 1)[0:1]
    out_ref[...] = jnp.broadcast_to(line[None], out_ref.shape)


def add_lines_kernel(lines_ref, out_ref):
    out_ref[...] = jnp.sum(lines_ref[...], axis=0)


def vmem(n):
    return [pl.BlockSpec(memory_space=pltpu.VMEM)] * n


def on_device(
    base_velocity, viscosity, friction, friction_probe, pixel_los, pixel_weight, pixel_cell, pixel_count, panels
):
    n_grp, n_tile = lax.axis_size("grp"), lax.axis_size("tile")
    rows, columns = viscosity.shape
    half = rows // 2
    span = rows + 2 * HALO
    params = pltpu.CompilerParams(vmem_limit_bytes=32 * 2**20)

    inputs = [
        pltpu.with_memory_space_constraint(x, pltpu.HBM)
        for x in (
            base_velocity, viscosity, friction, friction_probe, pixel_los, pixel_weight, pixel_cell, pixel_count
        )
    ]
    slots, fields = pl.pallas_call(
        functools.partial(pack_tiles_kernel, n_tile),
        out_shape=(
            jax.ShapeDtypeStruct((n_tile, half + 16, 128), BF16),
            jax.ShapeDtypeStruct((FIELDS, rows, columns), F32),
        ),
        in_specs=[pl.BlockSpec(memory_space=pltpu.HBM)] * len(inputs),
        out_specs=tuple(vmem(2)),
        scratch_shapes=[pltpu.VMEM(x.shape, x.dtype) for x in inputs] + [pltpu.SemaphoreType.DMA((len(inputs),))],
        compiler_params=params,
        name="pack_tiles",
    )(*inputs)
    got = lax.all_to_all(slots, "tile", split_axis=0, concat_axis=0, tiled=True)

    packet = (FIELDS + 1) * HALO + 6 * n_tile
    ext, pix, packets = pl.pallas_call(
        functools.partial(pack_rows_kernel, n_grp, n_tile),
        out_shape=(
            jax.ShapeDtypeStruct((FIELDS, rows, 256), F32),
            jax.ShapeDtypeStruct((6 * n_tile, 128), F32),
            jax.ShapeDtypeStruct((n_grp, packet, 128), BF16),
        ),
        in_specs=vmem(2),
        out_specs=tuple(vmem(3)),
        compiler_params=params,
        name="pack_rows",
    )(fields, got)
    rims = lax.all_to_all(packets, "grp", split_axis=0, concat_axis=0, tiled=True)

    increment, hessian_probe, probe_low, panels_near = pl.pallas_call(
        functools.partial(solve_kernel, n_grp, n_tile),
        out_shape=(
            jax.ShapeDtypeStruct((2, rows, columns), F32),
            jax.ShapeDtypeStruct((rows, columns), F32),
            jax.ShapeDtypeStruct((n_grp, rows, columns), BF16),
            jax.ShapeDtypeStruct(panels.shape, BF16),
        ),
        in_specs=vmem(3) + [pl.BlockSpec(memory_space=pltpu.HBM)] * 2,
        out_specs=tuple(vmem(4)),
        scratch_shapes=[
            pltpu.VMEM((FIELDS, 2, span, 128), F32),
            pltpu.VMEM((10, span, 256), F32),
            pltpu.VMEM((2, span, 256), F32),
            pltpu.VMEM((2, 2, span, 256), F32),
            pltpu.VMEM((2, 2, span, 128), F32),
            pltpu.VMEM(base_velocity.shape, F32),
            pltpu.SemaphoreType.DMA((2,)),
        ],
        compiler_params=params,
        name="solve",
    )(ext, pix, rims, inputs[0], pltpu.with_memory_space_constraint(panels, pltpu.HBM))

    column = lax.all_to_all(probe_low, "grp", split_axis=0, concat_axis=0, tiled=True)
    partial = pl.pallas_call(
        project_kernel,
        out_shape=jax.ShapeDtypeStruct((n_grp * n_tile, 1, 128), F32),
        in_specs=vmem(2),
        out_specs=pl.BlockSpec(memory_space=pltpu.VMEM),
        scratch_shapes=[pltpu.VMEM((panels.shape[0], 8, 128), F32)],
        compiler_params=params,
        name="project",
    )(panels_near, column)
    everyone = lax.all_to_all(partial, ("grp", "tile"), split_axis=0, concat_axis=0, tiled=True)
    coefficients = pl.pallas_call(
        add_lines_kernel,
        out_shape=jax.ShapeDtypeStruct((1, 128), F32),
        in_specs=vmem(1),
        out_specs=pl.BlockSpec(memory_space=pltpu.VMEM),
        compiler_params=params,
        name="add_lines",
    )(everyone)
    return increment, hessian_probe, coefficients.reshape(128)


def solution(mesh):
    in_specs = (
        P(None, "grp", "tile"),
        P("grp", "tile"),
        P("grp", "tile"),
        P("grp", "tile"),
        P("grp", "tile", None, None),
        P("grp", "tile", None, None),
        P("grp", "tile", None, None),
        P("grp", "tile", None, None),
        P("grp", None, "tile"),
    )
    out_specs = (P(None, "grp", "tile"), P("grp", "tile"), P())
    return jax.shard_map(
        on_device, mesh=mesh, in_specs=in_specs, out_specs=out_specs, check_vma=False
    )
```

```python
import functools

import jax
import jax.numpy as jnp
from jax import lax
from jax.experimental import pallas as pl
from jax.experimental.pallas import tpu as pltpu
from jax.sharding import PartitionSpec as P

SWEEPS = 8
RELAX = 0.8
CAP = 64
HALO = 16
EDGE = 8
FIELDS = 4
STRIPS = 8
F32 = jnp.float32
BF16 = jnp.bfloat16


def lanes(shape=(8, 128)):
    return lax.broadcasted_iota(jnp.int32, shape, len(shape) - 1)


def fetch(sources, targets, sems):
    copies = [pltpu.make_async_copy(s, d, sems.at[i]) for i, (s, d) in enumerate(zip(sources, targets))]
    for copy in copies:
        copy.start()
    return copies


def pack_tiles_kernel(n_tile, *refs):
    sources, (out_ref, fields_ref), targets, sems = refs[:8], refs[8:10], refs[10:18], refs[18]
    copies = fetch(sources, targets, sems)
    bv_ref, visc_ref, fric_ref, fp_ref, los_ref, weight_ref, cell_ref, count_ref = targets
    t = lax.axis_index("tile")
    parity = lax.rem(t, 2)
    rows = visc_ref.shape[0]
    half = rows // 2
    for copy in copies[4:]:
        copy.wait()
    row_lane = lanes((1, 128))
    low = lanes() < CAP
    straight, turned = [], []
    for j in range(n_tile // 2):
        at = pl.ds(j * 128, 128)
        count = jnp.where(
            row_lane < CAP, count_ref[0, 0, :, 2 * j : 2 * j + 1], count_ref[0, 0, :, 2 * j + 1 : 2 * j + 2]
        )
        live = (row_lane & (CAP - 1)) < count
        weight = jnp.where(live, weight_ref[0, 0, :, at], 0.0)
        scaled = jnp.sqrt(weight) * los_ref[0, 0, :, at]
        high = scaled.astype(BF16).astype(F32)
        cell = cell_ref[0, 0, :, at]
        block = jnp.concatenate(
            [
                high, scaled - high,
                lax.shift_right_logical(cell, 7).astype(F32), (cell & 127).astype(F32), jnp.zeros((2, 128), F32),
            ],
            axis=0,
        )
        straight.append(block)
        turned.append(pltpu.roll(block, CAP, 1))
    nothing = jnp.zeros((8, 128), F32)
    in_half = (lanes() // CAP) == parity

    def placed(owner, side):
        if owner < 0 or owner >= n_tile:
            return nothing
        return (straight if owner % 2 == side else turned)[owner // 2]

    for d in range(n_tile):
        solo = jnp.where(parity == d % 2, straight[d // 2], turned[d // 2])
        solo = jnp.where(in_half, solo, 0.0)
        pair = jnp.where(low, placed(d - 1, 0), placed(d + 1, 1))
        out_ref[d, half : half + 16, :] = jnp.concatenate([solo, pair], axis=0).astype(BF16)

    for copy in copies[:4]:
        copy.wait()
    probe = fp_ref[...]
    fields = [-(probe * bv_ref[0]), -(probe * bv_ref[1]), visc_ref[...], fric_ref[...]]
    for f, field in enumerate(fields):
        fields_ref[f] = field
    lane = lanes((half, 128))

    def fold(first_lane):
        packed = jnp.zeros((half, 128), F32)
        for part in range(2):
            for f, field in enumerate(fields):
                start = part * 64 + f * HALO
                piece = field[part * half : (part + 1) * half]
                piece = pltpu.roll(piece, (start - first_lane) % 128, 1)
                packed = jnp.where((lane >= start) & (lane < start + HALO), piece, packed)
        return packed

    @pl.when(t < n_tile - 1)
    def _():
        out_ref[t + 1, 0:half, :] = fold(128 - HALO).astype(BF16)

    @pl.when(t > 0)
    def _():
        out_ref[t - 1, 0:half, :] = fold(0).astype(BF16)


def pack_rows_kernel(n_grp, n_tile, fields_ref, got_ref, ext_ref, pix_ref, out_ref):
    g = lax.axis_index("grp")
    t = lax.axis_index("tile")
    rows = fields_ref.shape[1]
    half = rows // 2
    fields = [fields_ref[f] for f in range(FIELDS)]
    lane = lanes((half, 128))
    right = jnp.where(t < n_tile - 1, got_ref[jnp.minimum(t + 1, n_tile - 1), 0:half, :].astype(F32), 0.0)
    left = jnp.where(t > 0, got_ref[jnp.maximum(t - 1, 0), 0:half, :].astype(F32), 0.0)
    band = lanes((HALO, 128))
    edge_up = jnp.zeros((HALO, 128), F32)
    edge_down = jnp.zeros((HALO, 128), F32)
    for f, field in enumerate(fields):
        ext_ref[f, :, 0:128] = field
        edges = []
        for part in range(2):
            start = part * 64 + f * HALO
            edge = jnp.where(
                lane < HALO,
                pltpu.roll(right, (0 - start) % 128, 1),
                jnp.where(lane >= 128 - HALO, pltpu.roll(left, (128 - HALO - start) % 128, 1), 0.0),
            )
            ext_ref[f, part * half : (part + 1) * half, 128:256] = edge
            edges.append(edge)
        here = (band >= 2 * f * HALO) & (band < 2 * (f + 1) * HALO)
        turn = (2 * f + 1) * HALO % 128
        edge_up = jnp.where(here, pltpu.roll(edges[0][0:HALO], turn, 1), edge_up)
        edge_down = jnp.where(here, pltpu.roll(edges[1][half - HALO :], turn, 1), edge_down)
    low = lanes() < CAP
    near, far = [], []
    for s in range(0, n_tile, 2):
        one = got_ref[s, half : half + 16, :].astype(F32)
        two = got_ref[s + 1, half : half + 16, :].astype(F32)
        near.append(jnp.where(low, one[0:8], two[0:8]))
        far += [one[8:16], two[8:16]]
    blocks = near + far
    pixels = jnp.concatenate(
        [b[0:1] + b[2:3] for b in blocks]
        + [b[1:2] + b[3:4] for b in blocks]
        + [b[4:5] for b in blocks]
        + [b[5:6] for b in blocks],
        axis=0,
    )
    pix_ref[...] = pixels
    pixels = pixels.astype(BF16)

    def send(slot, first, edge):
        for f, field in enumerate(fields):
            out_ref[slot, f * HALO : (f + 1) * HALO, :] = field[first : first + HALO].astype(BF16)
        base = FIELDS * HALO
        out_ref[slot, base : base + HALO, :] = edge.astype(BF16)
        base = base + HALO
        out_ref[slot, base:, :] = pixels

    @pl.when(g > 0)
    def _():
        send(g - 1, 0, edge_up)

    @pl.when(g < n_grp - 1)
    def _():
        send(g + 1, rows - HALO, edge_down)


def solve_kernel(
    n_grp, n_tile, ext_ref, pix_ref, got_ref, bv_hbm, panels_hbm,
    inc_ref, hess_ref, low_ref, panels_ref,
    plane_ref, coef_ref, src_ref, w_ref, nat_ref, bv_ref, sems,
):
    copies = fetch((bv_hbm, panels_hbm), (bv_ref, panels_ref), sems)
    g = lax.axis_index("grp")
    t = lax.axis_index("tile")
    rows = ext_ref.shape[1]
    span = rows + 2 * HALO
    groups = span // STRIPS
    lane = lanes()

    def above(first, size):
        return jnp.where(g > 0, got_ref[jnp.maximum(g - 1, 0), first : first + size, :].astype(F32), 0.0)

    def below(first, size):
        return jnp.where(g < n_grp - 1, got_ref[jnp.minimum(g + 1, n_grp - 1), first : first + size, :].astype(F32), 0.0)

    first_lane = lane == 0
    last_lane = lane == 127

    band = lanes((HALO, 128))
    for f in range(FIELDS):
        for h in range(2):
            plane_ref[f, h, HALO : HALO + rows, :] = ext_ref[f, :, h * 128 : (h + 1) * 128]
        for load, at in ((above, 0), (below, HALO + rows)):
            plane_ref[f, 0, at : at + HALO, :] = load(f * HALO, HALO)
            edge = pltpu.roll(load(FIELDS * HALO, HALO), (0 - (2 * f + 1) * HALO) % 128, 1)
            plane_ref[f, 1, at : at + HALO, :] = jnp.where((band < HALO) | (band >= 128 - HALO), edge, 0.0)

    def strided(f, h, v):
        return plane_ref[f, h, pl.ds(v, STRIPS, stride=groups), :]

    def beside(pair):
        a, b = pair
        ra, rb = pltpu.roll(a, 1, 1), pltpu.roll(b, 1, 1)
        before = (jnp.where(first_lane, rb, ra), jnp.where(first_lane, ra, rb))
        ra, rb = pltpu.roll(a, 127, 1), pltpu.roll(b, 127, 1)
        after = (jnp.where(last_lane, rb, ra), jnp.where(last_lane, ra, rb))
        return before, pair, after

    def row(load, v):
        if v < 0:
            return beside(tuple(pltpu.roll(load(h, groups - 1), 1, 0) for h in range(2)))
        if v == groups:
            return beside(tuple(pltpu.roll(load(h, 0), STRIPS - 1, 0) for h in range(2)))
        return beside(tuple(load(h, v) for h in range(2)))

    strip = lax.broadcasted_iota(jnp.int32, (8, 128), 0)
    col_in = [
        None,
        ((lane < HALO) & (t < n_tile - 1)) | ((lane >= 128 - HALO) & (t > 0)),
    ]
    load_visc = functools.partial(strided, 2)
    prev, cur = row(load_visc, -1), row(load_visc, 0)
    for v in range(groups):
        nxt = row(load_visc, v + 1)
        place = g * rows - HALO + strip * groups + v
        row_in = (place >= 0) & (place < n_grp * rows)
        at = pl.ds(v * 8, 8)
        for h in range(2):
            centre = cur[1][h]
            east = 0.5 * (centre + nxt[1][h])
            west = 0.5 * (centre + prev[1][h])
            north = 0.5 * (centre + cur[2][h])
            south = 0.5 * (centre + cur[0][h])
            node_pp = 0.25 * (centre + nxt[1][h] + cur[2][h] + nxt[2][h])
            node_mm = 0.25 * (centre + prev[1][h] + cur[0][h] + prev[0][h])
            node_pm = 0.25 * (centre + nxt[1][h] + cur[0][h] + nxt[0][h])
            node_mp = 0.25 * (centre + prev[1][h] + cur[2][h] + prev[2][h])
            fric = strided(3, h, v)
            diag_x = fric + 2.0 * (east + west) + (north + south)
            diag_y = fric + (east + west) + 2.0 * (north + south)
            inside = row_in if col_in[h] is None else row_in & col_in[h]
            inv_x = jnp.where(inside, RELAX / jnp.where(inside, diag_x, 1.0), 0.0)
            inv_y = jnp.where(inside, RELAX / jnp.where(inside, diag_y, 1.0), 0.0)
            cols = pl.ds(h * 128, 128)
            for i, plane in enumerate(
                (east, west, north, south, 0.25 * node_pp, 0.25 * node_mm, 0.25 * node_pm, 0.25 * node_mp, inv_x, inv_y)
            ):
                coef_ref[i, at, cols] = plane
            src_ref[0, at, cols] = inv_x * strided(0, h, v)
            src_ref[1, at, cols] = inv_y * strided(1, h, v)
        prev, cur = cur, nxt

    def natural(h, v):
        return (h, pl.ds(v, STRIPS, stride=groups), slice(None))

    def relax():
        w_ref[0] = src_ref[...]

        def sweep(now, later, start):
            rows_seen = {}

            def both(v):
                if v not in rows_seen:
                    rows_seen[v] = tuple(
                        row(lambda h, u, c=c: now[c, pl.ds(u * 8, 8), pl.ds(h * 128, 128)], v) for c in range(2)
                    )
                return rows_seen[v]

            for p in range(groups):
                v = (p + start) % groups
                prev, cur, nxt = both(v - 1), both(v), both(v + 1)
                at = pl.ds(v * 8, 8)
                for h in range(2):
                    cols = pl.ds(h * 128, 128)
                    east, west, north, south, pp, mm, pm, mp, inv_x, inv_y = (
                        coef_ref[i, at, cols] for i in range(10)
                    )

                    def along(c):
                        return (
                            east * nxt[c][1][h] + west * prev[c][1][h],
                            north * cur[c][2][h] + south * cur[c][0][h],
                        )

                    def cross(c):
                        return (
                            pp * nxt[c][2][h] + mm * prev[c][0][h] - pm * nxt[c][0][h] - mp * prev[c][2][h]
                        )

                    one, two = along(0)
                    sum_x = 2.0 * one + two + cross(1)
                    one, two = along(1)
                    sum_y = one + 2.0 * two + cross(0)
                    for c, new in ((0, inv_x * sum_x), (1, inv_y * sum_y)):
                        new = (1.0 - RELAX) * cur[c][1][h] + src_ref[c, at, cols] + new
                        if later is None:
                            nat_ref[(c,) + natural(h, v)] = new
                        else:
                            later[c, at, cols] = new

        def two_sweeps(_, carry):
            sweep(w_ref.at[0], w_ref.at[1], 0)
            sweep(w_ref.at[1], w_ref.at[0], 1)
            return carry

        lax.fori_loop(0, (SWEEPS - 2) // 2, two_sweeps, 0)
        sweep(w_ref.at[0], None, 0)

    def solve(phase, carry):
        relax()

        @pl.when(phase == 0)
        def _():
            for c in range(2):
                inc_ref[c] = nat_ref[c, 0, HALO : HALO + rows, :]
            misfit()

        return carry

    def misfit():
        n_near, n_all = n_tile // 2, 3 * n_tile // 2
        low = lanes((n_tile, 128)) < CAP
        spans = ((0, HALO, rows), (-1, HALO - EDGE, EDGE), (1, HALO + rows, EDGE))
        rim_lane = lanes((2 * rows, 128))
        jobs = []
        for delta, first, size in spans:
            if delta == 0:
                values = pix_ref[...]
            else:
                base = (FIELDS + 1) * HALO
                values = (above if delta < 0 else below)(base, 4 * n_all)
            los_x, los_y, r, c = (values[q * n_all : (q + 1) * n_all] for q in range(4))
            if delta < 0:
                r = r - (rows - EDGE)
            in_rim = c[n_near:] + jnp.where(low, float(EDGE) - 128.0, float(EDGE))
            for h, begin, count, lane_of in ((0, 0, n_near, c[0:n_near]), (1, n_near, n_tile, in_rim)):
                parts = []
                for comp in range(2):
                    part = nat_ref[comp, h, first : first + size, :]
                    parts.append(part if h == 0 else pltpu.roll(part, EDGE, 1))
                field = jnp.concatenate(parts, axis=0)
                high = field.astype(BF16).astype(F32)
                rest = field - high
                if h == 0:
                    stacked = jnp.concatenate([high.astype(BF16), rest.astype(BF16)], axis=1)
                else:
                    lane_here = rim_lane[0 : 2 * size]
                    stacked = jnp.where(lane_here < 2 * EDGE, high, pltpu.roll(rest, 2 * EDGE, 1))
                    stacked = jnp.where(lane_here < 4 * EDGE, stacked, 0.0).astype(BF16)
                jobs.append((h, first, size, begin, count, lane_of, los_x, los_y, r, stacked))

        nat_ref[...] = jnp.zeros_like(nat_ref)
        for h, first, size, begin, count, lane_of, los_x, los_y, r, stacked in jobs:
            chunk = 4 if h == 0 else 8
            depth = 128 if h == 0 else 2 * EDGE
            wide = chunk * 128
            row_id = lax.broadcasted_iota(jnp.int32, (size, wide), 0).astype(F32)
            lane_id = lax.broadcasted_iota(jnp.int32, (depth, wide), 0).astype(F32)
            total = jnp.zeros((4 * size, 128), F32)
            for j in range(0, count, chunk):

                def line(table, offset):
                    return jnp.concatenate([table[offset + i : offset + i + 1] for i in range(j, j + chunk)], axis=1)

                line_x, line_y = line(los_x, begin), line(los_y, begin)
                hot = jnp.where(lane_id == line(lane_of, 0), 1.0, 0.0).astype(BF16)
                here = row_id == line(r, begin)
                twice = [hot, hot]
                if h == 1:
                    twice.append(jnp.zeros((128 - 2 * depth, wide), BF16))
                    hot = jnp.concatenate([hot, jnp.zeros((128 - depth, wide), BF16)], axis=0)
                got = jnp.dot(stacked, jnp.concatenate(twice, axis=0), preferred_element_type=F32)
                got_x = jnp.sum(jnp.where(here, got[0:size], 0.0), axis=0, keepdims=True)
                got_y = jnp.sum(jnp.where(here, got[size:], 0.0), axis=0, keepdims=True)
                amount = line_x * got_x + line_y * got_y
                terms = [amount * line_x, amount * line_y]
                highs = [p.astype(BF16).astype(F32) for p in terms]
                terms = highs + [p - q for p, q in zip(terms, highs)]
                spread = jnp.concatenate([jnp.where(here, p, 0.0) for p in terms], axis=0).astype(BF16)
                total = total + lax.dot_general(spread, hot, (((1,), (1,)), ((), ())), preferred_element_type=F32)
            total = total[0 : 2 * size] + total[2 * size :]
            if h == 1:
                total = pltpu.roll(total, 128 - EDGE, 1)
            for c in range(2):
                nat_ref[c, h, first : first + size, :] = total[c * size : (c + 1) * size]

        for v in range(groups):
            at = pl.ds(v * 8, 8)
            for h in range(2):
                cols = pl.ds(h * 128, 128)
                for c in range(2):
                    src_ref[c, at, cols] = coef_ref[8 + c, at, cols] * nat_ref[(c,) + natural(h, v)]

    lax.fori_loop(0, 2, solve, 0)
    for copy in copies:
        copy.wait()
    hess = -(bv_ref[0] * nat_ref[0, 0, HALO : HALO + rows, :] + bv_ref[1] * nat_ref[1, 0, HALO : HALO + rows, :])
    hess_ref[...] = hess
    low_ref[...] = jnp.broadcast_to(hess.astype(BF16)[None], low_ref.shape)


def project_kernel(panels_ref, probe_ref, out_ref):
    count = panels_ref.shape[0]
    probe = probe_ref[...].astype(F32).reshape(panels_ref.shape[1:])
    sums = []
    for k in range(count):
        product = panels_ref[k].astype(F32) * probe
        sums.append(jnp.sum(product, axis=0, keepdims=True))
    sums.append(jnp.zeros((128 - count, 128), F32))
    table = jnp.concatenate(sums, axis=0)
    line = lax.dot_general(
        jnp.ones((8, 128), F32), table, (((1,), (1,)), ((), ())),
        precision=lax.Precision.HIGHEST, preferred_element_type=F32,
    )
    line = pltpu.roll(line, lax.axis_index("grp") * count, 1)[0:1]
    out_ref[...] = jnp.broadcast_to(line[None], out_ref.shape)


def add_lines_kernel(lines_ref, out_ref):
    out_ref[...] = jnp.sum(lines_ref[...], axis=0)


def vmem(n):
    return [pl.BlockSpec(memory_space=pltpu.VMEM)] * n


def on_device(
    base_velocity, viscosity, friction, friction_probe, pixel_los, pixel_weight, pixel_cell, pixel_count, panels
):
    n_grp, n_tile = lax.axis_size("grp"), lax.axis_size("tile")
    rows, columns = viscosity.shape
    half = rows // 2
    span = rows + 2 * HALO
    params = pltpu.CompilerParams(vmem_limit_bytes=32 * 2**20)

    inputs = [
        pltpu.with_memory_space_constraint(x, pltpu.HBM)
        for x in (
            base_velocity, viscosity, friction, friction_probe, pixel_los, pixel_weight, pixel_cell, pixel_count
        )
    ]
    slots, fields = pl.pallas_call(
        functools.partial(pack_tiles_kernel, n_tile),
        out_shape=(
            jax.ShapeDtypeStruct((n_tile, half + 16, 128), BF16),
            jax.ShapeDtypeStruct((FIELDS, rows, columns), F32),
        ),
        in_specs=[pl.BlockSpec(memory_space=pltpu.HBM)] * len(inputs),
        out_specs=tuple(vmem(2)),
        scratch_shapes=[pltpu.VMEM(x.shape, x.dtype) for x in inputs] + [pltpu.SemaphoreType.DMA((len(inputs),))],
        compiler_params=params,
        name="pack_tiles",
    )(*inputs)
    got = lax.all_to_all(slots, "tile", split_axis=0, concat_axis=0, tiled=True)

    packet = (FIELDS + 1) * HALO + 6 * n_tile
    ext, pix, packets = pl.pallas_call(
        functools.partial(pack_rows_kernel, n_grp, n_tile),
        out_shape=(
            jax.ShapeDtypeStruct((FIELDS, rows, 256), F32),
            jax.ShapeDtypeStruct((6 * n_tile, 128), F32),
            jax.ShapeDtypeStruct((n_grp, packet, 128), BF16),
        ),
        in_specs=vmem(2),
        out_specs=tuple(vmem(3)),
        compiler_params=params,
        name="pack_rows",
    )(fields, got)
    rims = lax.all_to_all(packets, "grp", split_axis=0, concat_axis=0, tiled=True)

    increment, hessian_probe, probe_low, panels_near = pl.pallas_call(
        functools.partial(solve_kernel, n_grp, n_tile),
        out_shape=(
            jax.ShapeDtypeStruct((2, rows, columns), F32),
            jax.ShapeDtypeStruct((rows, columns), F32),
            jax.ShapeDtypeStruct((n_grp, rows, columns), BF16),
            jax.ShapeDtypeStruct(panels.shape, BF16),
        ),
        in_specs=vmem(3) + [pl.BlockSpec(memory_space=pltpu.HBM)] * 2,
        out_specs=tuple(vmem(4)),
        scratch_shapes=[
            pltpu.VMEM((FIELDS, 2, span, 128), F32),
            pltpu.VMEM((10, span, 256), F32),
            pltpu.VMEM((2, span, 256), F32),
            pltpu.VMEM((2, 2, span, 256), F32),
            pltpu.VMEM((2, 2, span, 128), F32),
            pltpu.VMEM(base_velocity.shape, F32),
            pltpu.SemaphoreType.DMA((2,)),
        ],
        compiler_params=params,
        name="solve",
    )(ext, pix, rims, inputs[0], pltpu.with_memory_space_constraint(panels, pltpu.HBM))

    column = lax.all_to_all(probe_low, "grp", split_axis=0, concat_axis=0, tiled=True)
    partial = pl.pallas_call(
        project_kernel,
        out_shape=jax.ShapeDtypeStruct((n_grp * n_tile, 1, 128), F32),
        in_specs=vmem(2),
        out_specs=pl.BlockSpec(memory_space=pltpu.VMEM),
        compiler_params=params,
        name="project",
    )(panels_near, column)
    everyone = lax.all_to_all(partial, ("grp", "tile"), split_axis=0, concat_axis=0, tiled=True)
    coefficients = pl.pallas_call(
        add_lines_kernel,
        out_shape=jax.ShapeDtypeStruct((1, 128), F32),
        in_specs=vmem(1),
        out_specs=pl.BlockSpec(memory_space=pltpu.VMEM),
        compiler_params=params,
        name="add_lines",
    )(everyone)
    return increment, hessian_probe, coefficients.reshape(128)


def solution(mesh):
    in_specs = (
        P(None, "grp", "tile"),
        P("grp", "tile"),
        P("grp", "tile"),
        P("grp", "tile"),
        P("grp", "tile", None, None),
        P("grp", "tile", None, None),
        P("grp", "tile", None, None),
        P("grp", "tile", None, None),
        P("grp", None, "tile"),
    )
    out_specs = (P(None, "grp", "tile"), P("grp", "tile"), P())
    return jax.shard_map(
        on_device, mesh=mesh, in_specs=in_specs, out_specs=out_specs, check_vma=False
    )
```

```python
import functools

import jax
import jax.numpy as jnp
from jax import lax
from jax.experimental import pallas as pl
from jax.experimental.pallas import tpu as pltpu
from jax.sharding import PartitionSpec as P

SWEEPS = 8
RELAX = 0.8
CAP = 64
HALO = 16
EDGE = 8
FIELDS = 4
STRIPS = 8
F32 = jnp.float32
BF16 = jnp.bfloat16


def lanes(shape=(8, 128)):
    return lax.broadcasted_iota(jnp.int32, shape, len(shape) - 1)


def fetch(sources, targets, sems):
    copies = [pltpu.make_async_copy(s, d, sems.at[i]) for i, (s, d) in enumerate(zip(sources, targets))]
    for copy in copies:
        copy.start()
    return copies


def pack_tiles_kernel(n_tile, *refs):
    sources, (out_ref, fields_ref), targets, sems = refs[:8], refs[8:10], refs[10:18], refs[18]
    copies = fetch(sources, targets, sems)
    bv_ref, visc_ref, fric_ref, fp_ref, los_ref, weight_ref, cell_ref, count_ref = targets
    t = lax.axis_index("tile")
    parity = lax.rem(t, 2)
    rows = visc_ref.shape[0]
    half = rows // 2
    for copy in copies[4:]:
        copy.wait()
    row_lane = lanes((1, 128))
    low = lanes() < CAP
    straight, turned = [], []
    for j in range(n_tile // 2):
        at = pl.ds(j * 128, 128)
        count = jnp.where(
            row_lane < CAP, count_ref[0, 0, :, 2 * j : 2 * j + 1], count_ref[0, 0, :, 2 * j + 1 : 2 * j + 2]
        )
        live = (row_lane & (CAP - 1)) < count
        weight = jnp.where(live, weight_ref[0, 0, :, at], 0.0)
        scaled = jnp.sqrt(weight) * los_ref[0, 0, :, at]
        high = scaled.astype(BF16).astype(F32)
        cell = cell_ref[0, 0, :, at]
        block = jnp.concatenate(
            [
                high, scaled - high,
                lax.shift_right_logical(cell, 7).astype(F32), (cell & 127).astype(F32), jnp.zeros((2, 128), F32),
            ],
            axis=0,
        )
        straight.append(block)
        turned.append(pltpu.roll(block, CAP, 1))
    nothing = jnp.zeros((8, 128), F32)
    in_half = (lanes() // CAP) == parity

    def placed(owner, side):
        if owner < 0 or owner >= n_tile:
            return nothing
        return (straight if owner % 2 == side else turned)[owner // 2]

    for d in range(n_tile):
        solo = jnp.where(parity == d % 2, straight[d // 2], turned[d // 2])
        solo = jnp.where(in_half, solo, 0.0)
        pair = jnp.where(low, placed(d - 1, 0), placed(d + 1, 1))
        out_ref[d, half : half + 16, :] = jnp.concatenate([solo, pair], axis=0).astype(BF16)

    for copy in copies[:4]:
        copy.wait()
    probe = fp_ref[...]
    fields = [-(probe * bv_ref[0]), -(probe * bv_ref[1]), visc_ref[...], fric_ref[...]]
    for f, field in enumerate(fields):
        fields_ref[f] = field
    lane = lanes((half, 128))

    def fold(first_lane):
        packed = jnp.zeros((half, 128), F32)
        for part in range(2):
            for f, field in enumerate(fields):
                start = part * 64 + f * HALO
                piece = field[part * half : (part + 1) * half]
                piece = pltpu.roll(piece, (start - first_lane) % 128, 1)
                packed = jnp.where((lane >= start) & (lane < start + HALO), piece, packed)
        return packed

    @pl.when(t < n_tile - 1)
    def _():
        out_ref[t + 1, 0:half, :] = fold(128 - HALO).astype(BF16)

    @pl.when(t > 0)
    def _():
        out_ref[t - 1, 0:half, :] = fold(0).astype(BF16)


def pack_rows_kernel(n_tile, fields_ref, got_ref, ext_ref, pix_ref, up_ref, down_ref):
    t = lax.axis_index("tile")
    rows = fields_ref.shape[1]
    half = rows // 2
    fields = [fields_ref[f] for f in range(FIELDS)]
    lane = lanes((half, 128))
    right = jnp.where(t < n_tile - 1, got_ref[jnp.minimum(t + 1, n_tile - 1), 0:half, :].astype(F32), 0.0)
    left = jnp.where(t > 0, got_ref[jnp.maximum(t - 1, 0), 0:half, :].astype(F32), 0.0)
    band = lanes((HALO, 128))
    edge_up = jnp.zeros((HALO, 128), F32)
    edge_down = jnp.zeros((HALO, 128), F32)
    for f, field in enumerate(fields):
        ext_ref[f, :, 0:128] = field
        edges = []
        for part in range(2):
            start = part * 64 + f * HALO
            edge = jnp.where(
                lane < HALO,
                pltpu.roll(right, (0 - start) % 128, 1),
                jnp.where(lane >= 128 - HALO, pltpu.roll(left, (128 - HALO - start) % 128, 1), 0.0),
            )
            ext_ref[f, part * half : (part + 1) * half, 128:256] = edge
            edges.append(edge)
        here = (band >= 2 * f * HALO) & (band < 2 * (f + 1) * HALO)
        turn = (2 * f + 1) * HALO % 128
        edge_up = jnp.where(here, pltpu.roll(edges[0][0:HALO], turn, 1), edge_up)
        edge_down = jnp.where(here, pltpu.roll(edges[1][half - HALO :], turn, 1), edge_down)
    low = lanes() < CAP
    near, far = [], []
    for s in range(0, n_tile, 2):
        one = got_ref[s, half : half + 16, :].astype(F32)
        two = got_ref[s + 1, half : half + 16, :].astype(F32)
        near.append(jnp.where(low, one[0:8], two[0:8]))
        far += [one[8:16], two[8:16]]
    blocks = near + far
    pixels = jnp.concatenate(
        [b[0:1] + b[2:3] for b in blocks]
        + [b[1:2] + b[3:4] for b in blocks]
        + [b[4:5] for b in blocks]
        + [b[5:6] for b in blocks],
        axis=0,
    )
    pix_ref[...] = pixels
    pixels = pixels.astype(BF16)

    for ref, first, edge in ((up_ref, 0, edge_up), (down_ref, rows - HALO, edge_down)):
        for f, field in enumerate(fields):
            ref[f * HALO : (f + 1) * HALO, :] = field[first : first + HALO].astype(BF16)
        base = FIELDS * HALO
        ref[base : base + HALO, :] = edge.astype(BF16)
        ref[base + HALO :, :] = pixels


def solve_kernel(
    n_grp, n_tile, ext_ref, pix_ref, above_ref, below_ref, bv_hbm, panels_hbm,
    inc_ref, hess_ref, low_ref, panels_ref,
    plane_ref, coef_ref, src_ref, w_ref, nat_ref, bv_ref, sems,
):
    copies = fetch((bv_hbm, panels_hbm), (bv_ref, panels_ref), sems)
    g = lax.axis_index("grp")
    t = lax.axis_index("tile")
    rows = ext_ref.shape[1]
    span = rows + 2 * HALO
    groups = span // STRIPS
    lane = lanes()

    def above(first, size):
        return jnp.where(g > 0, above_ref[first : first + size, :].astype(F32), 0.0)

    def below(first, size):
        return jnp.where(g < n_grp - 1, below_ref[first : first + size, :].astype(F32), 0.0)

    first_lane = lane == 0
    last_lane = lane == 127

    band = lanes((HALO, 128))
    for f in range(FIELDS):
        for h in range(2):
            plane_ref[f, h, HALO : HALO + rows, :] = ext_ref[f, :, h * 128 : (h + 1) * 128]
        for load, at in ((above, 0), (below, HALO + rows)):
            plane_ref[f, 0, at : at + HALO, :] = load(f * HALO, HALO)
            edge = pltpu.roll(load(FIELDS * HALO, HALO), (0 - (2 * f + 1) * HALO) % 128, 1)
            plane_ref[f, 1, at : at + HALO, :] = jnp.where((band < HALO) | (band >= 128 - HALO), edge, 0.0)

    def strided(f, h, v):
        return plane_ref[f, h, pl.ds(v, STRIPS, stride=groups), :]

    def beside(pair):
        a, b = pair
        ra, rb = pltpu.roll(a, 1, 1), pltpu.roll(b, 1, 1)
        before = (jnp.where(first_lane, rb, ra), jnp.where(first_lane, ra, rb))
        ra, rb = pltpu.roll(a, 127, 1), pltpu.roll(b, 127, 1)
        after = (jnp.where(last_lane, rb, ra), jnp.where(last_lane, ra, rb))
        return before, pair, after

    def row(load, v):
        if v < 0:
            return beside(tuple(pltpu.roll(load(h, groups - 1), 1, 0) for h in range(2)))
        if v == groups:
            return beside(tuple(pltpu.roll(load(h, 0), STRIPS - 1, 0) for h in range(2)))
        return beside(tuple(load(h, v) for h in range(2)))

    strip = lax.broadcasted_iota(jnp.int32, (8, 128), 0)
    col_in = [
        None,
        ((lane < HALO) & (t < n_tile - 1)) | ((lane >= 128 - HALO) & (t > 0)),
    ]
    load_visc = functools.partial(strided, 2)
    prev, cur = row(load_visc, -1), row(load_visc, 0)
    for v in range(groups):
        nxt = row(load_visc, v + 1)
        place = g * rows - HALO + strip * groups + v
        row_in = (place >= 0) & (place < n_grp * rows)
        at = pl.ds(v * 8, 8)
        for h in range(2):
            centre = cur[1][h]
            east = 0.5 * (centre + nxt[1][h])
            west = 0.5 * (centre + prev[1][h])
            north = 0.5 * (centre + cur[2][h])
            south = 0.5 * (centre + cur[0][h])
            node_pp = 0.25 * (centre + nxt[1][h] + cur[2][h] + nxt[2][h])
            node_mm = 0.25 * (centre + prev[1][h] + cur[0][h] + prev[0][h])
            node_pm = 0.25 * (centre + nxt[1][h] + cur[0][h] + nxt[0][h])
            node_mp = 0.25 * (centre + prev[1][h] + cur[2][h] + prev[2][h])
            fric = strided(3, h, v)
            diag_x = fric + 2.0 * (east + west) + (north + south)
            diag_y = fric + (east + west) + 2.0 * (north + south)
            inside = row_in if col_in[h] is None else row_in & col_in[h]
            inv_x = jnp.where(inside, RELAX / jnp.where(inside, diag_x, 1.0), 0.0)
            inv_y = jnp.where(inside, RELAX / jnp.where(inside, diag_y, 1.0), 0.0)
            cols = pl.ds(h * 128, 128)
            for i, plane in enumerate(
                (east, west, north, south, 0.25 * node_pp, 0.25 * node_mm, 0.25 * node_pm, 0.25 * node_mp, inv_x, inv_y)
            ):
                coef_ref[i, at, cols] = plane
            src_ref[0, at, cols] = inv_x * strided(0, h, v)
            src_ref[1, at, cols] = inv_y * strided(1, h, v)
        prev, cur = cur, nxt

    def natural(h, v):
        return (h, pl.ds(v, STRIPS, stride=groups), slice(None))

    def relax():
        w_ref[0] = src_ref[...]

        def sweep(now, later, start):
            rows_seen = {}

            def both(v):
                if v not in rows_seen:
                    rows_seen[v] = tuple(
                        row(lambda h, u, c=c: now[c, pl.ds(u * 8, 8), pl.ds(h * 128, 128)], v) for c in range(2)
                    )
                return rows_seen[v]

            for p in range(groups):
                v = (p + start) % groups
                prev, cur, nxt = both(v - 1), both(v), both(v + 1)
                at = pl.ds(v * 8, 8)
                for h in range(2):
                    cols = pl.ds(h * 128, 128)
                    east, west, north, south, pp, mm, pm, mp, inv_x, inv_y = (
                        coef_ref[i, at, cols] for i in range(10)
                    )

                    def along(c):
                        return (
                            east * nxt[c][1][h] + west * prev[c][1][h],
                            north * cur[c][2][h] + south * cur[c][0][h],
                        )

                    def cross(c):
                        return (
                            pp * nxt[c][2][h] + mm * prev[c][0][h] - pm * nxt[c][0][h] - mp * prev[c][2][h]
                        )

                    one, two = along(0)
                    sum_x = 2.0 * one + two + cross(1)
                    one, two = along(1)
                    sum_y = one + 2.0 * two + cross(0)
                    for c, new in ((0, inv_x * sum_x), (1, inv_y * sum_y)):
                        new = (1.0 - RELAX) * cur[c][1][h] + src_ref[c, at, cols] + new
                        if later is None:
                            nat_ref[(c,) + natural(h, v)] = new
                        else:
                            later[c, at, cols] = new

        def three_sweeps(_, carry):
            for k in range(3):
                sweep(w_ref.at[k], w_ref.at[(k + 1) % 3], k)
            return carry

        lax.fori_loop(0, (SWEEPS - 2) // 3, three_sweeps, 0)
        sweep(w_ref.at[0], None, 0)

    def solve(phase, carry):
        relax()

        @pl.when(phase == 0)
        def _():
            for c in range(2):
                inc_ref[c] = nat_ref[c, 0, HALO : HALO + rows, :]
            misfit()

        return carry

    def misfit():
        n_near, n_all = n_tile // 2, 3 * n_tile // 2
        low = lanes((n_tile, 128)) < CAP
        spans = ((0, HALO, rows), (-1, HALO - EDGE, EDGE), (1, HALO + rows, EDGE))
        rim_lane = lanes((2 * rows, 128))
        jobs = []
        for delta, first, size in spans:
            if delta == 0:
                values = pix_ref[...]
            else:
                base = (FIELDS + 1) * HALO
                values = (above if delta < 0 else below)(base, 4 * n_all)
            los_x, los_y, r, c = (values[q * n_all : (q + 1) * n_all] for q in range(4))
            if delta < 0:
                r = r - (rows - EDGE)
            in_rim = c[n_near:] + jnp.where(low, float(EDGE) - 128.0, float(EDGE))
            for h, begin, count, lane_of in ((0, 0, n_near, c[0:n_near]), (1, n_near, n_tile, in_rim)):
                parts = []
                for comp in range(2):
                    part = nat_ref[comp, h, first : first + size, :]
                    parts.append(part if h == 0 else pltpu.roll(part, EDGE, 1))
                field = jnp.concatenate(parts, axis=0)
                high = field.astype(BF16).astype(F32)
                rest = field - high
                if h == 0:
                    stacked = jnp.concatenate([high.astype(BF16), rest.astype(BF16)], axis=1)
                else:
                    lane_here = rim_lane[0 : 2 * size]
                    stacked = jnp.where(lane_here < 2 * EDGE, high, pltpu.roll(rest, 2 * EDGE, 1))
                    stacked = jnp.where(lane_here < 4 * EDGE, stacked, 0.0).astype(BF16)
                jobs.append((h, first, size, begin, count, lane_of, los_x, los_y, r, stacked))

        nat_ref[...] = jnp.zeros_like(nat_ref)
        for h, first, size, begin, count, lane_of, los_x, los_y, r, stacked in jobs:
            chunk = 4 if h == 0 else 8
            depth = 128 if h == 0 else 2 * EDGE
            wide = chunk * 128
            row_id = lax.broadcasted_iota(jnp.int32, (size, wide), 0).astype(F32)
            lane_id = lax.broadcasted_iota(jnp.int32, (depth, wide), 0).astype(F32)
            total = jnp.zeros((4 * size, 128), F32)
            for j in range(0, count, chunk):

                def line(table, offset):
                    return jnp.concatenate([table[offset + i : offset + i + 1] for i in range(j, j + chunk)], axis=1)

                line_x, line_y = line(los_x, begin), line(los_y, begin)
                hot = jnp.where(lane_id == line(lane_of, 0), 1.0, 0.0).astype(BF16)
                here = row_id == line(r, begin)
                twice = [hot, hot]
                if h == 1:
                    twice.append(jnp.zeros((128 - 2 * depth, wide), BF16))
                    hot = jnp.concatenate([hot, jnp.zeros((128 - depth, wide), BF16)], axis=0)
                got = jnp.dot(stacked, jnp.concatenate(twice, axis=0), preferred_element_type=F32)
                got_x = jnp.sum(jnp.where(here, got[0:size], 0.0), axis=0, keepdims=True)
                got_y = jnp.sum(jnp.where(here, got[size:], 0.0), axis=0, keepdims=True)
                amount = line_x * got_x + line_y * got_y
                terms = [amount * line_x, amount * line_y]
                highs = [p.astype(BF16).astype(F32) for p in terms]
                terms = highs + [p - q for p, q in zip(terms, highs)]
                spread = jnp.concatenate([jnp.where(here, p, 0.0) for p in terms], axis=0).astype(BF16)
                total = total + lax.dot_general(spread, hot, (((1,), (1,)), ((), ())), preferred_element_type=F32)
            total = total[0 : 2 * size] + total[2 * size :]
            if h == 1:
                total = pltpu.roll(total, 128 - EDGE, 1)
            for c in range(2):
                nat_ref[c, h, first : first + size, :] = total[c * size : (c + 1) * size]

        for v in range(groups):
            at = pl.ds(v * 8, 8)
            for h in range(2):
                cols = pl.ds(h * 128, 128)
                for c in range(2):
                    src_ref[c, at, cols] = coef_ref[8 + c, at, cols] * nat_ref[(c,) + natural(h, v)]

    lax.fori_loop(0, 2, solve, 0)
    for copy in copies:
        copy.wait()
    hess = -(bv_ref[0] * nat_ref[0, 0, HALO : HALO + rows, :] + bv_ref[1] * nat_ref[1, 0, HALO : HALO + rows, :])
    hess_ref[...] = hess
    low_ref[...] = hess.astype(BF16)


def project_kernel(panels_ref, *refs):
    blocks, out_ref, probe_ref = refs[:-2], refs[-2], refs[-1]
    count = panels_ref.shape[0]
    for k, block in enumerate(blocks):
        probe_ref[lax.rem(lax.axis_index("grp") + len(blocks) - k, len(blocks))] = block[...]
    probe = probe_ref[...].astype(F32).reshape(panels_ref.shape[1:])
    sums = []
    for k in range(count):
        product = panels_ref[k].astype(F32) * probe
        sums.append(jnp.sum(product, axis=0, keepdims=True))
    sums.append(jnp.zeros((128 - count, 128), F32))
    table = jnp.concatenate(sums, axis=0)
    line = lax.dot_general(
        jnp.ones((8, 128), F32), table, (((1,), (1,)), ((), ())),
        precision=lax.Precision.HIGHEST, preferred_element_type=F32,
    )
    line = pltpu.roll(line, lax.axis_index("grp") * count, 1)[0:1]
    out_ref[...] = jnp.broadcast_to(line[None], out_ref.shape)


def add_lines_kernel(lines_ref, out_ref):
    out_ref[...] = jnp.sum(lines_ref[...], axis=0)


def vmem(n):
    return [pl.BlockSpec(memory_space=pltpu.VMEM)] * n


def on_device(
    base_velocity, viscosity, friction, friction_probe, pixel_los, pixel_weight, pixel_cell, pixel_count, panels
):
    n_grp, n_tile = lax.axis_size("grp"), lax.axis_size("tile")
    rows, columns = viscosity.shape
    half = rows // 2
    span = rows + 2 * HALO
    params = pltpu.CompilerParams(vmem_limit_bytes=32 * 2**20)

    inputs = [
        pltpu.with_memory_space_constraint(x, pltpu.HBM)
        for x in (
            base_velocity, viscosity, friction, friction_probe, pixel_los, pixel_weight, pixel_cell, pixel_count
        )
    ]
    slots, fields = pl.pallas_call(
        functools.partial(pack_tiles_kernel, n_tile),
        out_shape=(
            jax.ShapeDtypeStruct((n_tile, half + 16, 128), BF16),
            jax.ShapeDtypeStruct((FIELDS, rows, columns), F32),
        ),
        in_specs=[pl.BlockSpec(memory_space=pltpu.HBM)] * len(inputs),
        out_specs=tuple(vmem(2)),
        scratch_shapes=[pltpu.VMEM(x.shape, x.dtype) for x in inputs] + [pltpu.SemaphoreType.DMA((len(inputs),))],
        compiler_params=params,
        name="pack_tiles",
    )(*inputs)
    got = lax.all_to_all(slots, "tile", split_axis=0, concat_axis=0, tiled=True)

    packet = (FIELDS + 1) * HALO + 6 * n_tile
    ext, pix, up, down = pl.pallas_call(
        functools.partial(pack_rows_kernel, n_tile),
        out_shape=(
            jax.ShapeDtypeStruct((FIELDS, rows, 256), F32),
            jax.ShapeDtypeStruct((6 * n_tile, 128), F32),
            jax.ShapeDtypeStruct((packet, 128), BF16),
            jax.ShapeDtypeStruct((packet, 128), BF16),
        ),
        in_specs=vmem(2),
        out_specs=tuple(vmem(4)),
        compiler_params=params,
        name="pack_rows",
    )(fields, got)
    above = lax.ppermute(down, "grp", [(i, (i + 1) % n_grp) for i in range(n_grp)])
    below = lax.ppermute(up, "grp", [((i + 1) % n_grp, i) for i in range(n_grp)])

    increment, hessian_probe, probe_low, panels_near = pl.pallas_call(
        functools.partial(solve_kernel, n_grp, n_tile),
        out_shape=(
            jax.ShapeDtypeStruct((2, rows, columns), F32),
            jax.ShapeDtypeStruct((rows, columns), F32),
            jax.ShapeDtypeStruct((rows, columns), BF16),
            jax.ShapeDtypeStruct(panels.shape, BF16),
        ),
        in_specs=vmem(4) + [pl.BlockSpec(memory_space=pltpu.HBM)] * 2,
        out_specs=tuple(vmem(4)),
        scratch_shapes=[
            pltpu.VMEM((FIELDS, 2, span, 128), F32),
            pltpu.VMEM((10, span, 256), F32),
            pltpu.VMEM((2, span, 256), F32),
            pltpu.VMEM((3, 2, span, 256), F32),
            pltpu.VMEM((2, 2, span, 128), F32),
            pltpu.VMEM(base_velocity.shape, F32),
            pltpu.SemaphoreType.DMA((2,)),
        ],
        compiler_params=params,
        name="solve",
    )(ext, pix, above, below, inputs[0], pltpu.with_memory_space_constraint(panels, pltpu.HBM))

    column = [probe_low] + [
        lax.ppermute(probe_low, "grp", [(i, (i + k) % n_grp) for i in range(n_grp)]) for k in range(1, n_grp)
    ]
    partial = pl.pallas_call(
        project_kernel,
        out_shape=jax.ShapeDtypeStruct((n_grp * n_tile, 1, 128), F32),
        in_specs=vmem(1 + n_grp),
        out_specs=pl.BlockSpec(memory_space=pltpu.VMEM),
        scratch_shapes=[pltpu.VMEM((n_grp, rows, columns), BF16)],
        compiler_params=params,
        name="project",
    )(panels_near, *column)
    everyone = lax.all_to_all(partial, ("grp", "tile"), split_axis=0, concat_axis=0, tiled=True)
    coefficients = pl.pallas_call(
        add_lines_kernel,
        out_shape=jax.ShapeDtypeStruct((1, 128), F32),
        in_specs=vmem(1),
        out_specs=pl.BlockSpec(memory_space=pltpu.VMEM),
        compiler_params=params,
        name="add_lines",
    )(everyone)
    return increment, hessian_probe, coefficients.reshape(128)


def solution(mesh):
    in_specs = (
        P(None, "grp", "tile"),
        P("grp", "tile"),
        P("grp", "tile"),
        P("grp", "tile"),
        P("grp", "tile", None, None),
        P("grp", "tile", None, None),
        P("grp", "tile", None, None),
        P("grp", "tile", None, None),
        P("grp", None, "tile"),
    )
    out_specs = (P(None, "grp", "tile"), P("grp", "tile"), P())
    return jax.shard_map(
        on_device, mesh=mesh, in_specs=in_specs, out_specs=out_specs, check_vma=False
    )
```

```python
import functools

import jax
import jax.numpy as jnp
from jax import lax
from jax.experimental import pallas as pl
from jax.experimental.pallas import tpu as pltpu
from jax.sharding import PartitionSpec as P

SWEEPS = 8
RELAX = 0.8
CAP = 64
HALO = 16
EDGE = 8
FIELDS = 4
STRIPS = 8
F32 = jnp.float32
BF16 = jnp.bfloat16


def lanes(shape=(8, 128)):
    return lax.broadcasted_iota(jnp.int32, shape, len(shape) - 1)


def fetch(sources, targets, sems):
    copies = [pltpu.make_async_copy(s, d, sems.at[i]) for i, (s, d) in enumerate(zip(sources, targets))]
    for copy in copies:
        copy.start()
    return copies


def pack_tiles_kernel(n_tile, *refs):
    sources, (out_ref, fields_ref), targets, sems = refs[:8], refs[8:10], refs[10:18], refs[18]
    copies = fetch(sources, targets, sems)
    bv_ref, visc_ref, fric_ref, fp_ref, los_ref, weight_ref, cell_ref, count_ref = targets
    t = lax.axis_index("tile")
    parity = lax.rem(t, 2)
    rows = visc_ref.shape[0]
    half = rows // 2
    for copy in copies[4:]:
        copy.wait()
    row_lane = lanes((1, 128))
    low = lanes() < CAP
    straight, turned = [], []
    for j in range(n_tile // 2):
        at = pl.ds(j * 128, 128)
        count = jnp.where(
            row_lane < CAP, count_ref[0, 0, :, 2 * j : 2 * j + 1], count_ref[0, 0, :, 2 * j + 1 : 2 * j + 2]
        )
        live = (row_lane & (CAP - 1)) < count
        weight = jnp.where(live, weight_ref[0, 0, :, at], 0.0)
        scaled = jnp.sqrt(weight) * los_ref[0, 0, :, at]
        high = scaled.astype(BF16).astype(F32)
        cell = cell_ref[0, 0, :, at]
        block = jnp.concatenate(
            [
                high, scaled - high,
                lax.shift_right_logical(cell, 7).astype(F32), (cell & 127).astype(F32), jnp.zeros((2, 128), F32),
            ],
            axis=0,
        )
        straight.append(block)
        turned.append(pltpu.roll(block, CAP, 1))
    nothing = jnp.zeros((8, 128), F32)
    in_half = (lanes() // CAP) == parity

    def placed(owner, side):
        if owner < 0 or owner >= n_tile:
            return nothing
        return (straight if owner % 2 == side else turned)[owner // 2]

    for d in range(n_tile):
        solo = jnp.where(parity == d % 2, straight[d // 2], turned[d // 2])
        solo = jnp.where(in_half, solo, 0.0)
        pair = jnp.where(low, placed(d - 1, 0), placed(d + 1, 1))
        out_ref[d, half : half + 16, :] = jnp.concatenate([solo, pair], axis=0).astype(BF16)

    for copy in copies[:4]:
        copy.wait()
    probe = fp_ref[...]
    fields = [-(probe * bv_ref[0]), -(probe * bv_ref[1]), visc_ref[...], fric_ref[...]]
    for f, field in enumerate(fields):
        fields_ref[f] = field
    lane = lanes((half, 128))

    def fold(first_lane):
        packed = jnp.zeros((half, 128), F32)
        for part in range(2):
            for f, field in enumerate(fields):
                start = part * 64 + f * HALO
                piece = field[part * half : (part + 1) * half]
                piece = pltpu.roll(piece, (start - first_lane) % 128, 1)
                packed = jnp.where((lane >= start) & (lane < start + HALO), piece, packed)
        return packed

    @pl.when(t < n_tile - 1)
    def _():
        out_ref[t + 1, 0:half, :] = fold(128 - HALO).astype(BF16)

    @pl.when(t > 0)
    def _():
        out_ref[t - 1, 0:half, :] = fold(0).astype(BF16)


def pack_rows_kernel(n_tile, fields_ref, got_ref, ext_ref, pix_ref, even_ref, odd_ref):
    g = lax.axis_index("grp")
    t = lax.axis_index("tile")
    rows = fields_ref.shape[1]
    half = rows // 2
    fields = [fields_ref[f] for f in range(FIELDS)]
    lane = lanes((half, 128))
    right = jnp.where(t < n_tile - 1, got_ref[jnp.minimum(t + 1, n_tile - 1), 0:half, :].astype(F32), 0.0)
    left = jnp.where(t > 0, got_ref[jnp.maximum(t - 1, 0), 0:half, :].astype(F32), 0.0)
    band = lanes((HALO, 128))
    edge_up = jnp.zeros((HALO, 128), F32)
    edge_down = jnp.zeros((HALO, 128), F32)
    for f, field in enumerate(fields):
        ext_ref[f, :, 0:128] = field
        edges = []
        for part in range(2):
            start = part * 64 + f * HALO
            edge = jnp.where(
                lane < HALO,
                pltpu.roll(right, (0 - start) % 128, 1),
                jnp.where(lane >= 128 - HALO, pltpu.roll(left, (128 - HALO - start) % 128, 1), 0.0),
            )
            ext_ref[f, part * half : (part + 1) * half, 128:256] = edge
            edges.append(edge)
        here = (band >= 2 * f * HALO) & (band < 2 * (f + 1) * HALO)
        turn = (2 * f + 1) * HALO % 128
        edge_up = jnp.where(here, pltpu.roll(edges[0][0:HALO], turn, 1), edge_up)
        edge_down = jnp.where(here, pltpu.roll(edges[1][half - HALO :], turn, 1), edge_down)
    low = lanes() < CAP
    near, far = [], []
    for s in range(0, n_tile, 2):
        one = got_ref[s, half : half + 16, :].astype(F32)
        two = got_ref[s + 1, half : half + 16, :].astype(F32)
        near.append(jnp.where(low, one[0:8], two[0:8]))
        far += [one[8:16], two[8:16]]
    blocks = near + far
    pixels = jnp.concatenate(
        [b[0:1] + b[2:3] for b in blocks]
        + [b[1:2] + b[3:4] for b in blocks]
        + [b[4:5] for b in blocks]
        + [b[5:6] for b in blocks],
        axis=0,
    )
    pix_ref[...] = pixels
    pixels = pixels.astype(BF16)

    even = lax.rem(g, 2) == 0

    def choose(one, two):
        even_ref_value, odd_ref_value = jnp.where(even, one, two), jnp.where(even, two, one)
        return even_ref_value.astype(BF16), odd_ref_value.astype(BF16)

    for f, field in enumerate(fields):
        at = pl.ds(f * HALO, HALO)
        even_ref[at, :], odd_ref[at, :] = choose(field[rows - HALO :], field[0:HALO])
    at = pl.ds(FIELDS * HALO, HALO)
    even_ref[at, :], odd_ref[at, :] = choose(edge_down, edge_up)
    for ref in (even_ref, odd_ref):
        ref[(FIELDS + 1) * HALO :, :] = pixels


def solve_kernel(
    n_grp, n_tile, ext_ref, pix_ref, even_ref, odd_ref, bv_hbm, panels_hbm,
    inc_ref, hess_ref, low_ref, panels_ref,
    plane_ref, coef_ref, src_ref, w_ref, nat_ref, bv_ref, sems,
):
    copies = fetch((bv_hbm, panels_hbm), (bv_ref, panels_ref), sems)
    g = lax.axis_index("grp")
    t = lax.axis_index("tile")
    rows = ext_ref.shape[1]
    span = rows + 2 * HALO
    groups = span // STRIPS
    lane = lanes()

    even = lax.rem(g, 2) == 0

    def above(first, size):
        at = pl.ds(first, size)
        got = jnp.where(even, odd_ref[at, :].astype(F32), even_ref[at, :].astype(F32))
        return jnp.where(g > 0, got, 0.0)

    def below(first, size):
        at = pl.ds(first, size)
        got = jnp.where(even, even_ref[at, :].astype(F32), odd_ref[at, :].astype(F32))
        return jnp.where(g < n_grp - 1, got, 0.0)

    first_lane = lane == 0
    last_lane = lane == 127

    band = lanes((HALO, 128))
    for f in range(FIELDS):
        for h in range(2):
            plane_ref[f, h, HALO : HALO + rows, :] = ext_ref[f, :, h * 128 : (h + 1) * 128]
        for load, at in ((above, 0), (below, HALO + rows)):
            plane_ref[f, 0, at : at + HALO, :] = load(f * HALO, HALO)
            edge = pltpu.roll(load(FIELDS * HALO, HALO), (0 - (2 * f + 1) * HALO) % 128, 1)
            plane_ref[f, 1, at : at + HALO, :] = jnp.where((band < HALO) | (band >= 128 - HALO), edge, 0.0)

    def strided(f, h, v):
        return plane_ref[f, h, pl.ds(v, STRIPS, stride=groups), :]

    def beside(pair):
        a, b = pair
        ra, rb = pltpu.roll(a, 1, 1), pltpu.roll(b, 1, 1)
        before = (jnp.where(first_lane, rb, ra), jnp.where(first_lane, ra, rb))
        ra, rb = pltpu.roll(a, 127, 1), pltpu.roll(b, 127, 1)
        after = (jnp.where(last_lane, rb, ra), jnp.where(last_lane, ra, rb))
        return before, pair, after

    def row(load, v):
        if v < 0:
            return beside(tuple(pltpu.roll(load(h, groups - 1), 1, 0) for h in range(2)))
        if v == groups:
            return beside(tuple(pltpu.roll(load(h, 0), STRIPS - 1, 0) for h in range(2)))
        return beside(tuple(load(h, v) for h in range(2)))

    strip = lax.broadcasted_iota(jnp.int32, (8, 128), 0)
    col_in = [
        None,
        ((lane < HALO) & (t < n_tile - 1)) | ((lane >= 128 - HALO) & (t > 0)),
    ]
    load_visc = functools.partial(strided, 2)
    prev, cur = row(load_visc, -1), row(load_visc, 0)
    for v in range(groups):
        nxt = row(load_visc, v + 1)
        place = g * rows - HALO + strip * groups + v
        row_in = (place >= 0) & (place < n_grp * rows)
        at = pl.ds(v * 8, 8)
        for h in range(2):
            centre = cur[1][h]
            east = 0.5 * (centre + nxt[1][h])
            west = 0.5 * (centre + prev[1][h])
            north = 0.5 * (centre + cur[2][h])
            south = 0.5 * (centre + cur[0][h])
            node_pp = 0.25 * (centre + nxt[1][h] + cur[2][h] + nxt[2][h])
            node_mm = 0.25 * (centre + prev[1][h] + cur[0][h] + prev[0][h])
            node_pm = 0.25 * (centre + nxt[1][h] + cur[0][h] + nxt[0][h])
            node_mp = 0.25 * (centre + prev[1][h] + cur[2][h] + prev[2][h])
            fric = strided(3, h, v)
            diag_x = fric + 2.0 * (east + west) + (north + south)
            diag_y = fric + (east + west) + 2.0 * (north + south)
            inside = row_in if col_in[h] is None else row_in & col_in[h]
            inv_x = jnp.where(inside, RELAX / jnp.where(inside, diag_x, 1.0), 0.0)
            inv_y = jnp.where(inside, RELAX / jnp.where(inside, diag_y, 1.0), 0.0)
            cols = pl.ds(h * 128, 128)
            for i, plane in enumerate(
                (east, west, north, south, 0.25 * node_pp, 0.25 * node_mm, 0.25 * node_pm, 0.25 * node_mp, inv_x, inv_y)
            ):
                coef_ref[i, at, cols] = plane
            src_ref[0, at, cols] = inv_x * strided(0, h, v)
            src_ref[1, at, cols] = inv_y * strided(1, h, v)
        prev, cur = cur, nxt

    def natural(h, v):
        return (h, pl.ds(v, STRIPS, stride=groups), slice(None))

    def relax():
        w_ref[0] = src_ref[...]

        def sweep(now, later, start):
            rows_seen = {}

            def both(v):
                if v not in rows_seen:
                    rows_seen[v] = tuple(
                        row(lambda h, u, c=c: now[c, pl.ds(u * 8, 8), pl.ds(h * 128, 128)], v) for c in range(2)
                    )
                return rows_seen[v]

            for p in range(groups):
                v = (p + start) % groups
                prev, cur, nxt = both(v - 1), both(v), both(v + 1)
                at = pl.ds(v * 8, 8)
                for h in range(2):
                    cols = pl.ds(h * 128, 128)
                    east, west, north, south, pp, mm, pm, mp, inv_x, inv_y = (
                        coef_ref[i, at, cols] for i in range(10)
                    )

                    def along(c):
                        return (
                            east * nxt[c][1][h] + west * prev[c][1][h],
                            north * cur[c][2][h] + south * cur[c][0][h],
                        )

                    def cross(c):
                        return (
                            pp * nxt[c][2][h] + mm * prev[c][0][h] - pm * nxt[c][0][h] - mp * prev[c][2][h]
                        )

                    one, two = along(0)
                    sum_x = 2.0 * one + two + cross(1)
                    one, two = along(1)
                    sum_y = one + 2.0 * two + cross(0)
                    for c, new in ((0, inv_x * sum_x), (1, inv_y * sum_y)):
                        new = (1.0 - RELAX) * cur[c][1][h] + src_ref[c, at, cols] + new
                        if later is None:
                            nat_ref[(c,) + natural(h, v)] = new
                        else:
                            later[c, at, cols] = new

        def three_sweeps(_, carry):
            for k in range(3):
                sweep(w_ref.at[k], w_ref.at[(k + 1) % 3], k)
            return carry

        lax.fori_loop(0, (SWEEPS - 2) // 3, three_sweeps, 0)
        sweep(w_ref.at[0], None, 0)

    def solve(phase, carry):
        relax()

        @pl.when(phase == 0)
        def _():
            for c in range(2):
                inc_ref[c] = nat_ref[c, 0, HALO : HALO + rows, :]
            misfit()

        return carry

    def misfit():
        n_near, n_all = n_tile // 2, 3 * n_tile // 2
        low = lanes((n_tile, 128)) < CAP
        spans = ((0, HALO, rows), (-1, HALO - EDGE, EDGE), (1, HALO + rows, EDGE))
        rim_lane = lanes((2 * rows, 128))
        jobs = []
        for delta, first, size in spans:
            if delta == 0:
                values = pix_ref[...]
            else:
                base = (FIELDS + 1) * HALO
                values = (above if delta < 0 else below)(base, 4 * n_all)
            los_x, los_y, r, c = (values[q * n_all : (q + 1) * n_all] for q in range(4))
            if delta < 0:
                r = r - (rows - EDGE)
            in_rim = c[n_near:] + jnp.where(low, float(EDGE) - 128.0, float(EDGE))
            for h, begin, count, lane_of in ((0, 0, n_near, c[0:n_near]), (1, n_near, n_tile, in_rim)):
                parts = []
                for comp in range(2):
                    part = nat_ref[comp, h, first : first + size, :]
                    parts.append(part if h == 0 else pltpu.roll(part, EDGE, 1))
                field = jnp.concatenate(parts, axis=0)
                high = field.astype(BF16).astype(F32)
                rest = field - high
                if h == 0:
                    stacked = jnp.concatenate([high.astype(BF16), rest.astype(BF16)], axis=1)
                else:
                    lane_here = rim_lane[0 : 2 * size]
                    stacked = jnp.where(lane_here < 2 * EDGE, high, pltpu.roll(rest, 2 * EDGE, 1))
                    stacked = jnp.where(lane_here < 4 * EDGE, stacked, 0.0).astype(BF16)
                jobs.append((h, first, size, begin, count, lane_of, los_x, los_y, r, stacked))

        nat_ref[...] = jnp.zeros_like(nat_ref)
        for h, first, size, begin, count, lane_of, los_x, los_y, r, stacked in jobs:
            chunk = 4 if h == 0 else 8
            depth = 128 if h == 0 else 2 * EDGE
            wide = chunk * 128
            row_id = lax.broadcasted_iota(jnp.int32, (size, wide), 0).astype(F32)
            lane_id = lax.broadcasted_iota(jnp.int32, (depth, wide), 0).astype(F32)
            total = jnp.zeros((4 * size, 128), F32)
            for j in range(0, count, chunk):

                def line(table, offset):
                    return jnp.concatenate([table[offset + i : offset + i + 1] for i in range(j, j + chunk)], axis=1)

                line_x, line_y = line(los_x, begin), line(los_y, begin)
                hot = jnp.where(lane_id == line(lane_of, 0), 1.0, 0.0).astype(BF16)
                here = row_id == line(r, begin)
                twice = [hot, hot]
                if h == 1:
                    twice.append(jnp.zeros((128 - 2 * depth, wide), BF16))
                    hot = jnp.concatenate([hot, jnp.zeros((128 - depth, wide), BF16)], axis=0)
                got = jnp.dot(stacked, jnp.concatenate(twice, axis=0), preferred_element_type=F32)
                got_x = jnp.sum(jnp.where(here, got[0:size], 0.0), axis=0, keepdims=True)
                got_y = jnp.sum(jnp.where(here, got[size:], 0.0), axis=0, keepdims=True)
                amount = line_x * got_x + line_y * got_y
                terms = [amount * line_x, amount * line_y]
                highs = [p.astype(BF16).astype(F32) for p in terms]
                terms = highs + [p - q for p, q in zip(terms, highs)]
                spread = jnp.concatenate([jnp.where(here, p, 0.0) for p in terms], axis=0).astype(BF16)
                total = total + lax.dot_general(spread, hot, (((1,), (1,)), ((), ())), preferred_element_type=F32)
            total = total[0 : 2 * size] + total[2 * size :]
            if h == 1:
                total = pltpu.roll(total, 128 - EDGE, 1)
            for c in range(2):
                nat_ref[c, h, first : first + size, :] = total[c * size : (c + 1) * size]

        for v in range(groups):
            at = pl.ds(v * 8, 8)
            for h in range(2):
                cols = pl.ds(h * 128, 128)
                for c in range(2):
                    src_ref[c, at, cols] = coef_ref[8 + c, at, cols] * nat_ref[(c,) + natural(h, v)]

    lax.fori_loop(0, 2, solve, 0)
    for copy in copies:
        copy.wait()
    hess = -(bv_ref[0] * nat_ref[0, 0, HALO : HALO + rows, :] + bv_ref[1] * nat_ref[1, 0, HALO : HALO + rows, :])
    hess_ref[...] = hess
    low_ref[...] = hess.astype(BF16)


def project_kernel(panels_ref, *refs):
    blocks, out_ref, probe_ref = refs[:-2], refs[-2], refs[-1]
    count = panels_ref.shape[0]
    for k, block in enumerate(blocks):
        probe_ref[lax.axis_index("grp") ^ (len(blocks) - 1 - k)] = block[...]
    probe = probe_ref[...].astype(F32).reshape(panels_ref.shape[1:])
    sums = []
    for k in range(count):
        product = panels_ref[k].astype(F32) * probe
        sums.append(jnp.sum(product, axis=0, keepdims=True))
    sums.append(jnp.zeros((128 - count, 128), F32))
    table = jnp.concatenate(sums, axis=0)
    line = lax.dot_general(
        jnp.ones((8, 128), F32), table, (((1,), (1,)), ((), ())),
        precision=lax.Precision.HIGHEST, preferred_element_type=F32,
    )
    line = pltpu.roll(line, lax.axis_index("grp") * count, 1)[0:1]
    out_ref[...] = jnp.broadcast_to(line[None], out_ref.shape)


def add_lines_kernel(lines_ref, out_ref):
    out_ref[...] = jnp.sum(lines_ref[...], axis=0)


def vmem(n):
    return [pl.BlockSpec(memory_space=pltpu.VMEM)] * n


def on_device(
    base_velocity, viscosity, friction, friction_probe, pixel_los, pixel_weight, pixel_cell, pixel_count, panels
):
    n_grp, n_tile = lax.axis_size("grp"), lax.axis_size("tile")
    rows, columns = viscosity.shape
    half = rows // 2
    span = rows + 2 * HALO
    params = pltpu.CompilerParams(vmem_limit_bytes=32 * 2**20)

    inputs = [
        pltpu.with_memory_space_constraint(x, pltpu.HBM)
        for x in (
            base_velocity, viscosity, friction, friction_probe, pixel_los, pixel_weight, pixel_cell, pixel_count
        )
    ]
    slots, fields = pl.pallas_call(
        functools.partial(pack_tiles_kernel, n_tile),
        out_shape=(
            jax.ShapeDtypeStruct((n_tile, half + 16, 128), BF16),
            jax.ShapeDtypeStruct((FIELDS, rows, columns), F32),
        ),
        in_specs=[pl.BlockSpec(memory_space=pltpu.HBM)] * len(inputs),
        out_specs=tuple(vmem(2)),
        scratch_shapes=[pltpu.VMEM(x.shape, x.dtype) for x in inputs] + [pltpu.SemaphoreType.DMA((len(inputs),))],
        compiler_params=params,
        name="pack_tiles",
    )(*inputs)
    got = lax.all_to_all(slots, "tile", split_axis=0, concat_axis=0, tiled=True)

    packet = (FIELDS + 1) * HALO + 6 * n_tile
    ext, pix, even, odd = pl.pallas_call(
        functools.partial(pack_rows_kernel, n_tile),
        out_shape=(
            jax.ShapeDtypeStruct((FIELDS, rows, 256), F32),
            jax.ShapeDtypeStruct((6 * n_tile, 128), F32),
            jax.ShapeDtypeStruct((packet, 128), BF16),
            jax.ShapeDtypeStruct((packet, 128), BF16),
        ),
        in_specs=vmem(2),
        out_specs=tuple(vmem(4)),
        compiler_params=params,
        name="pack_rows",
    )(fields, got)
    odd = lax.ppermute(odd, "grp", [(i, (i - 1 + 2 * (i % 2)) % n_grp) for i in range(n_grp)])
    even = lax.ppermute(even, "grp", [(i, i ^ 1) for i in range(n_grp)])

    increment, hessian_probe, probe_low, panels_near = pl.pallas_call(
        functools.partial(solve_kernel, n_grp, n_tile),
        out_shape=(
            jax.ShapeDtypeStruct((2, rows, columns), F32),
            jax.ShapeDtypeStruct((rows, columns), F32),
            jax.ShapeDtypeStruct((rows, columns), BF16),
            jax.ShapeDtypeStruct(panels.shape, BF16),
        ),
        in_specs=vmem(4) + [pl.BlockSpec(memory_space=pltpu.HBM)] * 2,
        out_specs=tuple(vmem(4)),
        scratch_shapes=[
            pltpu.VMEM((FIELDS, 2, span, 128), F32),
            pltpu.VMEM((10, span, 256), F32),
            pltpu.VMEM((2, span, 256), F32),
            pltpu.VMEM((3, 2, span, 256), F32),
            pltpu.VMEM((2, 2, span, 128), F32),
            pltpu.VMEM(base_velocity.shape, F32),
            pltpu.SemaphoreType.DMA((2,)),
        ],
        compiler_params=params,
        name="solve",
    )(ext, pix, even, odd, inputs[0], pltpu.with_memory_space_constraint(panels, pltpu.HBM))

    column = [
        lax.ppermute(probe_low, "grp", [(i, i ^ k) for i in range(n_grp)]) for k in range(n_grp - 1, 0, -1)
    ] + [probe_low]
    partial = pl.pallas_call(
        project_kernel,
        out_shape=jax.ShapeDtypeStruct((n_grp * n_tile, 1, 128), F32),
        in_specs=vmem(1 + n_grp),
        out_specs=pl.BlockSpec(memory_space=pltpu.VMEM),
        scratch_shapes=[pltpu.VMEM((n_grp, rows, columns), BF16)],
        compiler_params=params,
        name="project",
    )(panels_near, *column)
    everyone = lax.all_to_all(partial, ("grp", "tile"), split_axis=0, concat_axis=0, tiled=True)
    coefficients = pl.pallas_call(
        add_lines_kernel,
        out_shape=jax.ShapeDtypeStruct((1, 128), F32),
        in_specs=vmem(1),
        out_specs=pl.BlockSpec(memory_space=pltpu.VMEM),
        compiler_params=params,
        name="add_lines",
    )(everyone)
    return increment, hessian_probe, coefficients.reshape(128)


def solution(mesh):
    in_specs = (
        P(None, "grp", "tile"),
        P("grp", "tile"),
        P("grp", "tile"),
        P("grp", "tile"),
        P("grp", "tile", None, None),
        P("grp", "tile", None, None),
        P("grp", "tile", None, None),
        P("grp", "tile", None, None),
        P("grp", None, "tile"),
    )
    out_specs = (P(None, "grp", "tile"), P("grp", "tile"), P())
    return jax.shard_map(
        on_device, mesh=mesh, in_specs=in_specs, out_specs=out_specs, check_vma=False
    )
```

```python
import functools

import jax
import jax.numpy as jnp
from jax import lax
from jax.experimental import pallas as pl
from jax.experimental.pallas import tpu as pltpu
from jax.sharding import PartitionSpec as P

SWEEPS = 8
RELAX = 0.8
CAP = 64
HALO = 16
EDGE = 8
FIELDS = 4
STRIPS = 8
F32 = jnp.float32
BF16 = jnp.bfloat16


def lanes(shape=(8, 128)):
    return lax.broadcasted_iota(jnp.int32, shape, len(shape) - 1)


def fetch(sources, targets, sems):
    copies = [pltpu.make_async_copy(s, d, sems.at[i]) for i, (s, d) in enumerate(zip(sources, targets))]
    for copy in copies:
        copy.start()
    return copies


def pack_tiles_kernel(n_tile, *refs):
    sources, (out_ref, fields_ref), targets, sems = refs[:8], refs[8:10], refs[10:18], refs[18]
    copies = fetch(sources, targets, sems)
    bv_ref, visc_ref, fric_ref, fp_ref, los_ref, weight_ref, cell_ref, count_ref = targets
    t = lax.axis_index("tile")
    parity = lax.rem(t, 2)
    rows = visc_ref.shape[0]
    half = rows // 2
    for copy in copies[4:]:
        copy.wait()
    row_lane = lanes((1, 128))
    low = lanes() < CAP
    straight, turned = [], []
    for j in range(n_tile // 2):
        at = pl.ds(j * 128, 128)
        count = jnp.where(
            row_lane < CAP, count_ref[0, 0, :, 2 * j : 2 * j + 1], count_ref[0, 0, :, 2 * j + 1 : 2 * j + 2]
        )
        live = (row_lane & (CAP - 1)) < count
        weight = jnp.where(live, weight_ref[0, 0, :, at], 0.0)
        scaled = jnp.sqrt(weight) * los_ref[0, 0, :, at]
        high = scaled.astype(BF16).astype(F32)
        cell = cell_ref[0, 0, :, at]
        block = jnp.concatenate(
            [
                high, scaled - high,
                lax.shift_right_logical(cell, 7).astype(F32), (cell & 127).astype(F32), jnp.zeros((2, 128), F32),
            ],
            axis=0,
        )
        straight.append(block)
        turned.append(pltpu.roll(block, CAP, 1))
    nothing = jnp.zeros((8, 128), F32)
    in_half = (lanes() // CAP) == parity

    def placed(owner, side):
        if owner < 0 or owner >= n_tile:
            return nothing
        return (straight if owner % 2 == side else turned)[owner // 2]

    for d in range(n_tile):
        solo = jnp.where(parity == d % 2, straight[d // 2], turned[d // 2])
        solo = jnp.where(in_half, solo, 0.0)
        pair = jnp.where(low, placed(d - 1, 0), placed(d + 1, 1))
        out_ref[d, half : half + 16, :] = jnp.concatenate([solo, pair], axis=0).astype(BF16)

    for copy in copies[:4]:
        copy.wait()
    probe = fp_ref[...]
    fields = [-(probe * bv_ref[0]), -(probe * bv_ref[1]), visc_ref[...], fric_ref[...]]
    for f, field in enumerate(fields):
        fields_ref[f] = field
    lane = lanes((half, 128))

    def fold(first_lane):
        packed = jnp.zeros((half, 128), F32)
        for part in range(2):
            for f, field in enumerate(fields):
                start = part * 64 + f * HALO
                piece = field[part * half : (part + 1) * half]
                piece = pltpu.roll(piece, (start - first_lane) % 128, 1)
                packed = jnp.where((lane >= start) & (lane < start + HALO), piece, packed)
        return packed

    @pl.when(t < n_tile - 1)
    def _():
        out_ref[t + 1, 0:half, :] = fold(128 - HALO).astype(BF16)

    @pl.when(t > 0)
    def _():
        out_ref[t - 1, 0:half, :] = fold(0).astype(BF16)


def pack_rows_kernel(n_tile, fields_ref, got_ref, ext_ref, pix_ref, even_ref, odd_ref):
    g = lax.axis_index("grp")
    t = lax.axis_index("tile")
    rows = fields_ref.shape[1]
    half = rows // 2
    fields = [fields_ref[f] for f in range(FIELDS)]
    lane = lanes((half, 128))
    right = jnp.where(t < n_tile - 1, got_ref[jnp.minimum(t + 1, n_tile - 1), 0:half, :].astype(F32), 0.0)
    left = jnp.where(t > 0, got_ref[jnp.maximum(t - 1, 0), 0:half, :].astype(F32), 0.0)
    band = lanes((HALO, 128))
    edge_up = jnp.zeros((HALO, 128), F32)
    edge_down = jnp.zeros((HALO, 128), F32)
    for f, field in enumerate(fields):
        ext_ref[f, :, 0:128] = field
        edges = []
        for part in range(2):
            start = part * 64 + f * HALO
            edge = jnp.where(
                lane < HALO,
                pltpu.roll(right, (0 - start) % 128, 1),
                jnp.where(lane >= 128 - HALO, pltpu.roll(left, (128 - HALO - start) % 128, 1), 0.0),
            )
            ext_ref[f, part * half : (part + 1) * half, 128:256] = edge
            edges.append(edge)
        here = (band >= 2 * f * HALO) & (band < 2 * (f + 1) * HALO)
        turn = (2 * f + 1) * HALO % 128
        edge_up = jnp.where(here, pltpu.roll(edges[0][0:HALO], turn, 1), edge_up)
        edge_down = jnp.where(here, pltpu.roll(edges[1][half - HALO :], turn, 1), edge_down)
    low = lanes() < CAP
    near, far = [], []
    for s in range(0, n_tile, 2):
        one = got_ref[s, half : half + 16, :].astype(F32)
        two = got_ref[s + 1, half : half + 16, :].astype(F32)
        near.append(jnp.where(low, one[0:8], two[0:8]))
        far += [one[8:16], two[8:16]]
    blocks = near + far
    pixels = jnp.concatenate(
        [b[0:1] + b[2:3] for b in blocks]
        + [b[1:2] + b[3:4] for b in blocks]
        + [b[4:5] for b in blocks]
        + [b[5:6] for b in blocks],
        axis=0,
    )
    pix_ref[...] = pixels
    pixels = pixels.astype(BF16)

    even = lax.rem(g, 2) == 0

    def choose(one, two):
        even_ref_value, odd_ref_value = jnp.where(even, one, two), jnp.where(even, two, one)
        return even_ref_value.astype(BF16), odd_ref_value.astype(BF16)

    for f, field in enumerate(fields):
        at = pl.ds(f * HALO, HALO)
        even_ref[at, :], odd_ref[at, :] = choose(field[rows - HALO :], field[0:HALO])
    at = pl.ds(FIELDS * HALO, HALO)
    even_ref[at, :], odd_ref[at, :] = choose(edge_down, edge_up)
    for ref in (even_ref, odd_ref):
        ref[(FIELDS + 1) * HALO :, :] = pixels


def solve_kernel(
    n_grp, n_tile, ext_ref, pix_ref, odd_ref, even_ref, bv_hbm, panels_hbm,
    inc_ref, hess_ref, low_ref, panels_ref,
    plane_ref, coef_ref, src_ref, w_ref, nat_ref, bv_ref, sems,
):
    size = panels_ref.shape[2]
    copies = fetch(
        [bv_hbm] + [panels_hbm.at[:, pl.ds(i * size, size), :] for i in range(n_grp)],
        [bv_ref] + [panels_ref.at[:, i] for i in range(n_grp)],
        sems,
    )
    g = lax.axis_index("grp")
    t = lax.axis_index("tile")
    rows = ext_ref.shape[1]
    span = rows + 2 * HALO
    groups = span // STRIPS
    lane = lanes()

    even = lax.rem(g, 2) == 0

    def above(first, size):
        at = pl.ds(first, size)
        got = jnp.where(even, odd_ref[at, :].astype(F32), even_ref[at, :].astype(F32))
        return jnp.where(g > 0, got, 0.0)

    def below(first, size):
        at = pl.ds(first, size)
        got = jnp.where(even, even_ref[at, :].astype(F32), odd_ref[at, :].astype(F32))
        return jnp.where(g < n_grp - 1, got, 0.0)

    first_lane = lane == 0
    last_lane = lane == 127

    band = lanes((HALO, 128))
    for f in range(FIELDS):
        for h in range(2):
            plane_ref[f, h, HALO : HALO + rows, :] = ext_ref[f, :, h * 128 : (h + 1) * 128]
        for load, at in ((above, 0), (below, HALO + rows)):
            plane_ref[f, 0, at : at + HALO, :] = load(f * HALO, HALO)
            edge = pltpu.roll(load(FIELDS * HALO, HALO), (0 - (2 * f + 1) * HALO) % 128, 1)
            plane_ref[f, 1, at : at + HALO, :] = jnp.where((band < HALO) | (band >= 128 - HALO), edge, 0.0)

    def strided(f, h, v):
        return plane_ref[f, h, pl.ds(v, STRIPS, stride=groups), :]

    def beside(pair):
        a, b = pair
        ra, rb = pltpu.roll(a, 1, 1), pltpu.roll(b, 1, 1)
        before = (jnp.where(first_lane, rb, ra), jnp.where(first_lane, ra, rb))
        ra, rb = pltpu.roll(a, 127, 1), pltpu.roll(b, 127, 1)
        after = (jnp.where(last_lane, rb, ra), jnp.where(last_lane, ra, rb))
        return before, pair, after

    def row(load, v):
        if v < 0:
            return beside(tuple(pltpu.roll(load(h, groups - 1), 1, 0) for h in range(2)))
        if v == groups:
            return beside(tuple(pltpu.roll(load(h, 0), STRIPS - 1, 0) for h in range(2)))
        return beside(tuple(load(h, v) for h in range(2)))

    strip = lax.broadcasted_iota(jnp.int32, (8, 128), 0)
    col_in = [
        None,
        ((lane < HALO) & (t < n_tile - 1)) | ((lane >= 128 - HALO) & (t > 0)),
    ]
    load_visc = functools.partial(strided, 2)
    prev, cur = row(load_visc, -1), row(load_visc, 0)
    for v in range(groups):
        nxt = row(load_visc, v + 1)
        place = g * rows - HALO + strip * groups + v
        row_in = (place >= 0) & (place < n_grp * rows)
        at = pl.ds(v * 8, 8)
        for h in range(2):
            centre = cur[1][h]
            east = 0.5 * (centre + nxt[1][h])
            west = 0.5 * (centre + prev[1][h])
            north = 0.5 * (centre + cur[2][h])
            south = 0.5 * (centre + cur[0][h])
            node_pp = 0.25 * (centre + nxt[1][h] + cur[2][h] + nxt[2][h])
            node_mm = 0.25 * (centre + prev[1][h] + cur[0][h] + prev[0][h])
            node_pm = 0.25 * (centre + nxt[1][h] + cur[0][h] + nxt[0][h])
            node_mp = 0.25 * (centre + prev[1][h] + cur[2][h] + prev[2][h])
            fric = strided(3, h, v)
            diag_x = fric + 2.0 * (east + west) + (north + south)
            diag_y = fric + (east + west) + 2.0 * (north + south)
            inside = row_in if col_in[h] is None else row_in & col_in[h]
            inv_x = jnp.where(inside, RELAX / jnp.where(inside, diag_x, 1.0), 0.0)
            inv_y = jnp.where(inside, RELAX / jnp.where(inside, diag_y, 1.0), 0.0)
            cols = pl.ds(h * 128, 128)
            for i, plane in enumerate(
                (east, west, north, south, 0.25 * node_pp, 0.25 * node_mm, 0.25 * node_pm, 0.25 * node_mp, inv_x, inv_y)
            ):
                coef_ref[i, at, cols] = plane
            src_ref[0, at, cols] = inv_x * strided(0, h, v)
            src_ref[1, at, cols] = inv_y * strided(1, h, v)
        prev, cur = cur, nxt

    def natural(h, v):
        return (h, pl.ds(v, STRIPS, stride=groups), slice(None))

    def relax():
        w_ref[0] = src_ref[...]

        def sweep(now, later, start):
            rows_seen = {}

            def both(v):
                if v not in rows_seen:
                    rows_seen[v] = tuple(
                        row(lambda h, u, c=c: now[c, pl.ds(u * 8, 8), pl.ds(h * 128, 128)], v) for c in range(2)
                    )
                return rows_seen[v]

            for p in range(groups):
                v = (p + start) % groups
                prev, cur, nxt = both(v - 1), both(v), both(v + 1)
                at = pl.ds(v * 8, 8)
                for h in range(2):
                    cols = pl.ds(h * 128, 128)
                    east, west, north, south, pp, mm, pm, mp, inv_x, inv_y = (
                        coef_ref[i, at, cols] for i in range(10)
                    )

                    def along(c):
                        return (
                            east * nxt[c][1][h] + west * prev[c][1][h],
                            north * cur[c][2][h] + south * cur[c][0][h],
                        )

                    def cross(c):
                        return (
                            pp * nxt[c][2][h] + mm * prev[c][0][h] - pm * nxt[c][0][h] - mp * prev[c][2][h]
                        )

                    one, two = along(0)
                    sum_x = 2.0 * one + two + cross(1)
                    one, two = along(1)
                    sum_y = one + 2.0 * two + cross(0)
                    for c, new in ((0, inv_x * sum_x), (1, inv_y * sum_y)):
                        new = (1.0 - RELAX) * cur[c][1][h] + src_ref[c, at, cols] + new
                        if later is None:
                            nat_ref[(c,) + natural(h, v)] = new
                        else:
                            later[c, at, cols] = new

        def three_sweeps(_, carry):
            for k in range(3):
                sweep(w_ref.at[k], w_ref.at[(k + 1) % 3], k)
            return carry

        lax.fori_loop(0, (SWEEPS - 2) // 3, three_sweeps, 0)
        sweep(w_ref.at[0], None, 0)

    def solve(phase, carry):
        relax()

        @pl.when(phase == 0)
        def _():
            for c in range(2):
                inc_ref[c] = nat_ref[c, 0, HALO : HALO + rows, :]
            misfit()

        return carry

    def misfit():
        n_near, n_all = n_tile // 2, 3 * n_tile // 2
        low = lanes((n_tile, 128)) < CAP
        spans = ((0, HALO, rows), (-1, HALO - EDGE, EDGE), (1, HALO + rows, EDGE))
        rim_lane = lanes((2 * rows, 128))
        jobs = []
        for delta, first, size in spans:
            if delta == 0:
                values = pix_ref[...]
            else:
                base = (FIELDS + 1) * HALO
                values = (above if delta < 0 else below)(base, 4 * n_all)
            los_x, los_y, r, c = (values[q * n_all : (q + 1) * n_all] for q in range(4))
            if delta < 0:
                r = r - (rows - EDGE)
            in_rim = c[n_near:] + jnp.where(low, float(EDGE) - 128.0, float(EDGE))
            for h, begin, count, lane_of in ((0, 0, n_near, c[0:n_near]), (1, n_near, n_tile, in_rim)):
                parts = []
                for comp in range(2):
                    part = nat_ref[comp, h, first : first + size, :]
                    parts.append(part if h == 0 else pltpu.roll(part, EDGE, 1))
                field = jnp.concatenate(parts, axis=0)
                high = field.astype(BF16).astype(F32)
                rest = field - high
                if h == 0:
                    stacked = jnp.concatenate([high.astype(BF16), rest.astype(BF16)], axis=1)
                else:
                    lane_here = rim_lane[0 : 2 * size]
                    stacked = jnp.where(lane_here < 2 * EDGE, high, pltpu.roll(rest, 2 * EDGE, 1))
                    stacked = jnp.where(lane_here < 4 * EDGE, stacked, 0.0).astype(BF16)
                jobs.append((h, first, size, begin, count, lane_of, los_x, los_y, r, stacked))

        nat_ref[...] = jnp.zeros_like(nat_ref)
        for h, first, size, begin, count, lane_of, los_x, los_y, r, stacked in jobs:
            chunk = 4 if h == 0 else 8
            depth = 128 if h == 0 else 2 * EDGE
            wide = chunk * 128
            row_id = lax.broadcasted_iota(jnp.int32, (size, wide), 0).astype(F32)
            lane_id = lax.broadcasted_iota(jnp.int32, (depth, wide), 0).astype(F32)
            total = jnp.zeros((4 * size, 128), F32)
            for j in range(0, count, chunk):

                def line(table, offset):
                    return jnp.concatenate([table[offset + i : offset + i + 1] for i in range(j, j + chunk)], axis=1)

                line_x, line_y = line(los_x, begin), line(los_y, begin)
                hot = jnp.where(lane_id == line(lane_of, 0), 1.0, 0.0).astype(BF16)
                here = row_id == line(r, begin)
                twice = [hot, hot]
                if h == 1:
                    twice.append(jnp.zeros((128 - 2 * depth, wide), BF16))
                    hot = jnp.concatenate([hot, jnp.zeros((128 - depth, wide), BF16)], axis=0)
                got = jnp.dot(stacked, jnp.concatenate(twice, axis=0), preferred_element_type=F32)
                got_x = jnp.sum(jnp.where(here, got[0:size], 0.0), axis=0, keepdims=True)
                got_y = jnp.sum(jnp.where(here, got[size:], 0.0), axis=0, keepdims=True)
                amount = line_x * got_x + line_y * got_y
                terms = [amount * line_x, amount * line_y]
                highs = [p.astype(BF16).astype(F32) for p in terms]
                terms = highs + [p - q for p, q in zip(terms, highs)]
                spread = jnp.concatenate([jnp.where(here, p, 0.0) for p in terms], axis=0).astype(BF16)
                total = total + lax.dot_general(spread, hot, (((1,), (1,)), ((), ())), preferred_element_type=F32)
            total = total[0 : 2 * size] + total[2 * size :]
            if h == 1:
                total = pltpu.roll(total, 128 - EDGE, 1)
            for c in range(2):
                nat_ref[c, h, first : first + size, :] = total[c * size : (c + 1) * size]

        for v in range(groups):
            at = pl.ds(v * 8, 8)
            for h in range(2):
                cols = pl.ds(h * 128, 128)
                for c in range(2):
                    src_ref[c, at, cols] = coef_ref[8 + c, at, cols] * nat_ref[(c,) + natural(h, v)]

    lax.fori_loop(0, 2, solve, 0)
    for copy in copies:
        copy.wait()
    hess = -(bv_ref[0] * nat_ref[0, 0, HALO : HALO + rows, :] + bv_ref[1] * nat_ref[1, 0, HALO : HALO + rows, :])
    hess_ref[...] = hess
    low_ref[...] = hess.astype(BF16)


def distances(n_grp):
    return [0] + list(range(2, n_grp)) + [1]


def project_block(panels_ref, probe_ref, k, distance):
    count, n_grp, rows, columns = panels_ref.shape
    product = panels_ref[k, lax.axis_index("grp") ^ distance].astype(F32) * probe_ref[...].astype(F32)
    return jnp.sum(product.reshape(-1, 8, columns), axis=0)


def project_kernel(panels_ref, *refs):
    blocks, sums_ref = refs[:-1], refs[-1]
    order = distances(panels_ref.shape[1])
    for k in range(panels_ref.shape[0]):
        sums_ref[k] = sum(project_block(panels_ref, block, k, i) for i, block in zip(order, blocks))


def project_last_kernel(panels_ref, block_ref, sums_ref, out_ref):
    count, n_grp = panels_ref.shape[:2]
    sums = []
    for k in range(count):
        total = sums_ref[k] + project_block(panels_ref, block_ref, k, distances(n_grp)[-1])
        sums.append(jnp.sum(total, axis=0, keepdims=True))
    sums.append(jnp.zeros((128 - count, 128), F32))
    table = jnp.concatenate(sums, axis=0)
    line = lax.dot_general(
        jnp.ones((8, 128), F32), table, (((1,), (1,)), ((), ())),
        precision=lax.Precision.HIGHEST, preferred_element_type=F32,
    )
    line = pltpu.roll(line, lax.axis_index("grp") * count, 1)[0:1]
    out_ref[...] = jnp.broadcast_to(line[None], out_ref.shape)


def add_lines_kernel(lines_ref, out_ref):
    out_ref[...] = jnp.sum(lines_ref[...], axis=0)


def vmem(n):
    return [pl.BlockSpec(memory_space=pltpu.VMEM)] * n


def on_device(
    base_velocity, viscosity, friction, friction_probe, pixel_los, pixel_weight, pixel_cell, pixel_count, panels
):
    n_grp, n_tile = lax.axis_size("grp"), lax.axis_size("tile")
    rows, columns = viscosity.shape
    half = rows // 2
    span = rows + 2 * HALO
    params = pltpu.CompilerParams(vmem_limit_bytes=32 * 2**20)

    inputs = [
        pltpu.with_memory_space_constraint(x, pltpu.HBM)
        for x in (
            base_velocity, viscosity, friction, friction_probe, pixel_los, pixel_weight, pixel_cell, pixel_count
        )
    ]
    slots, fields = pl.pallas_call(
        functools.partial(pack_tiles_kernel, n_tile),
        out_shape=(
            jax.ShapeDtypeStruct((n_tile, half + 16, 128), BF16),
            jax.ShapeDtypeStruct((FIELDS, rows, columns), F32),
        ),
        in_specs=[pl.BlockSpec(memory_space=pltpu.HBM)] * len(inputs),
        out_specs=tuple(vmem(2)),
        scratch_shapes=[pltpu.VMEM(x.shape, x.dtype) for x in inputs] + [pltpu.SemaphoreType.DMA((len(inputs),))],
        compiler_params=params,
        name="pack_tiles",
    )(*inputs)
    got = lax.all_to_all(slots, "tile", split_axis=0, concat_axis=0, tiled=True)

    packet = (FIELDS + 1) * HALO + 6 * n_tile
    ext, pix, even, odd = pl.pallas_call(
        functools.partial(pack_rows_kernel, n_tile),
        out_shape=(
            jax.ShapeDtypeStruct((FIELDS, rows, 256), F32),
            jax.ShapeDtypeStruct((6 * n_tile, 128), F32),
            jax.ShapeDtypeStruct((packet, 128), BF16),
            jax.ShapeDtypeStruct((packet, 128), BF16),
        ),
        in_specs=vmem(2),
        out_specs=tuple(vmem(4)),
        compiler_params=params,
        name="pack_rows",
    )(fields, got)
    even = lax.ppermute(even, "grp", [(i, i ^ 1) for i in range(n_grp)])
    odd = lax.ppermute(odd, "grp", [(i, (i - 1 + 2 * (i % 2)) % n_grp) for i in range(n_grp)])

    increment, hessian_probe, probe_low, panels_near = pl.pallas_call(
        functools.partial(solve_kernel, n_grp, n_tile),
        out_shape=(
            jax.ShapeDtypeStruct((2, rows, columns), F32),
            jax.ShapeDtypeStruct((rows, columns), F32),
            jax.ShapeDtypeStruct((rows, columns), BF16),
            jax.ShapeDtypeStruct((panels.shape[0], n_grp, rows, columns), BF16),
        ),
        in_specs=vmem(4) + [pl.BlockSpec(memory_space=pltpu.HBM)] * 2,
        out_specs=tuple(vmem(4)),
        scratch_shapes=[
            pltpu.VMEM((FIELDS, 2, span, 128), F32),
            pltpu.VMEM((10, span, 256), F32),
            pltpu.VMEM((2, span, 256), F32),
            pltpu.VMEM((3, 2, span, 256), F32),
            pltpu.VMEM((2, 2, span, 128), F32),
            pltpu.VMEM(base_velocity.shape, F32),
            pltpu.SemaphoreType.DMA((1 + n_grp,)),
        ],
        compiler_params=params,
        name="solve",
    )(ext, pix, odd, even, inputs[0], pltpu.with_memory_space_constraint(panels, pltpu.HBM))

    column = [probe_low] + [
        lax.ppermute(probe_low, "grp", [(i, i ^ k) for i in range(n_grp)]) for k in distances(n_grp)[1:]
    ]
    sums = pl.pallas_call(
        project_kernel,
        out_shape=jax.ShapeDtypeStruct((panels.shape[0], 8, 128), F32),
        in_specs=vmem(n_grp),
        out_specs=pl.BlockSpec(memory_space=pltpu.VMEM),
        compiler_params=params,
        cost_estimate=pl.CostEstimate(
            flops=2 * panels.size * (n_grp - 1) // n_grp, bytes_accessed=2 * panels.size, transcendentals=0
        ),
        name="project",
    )(panels_near, *column[:-1])
    partial = pl.pallas_call(
        project_last_kernel,
        out_shape=jax.ShapeDtypeStruct((n_grp * n_tile, 1, 128), F32),
        in_specs=vmem(3),
        out_specs=pl.BlockSpec(memory_space=pltpu.VMEM),
        compiler_params=params,
        name="project_last",
    )(panels_near, column[-1], sums)
    everyone = lax.all_to_all(partial, ("grp", "tile"), split_axis=0, concat_axis=0, tiled=True)
    coefficients = pl.pallas_call(
        add_lines_kernel,
        out_shape=jax.ShapeDtypeStruct((1, 128), F32),
        in_specs=vmem(1),
        out_specs=pl.BlockSpec(memory_space=pltpu.VMEM),
        compiler_params=params,
        name="add_lines",
    )(everyone)
    return increment, hessian_probe, coefficients.reshape(128)


def solution(mesh):
    in_specs = (
        P(None, "grp", "tile"),
        P("grp", "tile"),
        P("grp", "tile"),
        P("grp", "tile"),
        P("grp", "tile", None, None),
        P("grp", "tile", None, None),
        P("grp", "tile", None, None),
        P("grp", "tile", None, None),
        P("grp", None, "tile"),
    )
    out_specs = (P(None, "grp", "tile"), P("grp", "tile"), P())
    return jax.shard_map(
        on_device, mesh=mesh, in_specs=in_specs, out_specs=out_specs, check_vma=False
    )
```

```python
import functools

import jax
import jax.numpy as jnp
from jax import lax
from jax.experimental import pallas as pl
from jax.experimental.pallas import tpu as pltpu
from jax.sharding import PartitionSpec as P

SWEEPS = 8
RELAX = 0.8
CAP = 64
HALO = 16
EDGE = 8
FIELDS = 4
STRIPS = 8
F32 = jnp.float32
BF16 = jnp.bfloat16


def lanes(shape=(8, 128)):
    return lax.broadcasted_iota(jnp.int32, shape, len(shape) - 1)


def fetch(sources, targets, sems):
    copies = [pltpu.make_async_copy(s, d, sems.at[i]) for i, (s, d) in enumerate(zip(sources, targets))]
    for copy in copies:
        copy.start()
    return copies


def pack_tiles_kernel(n_tile, *refs):
    sources, (out_ref, fields_ref), targets, sems = refs[:8], refs[8:10], refs[10:18], refs[18]
    copies = fetch(sources, targets, sems)
    bv_ref, visc_ref, fric_ref, fp_ref, los_ref, weight_ref, cell_ref, count_ref = targets
    t = lax.axis_index("tile")
    parity = lax.rem(t, 2)
    rows = visc_ref.shape[0]
    half = rows // 2
    for copy in copies[4:]:
        copy.wait()
    row_lane = lanes((1, 128))
    low = lanes() < CAP
    straight, turned = [], []
    for j in range(n_tile // 2):
        at = pl.ds(j * 128, 128)
        count = jnp.where(
            row_lane < CAP, count_ref[0, 0, :, 2 * j : 2 * j + 1], count_ref[0, 0, :, 2 * j + 1 : 2 * j + 2]
        )
        live = (row_lane & (CAP - 1)) < count
        weight = jnp.where(live, weight_ref[0, 0, :, at], 0.0)
        scaled = jnp.sqrt(weight) * los_ref[0, 0, :, at]
        high = scaled.astype(BF16).astype(F32)
        cell = cell_ref[0, 0, :, at]
        block = jnp.concatenate(
            [
                high, scaled - high,
                lax.shift_right_logical(cell, 7).astype(F32), (cell & 127).astype(F32), jnp.zeros((2, 128), F32),
            ],
            axis=0,
        )
        straight.append(block)
        turned.append(pltpu.roll(block, CAP, 1))
    nothing = jnp.zeros((8, 128), F32)
    in_half = (lanes() // CAP) == parity

    def placed(owner, side):
        if owner < 0 or owner >= n_tile:
            return nothing
        return (straight if owner % 2 == side else turned)[owner // 2]

    for d in range(n_tile):
        solo = jnp.where(parity == d % 2, straight[d // 2], turned[d // 2])
        solo = jnp.where(in_half, solo, 0.0)
        pair = jnp.where(low, placed(d - 1, 0), placed(d + 1, 1))
        out_ref[d, half : half + 16, :] = jnp.concatenate([solo, pair], axis=0).astype(BF16)

    for copy in copies[:4]:
        copy.wait()
    probe = fp_ref[...]
    fields = [-(probe * bv_ref[0]), -(probe * bv_ref[1]), visc_ref[...], fric_ref[...]]
    for f, field in enumerate(fields):
        fields_ref[f] = field
    lane = lanes((half, 128))

    def fold(first_lane):
        packed = jnp.zeros((half, 128), F32)
        for part in range(2):
            for f, field in enumerate(fields):
                start = part * 64 + f * HALO
                piece = field[part * half : (part + 1) * half]
                piece = pltpu.roll(piece, (start - first_lane) % 128, 1)
                packed = jnp.where((lane >= start) & (lane < start + HALO), piece, packed)
        return packed

    @pl.when(t < n_tile - 1)
    def _():
        out_ref[t + 1, 0:half, :] = fold(128 - HALO).astype(BF16)

    @pl.when(t > 0)
    def _():
        out_ref[t - 1, 0:half, :] = fold(0).astype(BF16)


def pack_rows_kernel(n_tile, fields_ref, got_ref, ext_ref, pix_ref, even_ref, odd_ref):
    g = lax.axis_index("grp")
    t = lax.axis_index("tile")
    rows = fields_ref.shape[1]
    half = rows // 2
    fields = [fields_ref[f] for f in range(FIELDS)]
    lane = lanes((half, 128))
    right = jnp.where(t < n_tile - 1, got_ref[jnp.minimum(t + 1, n_tile - 1), 0:half, :].astype(F32), 0.0)
    left = jnp.where(t > 0, got_ref[jnp.maximum(t - 1, 0), 0:half, :].astype(F32), 0.0)
    band = lanes((HALO, 128))
    edge_up = jnp.zeros((HALO, 128), F32)
    edge_down = jnp.zeros((HALO, 128), F32)
    for f, field in enumerate(fields):
        ext_ref[f, :, 0:128] = field
        edges = []
        for part in range(2):
            start = part * 64 + f * HALO
            edge = jnp.where(
                lane < HALO,
                pltpu.roll(right, (0 - start) % 128, 1),
                jnp.where(lane >= 128 - HALO, pltpu.roll(left, (128 - HALO - start) % 128, 1), 0.0),
            )
            ext_ref[f, part * half : (part + 1) * half, 128:256] = edge
            edges.append(edge)
        here = (band >= 2 * f * HALO) & (band < 2 * (f + 1) * HALO)
        turn = (2 * f + 1) * HALO % 128
        edge_up = jnp.where(here, pltpu.roll(edges[0][0:HALO], turn, 1), edge_up)
        edge_down = jnp.where(here, pltpu.roll(edges[1][half - HALO :], turn, 1), edge_down)
    low = lanes() < CAP
    near, far = [], []
    for s in range(0, n_tile, 2):
        one = got_ref[s, half : half + 16, :].astype(F32)
        two = got_ref[s + 1, half : half + 16, :].astype(F32)
        near.append(jnp.where(low, one[0:8], two[0:8]))
        far += [one[8:16], two[8:16]]
    blocks = near + far
    pixels = jnp.concatenate(
        [b[0:1] + b[2:3] for b in blocks]
        + [b[1:2] + b[3:4] for b in blocks]
        + [b[4:5] for b in blocks]
        + [b[5:6] for b in blocks],
        axis=0,
    )
    pix_ref[...] = pixels
    pixels = pixels.astype(BF16)

    even = lax.rem(g, 2) == 0

    def choose(one, two):
        even_ref_value, odd_ref_value = jnp.where(even, one, two), jnp.where(even, two, one)
        return even_ref_value.astype(BF16), odd_ref_value.astype(BF16)

    for f, field in enumerate(fields):
        at = pl.ds(f * HALO, HALO)
        even_ref[at, :], odd_ref[at, :] = choose(field[rows - HALO :], field[0:HALO])
    at = pl.ds(FIELDS * HALO, HALO)
    even_ref[at, :], odd_ref[at, :] = choose(edge_down, edge_up)
    for ref in (even_ref, odd_ref):
        ref[(FIELDS + 1) * HALO :, :] = pixels


def solve_kernel(
    n_grp, n_tile, ext_ref, pix_ref, odd_ref, even_ref, bv_hbm, panels_hbm,
    inc_hbm, hess_ref, low_ref, panels_ref,
    plane_ref, coef_ref, src_ref, w_ref, nat_ref, bv_ref, inc_ref, sems, inc_sem,
):
    size = panels_ref.shape[2]
    copies = fetch(
        [bv_hbm] + [panels_hbm.at[:, pl.ds(i * size, size), :] for i in range(n_grp)],
        [bv_ref] + [panels_ref.at[:, i] for i in range(n_grp)],
        sems,
    )
    g = lax.axis_index("grp")
    t = lax.axis_index("tile")
    rows = ext_ref.shape[1]
    span = rows + 2 * HALO
    groups = span // STRIPS
    lane = lanes()

    even = lax.rem(g, 2) == 0

    def above(first, size):
        at = pl.ds(first, size)
        got = jnp.where(even, odd_ref[at, :].astype(F32), even_ref[at, :].astype(F32))
        return jnp.where(g > 0, got, 0.0)

    def below(first, size):
        at = pl.ds(first, size)
        got = jnp.where(even, even_ref[at, :].astype(F32), odd_ref[at, :].astype(F32))
        return jnp.where(g < n_grp - 1, got, 0.0)

    first_lane = lane == 0
    last_lane = lane == 127

    band = lanes((HALO, 128))
    for f in range(FIELDS):
        for h in range(2):
            plane_ref[f, h, HALO : HALO + rows, :] = ext_ref[f, :, h * 128 : (h + 1) * 128]
        for load, at in ((above, 0), (below, HALO + rows)):
            plane_ref[f, 0, at : at + HALO, :] = load(f * HALO, HALO)
            edge = pltpu.roll(load(FIELDS * HALO, HALO), (0 - (2 * f + 1) * HALO) % 128, 1)
            plane_ref[f, 1, at : at + HALO, :] = jnp.where((band < HALO) | (band >= 128 - HALO), edge, 0.0)

    def strided(f, h, v):
        return plane_ref[f, h, pl.ds(v, STRIPS, stride=groups), :]

    def beside(pair):
        a, b = pair
        ra, rb = pltpu.roll(a, 1, 1), pltpu.roll(b, 1, 1)
        before = (jnp.where(first_lane, rb, ra), jnp.where(first_lane, ra, rb))
        ra, rb = pltpu.roll(a, 127, 1), pltpu.roll(b, 127, 1)
        after = (jnp.where(last_lane, rb, ra), jnp.where(last_lane, ra, rb))
        return before, pair, after

    def row(load, v):
        if v < 0:
            return beside(tuple(pltpu.roll(load(h, groups - 1), 1, 0) for h in range(2)))
        if v == groups:
            return beside(tuple(pltpu.roll(load(h, 0), STRIPS - 1, 0) for h in range(2)))
        return beside(tuple(load(h, v) for h in range(2)))

    strip = lax.broadcasted_iota(jnp.int32, (8, 128), 0)
    col_in = [
        None,
        ((lane < HALO) & (t < n_tile - 1)) | ((lane >= 128 - HALO) & (t > 0)),
    ]
    load_visc = functools.partial(strided, 2)
    prev, cur = row(load_visc, -1), row(load_visc, 0)
    for v in range(groups):
        nxt = row(load_visc, v + 1)
        place = g * rows - HALO + strip * groups + v
        row_in = (place >= 0) & (place < n_grp * rows)
        at = pl.ds(v * 8, 8)
        for h in range(2):
            centre = cur[1][h]
            east = 0.5 * (centre + nxt[1][h])
            west = 0.5 * (centre + prev[1][h])
            north = 0.5 * (centre + cur[2][h])
            south = 0.5 * (centre + cur[0][h])
            node_pp = 0.25 * (centre + nxt[1][h] + cur[2][h] + nxt[2][h])
            node_mm = 0.25 * (centre + prev[1][h] + cur[0][h] + prev[0][h])
            node_pm = 0.25 * (centre + nxt[1][h] + cur[0][h] + nxt[0][h])
            node_mp = 0.25 * (centre + prev[1][h] + cur[2][h] + prev[2][h])
            fric = strided(3, h, v)
            diag_x = fric + 2.0 * (east + west) + (north + south)
            diag_y = fric + (east + west) + 2.0 * (north + south)
            inside = row_in if col_in[h] is None else row_in & col_in[h]
            inv_x = jnp.where(inside, RELAX / jnp.where(inside, diag_x, 1.0), 0.0)
            inv_y = jnp.where(inside, RELAX / jnp.where(inside, diag_y, 1.0), 0.0)
            cols = pl.ds(h * 128, 128)
            for i, plane in enumerate(
                (east, west, north, south, 0.25 * node_pp, 0.25 * node_mm, 0.25 * node_pm, 0.25 * node_mp, inv_x, inv_y)
            ):
                coef_ref[i, at, cols] = plane
            src_ref[0, at, cols] = inv_x * strided(0, h, v)
            src_ref[1, at, cols] = inv_y * strided(1, h, v)
        prev, cur = cur, nxt

    def natural(h, v):
        return (h, pl.ds(v, STRIPS, stride=groups), slice(None))

    def relax():
        w_ref[0] = src_ref[...]

        def sweep(now, later, start):
            rows_seen = {}

            def both(v):
                if v not in rows_seen:
                    rows_seen[v] = tuple(
                        row(lambda h, u, c=c: now[c, pl.ds(u * 8, 8), pl.ds(h * 128, 128)], v) for c in range(2)
                    )
                return rows_seen[v]

            for p in range(groups):
                v = (p + start) % groups
                prev, cur, nxt = both(v - 1), both(v), both(v + 1)
                at = pl.ds(v * 8, 8)
                for h in range(2):
                    cols = pl.ds(h * 128, 128)
                    east, west, north, south, pp, mm, pm, mp, inv_x, inv_y = (
                        coef_ref[i, at, cols] for i in range(10)
                    )

                    def along(c):
                        return (
                            east * nxt[c][1][h] + west * prev[c][1][h],
                            north * cur[c][2][h] + south * cur[c][0][h],
                        )

                    def cross(c):
                        return (
                            pp * nxt[c][2][h] + mm * prev[c][0][h] - pm * nxt[c][0][h] - mp * prev[c][2][h]
                        )

                    one, two = along(0)
                    sum_x = 2.0 * one + two + cross(1)
                    one, two = along(1)
                    sum_y = one + 2.0 * two + cross(0)
                    for c, new in ((0, inv_x * sum_x), (1, inv_y * sum_y)):
                        new = (1.0 - RELAX) * cur[c][1][h] + src_ref[c, at, cols] + new
                        if later is None:
                            nat_ref[(c,) + natural(h, v)] = new
                        else:
                            later[c, at, cols] = new

        def three_sweeps(_, carry):
            for k in range(3):
                sweep(w_ref.at[k], w_ref.at[(k + 1) % 3], k)
            return carry

        lax.fori_loop(0, (SWEEPS - 2) // 3, three_sweeps, 0)
        sweep(w_ref.at[0], None, 0)

    def solve(phase, carry):
        relax()

        @pl.when(phase == 0)
        def _():
            for c in range(2):
                inc_ref[c] = nat_ref[c, 0, HALO : HALO + rows, :]
            pltpu.make_async_copy(inc_ref, inc_hbm, inc_sem).start()
            misfit()

        return carry

    def misfit():
        n_near, n_all = n_tile // 2, 3 * n_tile // 2
        low = lanes((n_tile, 128)) < CAP
        spans = ((0, HALO, rows), (-1, HALO - EDGE, EDGE), (1, HALO + rows, EDGE))
        rim_lane = lanes((2 * rows, 128))
        jobs = []
        for delta, first, size in spans:
            if delta == 0:
                values = pix_ref[...]
            else:
                base = (FIELDS + 1) * HALO
                values = (above if delta < 0 else below)(base, 4 * n_all)
            los_x, los_y, r, c = (values[q * n_all : (q + 1) * n_all] for q in range(4))
            if delta < 0:
                r = r - (rows - EDGE)
            in_rim = c[n_near:] + jnp.where(low, float(EDGE) - 128.0, float(EDGE))
            for h, begin, count, lane_of in ((0, 0, n_near, c[0:n_near]), (1, n_near, n_tile, in_rim)):
                parts = []
                for comp in range(2):
                    part = nat_ref[comp, h, first : first + size, :]
                    parts.append(part if h == 0 else pltpu.roll(part, EDGE, 1))
                field = jnp.concatenate(parts, axis=0)
                high = field.astype(BF16).astype(F32)
                rest = field - high
                if h == 0:
                    stacked = jnp.concatenate([high.astype(BF16), rest.astype(BF16)], axis=1)
                else:
                    lane_here = rim_lane[0 : 2 * size]
                    stacked = jnp.where(lane_here < 2 * EDGE, high, pltpu.roll(rest, 2 * EDGE, 1))
                    stacked = jnp.where(lane_here < 4 * EDGE, stacked, 0.0).astype(BF16)
                jobs.append((h, first, size, begin, count, lane_of, los_x, los_y, r, stacked))

        nat_ref[...] = jnp.zeros_like(nat_ref)
        for h, first, size, begin, count, lane_of, los_x, los_y, r, stacked in jobs:
            chunk = 4 if h == 0 else 8
            depth = 128 if h == 0 else 2 * EDGE
            wide = chunk * 128
            row_id = lax.broadcasted_iota(jnp.int32, (size, wide), 0).astype(F32)
            lane_id = lax.broadcasted_iota(jnp.int32, (depth, wide), 0).astype(F32)
            total = jnp.zeros((4 * size, 128), F32)
            for j in range(0, count, chunk):

                def line(table, offset):
                    return jnp.concatenate([table[offset + i : offset + i + 1] for i in range(j, j + chunk)], axis=1)

                line_x, line_y = line(los_x, begin), line(los_y, begin)
                hot = jnp.where(lane_id == line(lane_of, 0), 1.0, 0.0).astype(BF16)
                here = row_id == line(r, begin)
                twice = [hot, hot]
                if h == 1:
                    twice.append(jnp.zeros((128 - 2 * depth, wide), BF16))
                    hot = jnp.concatenate([hot, jnp.zeros((128 - depth, wide), BF16)], axis=0)
                got = jnp.dot(stacked, jnp.concatenate(twice, axis=0), preferred_element_type=F32)
                got_x = jnp.sum(jnp.where(here, got[0:size], 0.0), axis=0, keepdims=True)
                got_y = jnp.sum(jnp.where(here, got[size:], 0.0), axis=0, keepdims=True)
                amount = line_x * got_x + line_y * got_y
                terms = [amount * line_x, amount * line_y]
                highs = [p.astype(BF16).astype(F32) for p in terms]
                terms = highs + [p - q for p, q in zip(terms, highs)]
                spread = jnp.concatenate([jnp.where(here, p, 0.0) for p in terms], axis=0).astype(BF16)
                total = total + lax.dot_general(spread, hot, (((1,), (1,)), ((), ())), preferred_element_type=F32)
            total = total[0 : 2 * size] + total[2 * size :]
            if h == 1:
                total = pltpu.roll(total, 128 - EDGE, 1)
            for c in range(2):
                nat_ref[c, h, first : first + size, :] = total[c * size : (c + 1) * size]

        for v in range(groups):
            at = pl.ds(v * 8, 8)
            for h in range(2):
                cols = pl.ds(h * 128, 128)
                for c in range(2):
                    src_ref[c, at, cols] = coef_ref[8 + c, at, cols] * nat_ref[(c,) + natural(h, v)]

    lax.fori_loop(0, 2, solve, 0)
    for copy in copies:
        copy.wait()
    pltpu.make_async_copy(inc_ref, inc_hbm, inc_sem).wait()
    hess = -(bv_ref[0] * nat_ref[0, 0, HALO : HALO + rows, :] + bv_ref[1] * nat_ref[1, 0, HALO : HALO + rows, :])
    hess_ref[...] = hess
    low_ref[...] = hess.astype(BF16)


def distances(n_grp):
    return [0] + list(range(2, n_grp)) + [1]


def project_block(panels_ref, probe_ref, k, distance):
    count, n_grp, rows, columns = panels_ref.shape
    product = panels_ref[k, lax.axis_index("grp") ^ distance].astype(F32) * probe_ref[...].astype(F32)
    return jnp.sum(product.reshape(-1, 8, columns), axis=0)


def project_kernel(panels_ref, hess_ref, *refs):
    blocks, (sums_ref, hess_hbm, sem) = refs[:-3], refs[-3:]
    copy = pltpu.make_async_copy(hess_ref, hess_hbm, sem)
    copy.start()
    order = distances(panels_ref.shape[1])
    for k in range(panels_ref.shape[0]):
        sums_ref[k] = sum(project_block(panels_ref, block, k, i) for i, block in zip(order, blocks))
    copy.wait()


def project_last_kernel(panels_ref, block_ref, sums_ref, out_ref):
    count, n_grp = panels_ref.shape[:2]
    sums = []
    for k in range(count):
        total = sums_ref[k] + project_block(panels_ref, block_ref, k, distances(n_grp)[-1])
        sums.append(jnp.sum(total, axis=0, keepdims=True))
    sums.append(jnp.zeros((128 - count, 128), F32))
    table = jnp.concatenate(sums, axis=0)
    line = lax.dot_general(
        jnp.ones((8, 128), F32), table, (((1,), (1,)), ((), ())),
        precision=lax.Precision.HIGHEST, preferred_element_type=F32,
    )
    line = pltpu.roll(line, lax.axis_index("grp") * count, 1)[0:1]
    out_ref[...] = jnp.broadcast_to(line[None], out_ref.shape)


def add_lines_kernel(lines_ref, out_ref):
    out_ref[...] = jnp.sum(lines_ref[...], axis=0)


def vmem(n):
    return [pl.BlockSpec(memory_space=pltpu.VMEM)] * n


def on_device(
    base_velocity, viscosity, friction, friction_probe, pixel_los, pixel_weight, pixel_cell, pixel_count, panels
):
    n_grp, n_tile = lax.axis_size("grp"), lax.axis_size("tile")
    rows, columns = viscosity.shape
    half = rows // 2
    span = rows + 2 * HALO
    params = pltpu.CompilerParams(vmem_limit_bytes=32 * 2**20)

    inputs = [
        pltpu.with_memory_space_constraint(x, pltpu.HBM)
        for x in (
            base_velocity, viscosity, friction, friction_probe, pixel_los, pixel_weight, pixel_cell, pixel_count
        )
    ]
    slots, fields = pl.pallas_call(
        functools.partial(pack_tiles_kernel, n_tile),
        out_shape=(
            jax.ShapeDtypeStruct((n_tile, half + 16, 128), BF16),
            jax.ShapeDtypeStruct((FIELDS, rows, columns), F32),
        ),
        in_specs=[pl.BlockSpec(memory_space=pltpu.HBM)] * len(inputs),
        out_specs=tuple(vmem(2)),
        scratch_shapes=[pltpu.VMEM(x.shape, x.dtype) for x in inputs] + [pltpu.SemaphoreType.DMA((len(inputs),))],
        compiler_params=params,
        name="pack_tiles",
    )(*inputs)
    got = lax.all_to_all(slots, "tile", split_axis=0, concat_axis=0, tiled=True)

    packet = (FIELDS + 1) * HALO + 6 * n_tile
    ext, pix, even, odd = pl.pallas_call(
        functools.partial(pack_rows_kernel, n_tile),
        out_shape=(
            jax.ShapeDtypeStruct((FIELDS, rows, 256), F32),
            jax.ShapeDtypeStruct((6 * n_tile, 128), F32),
            jax.ShapeDtypeStruct((packet, 128), BF16),
            jax.ShapeDtypeStruct((packet, 128), BF16),
        ),
        in_specs=vmem(2),
        out_specs=tuple(vmem(4)),
        compiler_params=params,
        name="pack_rows",
    )(fields, got)
    even = lax.ppermute(even, "grp", [(i, i ^ 1) for i in range(n_grp)])
    odd = lax.ppermute(odd, "grp", [(i, (i - 1 + 2 * (i % 2)) % n_grp) for i in range(n_grp)])

    increment, hess, probe_low, panels_near = pl.pallas_call(
        functools.partial(solve_kernel, n_grp, n_tile),
        out_shape=(
            jax.ShapeDtypeStruct((2, rows, columns), F32),
            jax.ShapeDtypeStruct((rows, columns), F32),
            jax.ShapeDtypeStruct((rows, columns), BF16),
            jax.ShapeDtypeStruct((panels.shape[0], n_grp, rows, columns), BF16),
        ),
        in_specs=vmem(4) + [pl.BlockSpec(memory_space=pltpu.HBM)] * 2,
        out_specs=tuple([pl.BlockSpec(memory_space=pltpu.HBM)] + vmem(3)),
        scratch_shapes=[
            pltpu.VMEM((FIELDS, 2, span, 128), F32),
            pltpu.VMEM((10, span, 256), F32),
            pltpu.VMEM((2, span, 256), F32),
            pltpu.VMEM((3, 2, span, 256), F32),
            pltpu.VMEM((2, 2, span, 128), F32),
            pltpu.VMEM(base_velocity.shape, F32),
            pltpu.VMEM(base_velocity.shape, F32),
            pltpu.SemaphoreType.DMA((1 + n_grp,)),
            pltpu.SemaphoreType.DMA,
        ],
        compiler_params=params,
        name="solve",
    )(ext, pix, odd, even, inputs[0], pltpu.with_memory_space_constraint(panels, pltpu.HBM))

    column = [probe_low] + [
        lax.ppermute(probe_low, "grp", [(i, i ^ k) for i in range(n_grp)]) for k in distances(n_grp)[1:]
    ]
    sums, hessian_probe = pl.pallas_call(
        project_kernel,
        out_shape=(
            jax.ShapeDtypeStruct((panels.shape[0], 8, 128), F32),
            jax.ShapeDtypeStruct((rows, columns), F32),
        ),
        in_specs=vmem(1 + n_grp),
        out_specs=(pl.BlockSpec(memory_space=pltpu.VMEM), pl.BlockSpec(memory_space=pltpu.HBM)),
        scratch_shapes=[pltpu.SemaphoreType.DMA],
        compiler_params=params,
        cost_estimate=pl.CostEstimate(
            flops=2 * panels.size * (n_grp - 1) // n_grp, bytes_accessed=2 * panels.size, transcendentals=0
        ),
        name="project",
    )(panels_near, hess, *column[:-1])
    partial = pl.pallas_call(
        project_last_kernel,
        out_shape=jax.ShapeDtypeStruct((n_grp * n_tile, 1, 128), F32),
        in_specs=vmem(3),
        out_specs=pl.BlockSpec(memory_space=pltpu.VMEM),
        compiler_params=params,
        name="project_last",
    )(panels_near, column[-1], sums)
    everyone = lax.all_to_all(partial, ("grp", "tile"), split_axis=0, concat_axis=0, tiled=True)
    coefficients = pl.pallas_call(
        add_lines_kernel,
        out_shape=jax.ShapeDtypeStruct((1, 128), F32),
        in_specs=vmem(1),
        out_specs=pl.BlockSpec(memory_space=pltpu.VMEM),
        compiler_params=params,
        name="add_lines",
    )(everyone)
    return increment, hessian_probe, coefficients.reshape(128)


def solution(mesh):
    in_specs = (
        P(None, "grp", "tile"),
        P("grp", "tile"),
        P("grp", "tile"),
        P("grp", "tile"),
        P("grp", "tile", None, None),
        P("grp", "tile", None, None),
        P("grp", "tile", None, None),
        P("grp", "tile", None, None),
        P("grp", None, "tile"),
    )
    out_specs = (P(None, "grp", "tile"), P("grp", "tile"), P())
    return jax.shard_map(
        on_device, mesh=mesh, in_specs=in_specs, out_specs=out_specs, check_vma=False
    )
```

```python
import functools

import jax
import jax.numpy as jnp
from jax import lax
from jax.experimental import pallas as pl
from jax.experimental.pallas import tpu as pltpu
from jax.sharding import PartitionSpec as P

SWEEPS = 8
RELAX = 0.8
CAP = 64
HALO = 16
EDGE = 8
FIELDS = 4
STRIPS = 8
F32 = jnp.float32
BF16 = jnp.bfloat16


def lanes(shape=(8, 128)):
    return lax.broadcasted_iota(jnp.int32, shape, len(shape) - 1)


def fetch(sources, targets, sems):
    copies = [pltpu.make_async_copy(s, d, sems.at[i]) for i, (s, d) in enumerate(zip(sources, targets))]
    for copy in copies:
        copy.start()
    return copies


def pack_tiles_kernel(n_tile, *refs):
    sources, (out_ref, fields_ref), targets, sems = refs[:8], refs[8:10], refs[10:18], refs[18]
    copies = fetch(sources, targets, sems)
    bv_ref, visc_ref, fric_ref, fp_ref, los_ref, weight_ref, cell_ref, count_ref = targets
    t = lax.axis_index("tile")
    parity = lax.rem(t, 2)
    rows = visc_ref.shape[0]
    half = rows // 2
    for copy in copies[4:]:
        copy.wait()
    row_lane = lanes((1, 128))
    low = lanes() < CAP
    straight, turned = [], []
    for j in range(n_tile // 2):
        at = pl.ds(j * 128, 128)
        count = jnp.where(
            row_lane < CAP, count_ref[0, 0, :, 2 * j : 2 * j + 1], count_ref[0, 0, :, 2 * j + 1 : 2 * j + 2]
        )
        live = (row_lane & (CAP - 1)) < count
        weight = jnp.where(live, weight_ref[0, 0, :, at], 0.0)
        scaled = jnp.sqrt(weight) * los_ref[0, 0, :, at]
        high = scaled.astype(BF16).astype(F32)
        cell = cell_ref[0, 0, :, at]
        block = jnp.concatenate(
            [
                high, scaled - high,
                lax.shift_right_logical(cell, 7).astype(F32), (cell & 127).astype(F32), jnp.zeros((2, 128), F32),
            ],
            axis=0,
        )
        straight.append(block)
        turned.append(pltpu.roll(block, CAP, 1))
    nothing = jnp.zeros((8, 128), F32)
    in_half = (lanes() // CAP) == parity

    def placed(owner, side):
        if owner < 0 or owner >= n_tile:
            return nothing
        return (straight if owner % 2 == side else turned)[owner // 2]

    for d in range(n_tile):
        solo = jnp.where(parity == d % 2, straight[d // 2], turned[d // 2])
        solo = jnp.where(in_half, solo, 0.0)
        pair = jnp.where(low, placed(d - 1, 0), placed(d + 1, 1))
        out_ref[d, half : half + 16, :] = jnp.concatenate([solo, pair], axis=0).astype(BF16)

    for copy in copies[:4]:
        copy.wait()
    probe = fp_ref[...]
    fields = [-(probe * bv_ref[0]), -(probe * bv_ref[1]), visc_ref[...], fric_ref[...]]
    for f, field in enumerate(fields):
        fields_ref[f] = field
    lane = lanes((half, 128))

    def fold(first_lane):
        packed = jnp.zeros((half, 128), F32)
        for part in range(2):
            for f, field in enumerate(fields):
                start = part * 64 + f * HALO
                piece = field[part * half : (part + 1) * half]
                piece = pltpu.roll(piece, (start - first_lane) % 128, 1)
                packed = jnp.where((lane >= start) & (lane < start + HALO), piece, packed)
        return packed

    @pl.when(t < n_tile - 1)
    def _():
        out_ref[t + 1, 0:half, :] = fold(128 - HALO).astype(BF16)

    @pl.when(t > 0)
    def _():
        out_ref[t - 1, 0:half, :] = fold(0).astype(BF16)


def pack_rows_kernel(n_tile, fields_ref, got_ref, ext_ref, pix_ref, even_ref, odd_ref):
    g = lax.axis_index("grp")
    t = lax.axis_index("tile")
    rows = fields_ref.shape[1]
    half = rows // 2
    fields = [fields_ref[f] for f in range(FIELDS)]
    lane = lanes((half, 128))
    right = jnp.where(t < n_tile - 1, got_ref[jnp.minimum(t + 1, n_tile - 1), 0:half, :].astype(F32), 0.0)
    left = jnp.where(t > 0, got_ref[jnp.maximum(t - 1, 0), 0:half, :].astype(F32), 0.0)
    band = lanes((HALO, 128))
    edge_up = jnp.zeros((HALO, 128), F32)
    edge_down = jnp.zeros((HALO, 128), F32)
    for f, field in enumerate(fields):
        ext_ref[f, :, 0:128] = field
        edges = []
        for part in range(2):
            start = part * 64 + f * HALO
            edge = jnp.where(
                lane < HALO,
                pltpu.roll(right, (0 - start) % 128, 1),
                jnp.where(lane >= 128 - HALO, pltpu.roll(left, (128 - HALO - start) % 128, 1), 0.0),
            )
            ext_ref[f, part * half : (part + 1) * half, 128:256] = edge
            edges.append(edge)
        here = (band >= 2 * f * HALO) & (band < 2 * (f + 1) * HALO)
        turn = (2 * f + 1) * HALO % 128
        edge_up = jnp.where(here, pltpu.roll(edges[0][0:HALO], turn, 1), edge_up)
        edge_down = jnp.where(here, pltpu.roll(edges[1][half - HALO :], turn, 1), edge_down)
    low = lanes() < CAP
    near, far = [], []
    for s in range(0, n_tile, 2):
        one = got_ref[s, half : half + 16, :].astype(F32)
        two = got_ref[s + 1, half : half + 16, :].astype(F32)
        near.append(jnp.where(low, one[0:8], two[0:8]))
        far += [one[8:16], two[8:16]]
    blocks = near + far
    pixels = jnp.concatenate(
        [b[0:1] + b[2:3] for b in blocks]
        + [b[1:2] + b[3:4] for b in blocks]
        + [b[4:5] for b in blocks]
        + [b[5:6] for b in blocks],
        axis=0,
    )
    pix_ref[...] = pixels
    pixels = pixels.astype(BF16)

    even = lax.rem(g, 2) == 0

    def choose(one, two):
        even_ref_value, odd_ref_value = jnp.where(even, one, two), jnp.where(even, two, one)
        return even_ref_value.astype(BF16), odd_ref_value.astype(BF16)

    for f, field in enumerate(fields):
        at = pl.ds(f * HALO, HALO)
        even_ref[at, :], odd_ref[at, :] = choose(field[rows - HALO :], field[0:HALO])
    at = pl.ds(FIELDS * HALO, HALO)
    even_ref[at, :], odd_ref[at, :] = choose(edge_down, edge_up)
    for ref in (even_ref, odd_ref):
        ref[(FIELDS + 1) * HALO :, :] = pixels


def solve_kernel(
    n_grp, n_tile, ext_ref, pix_ref, odd_ref, even_ref, bv_hbm, panels_hbm,
    inc_hbm, hess_ref, low_ref, panels_ref,
    plane_ref, coef_ref, src_ref, w_ref, nat_ref, bv_ref, inc_ref, sems, inc_sem,
):
    size = panels_ref.shape[2]
    copies = fetch(
        [bv_hbm] + [panels_hbm.at[:, pl.ds(i * size, size), :] for i in range(n_grp)],
        [bv_ref] + [panels_ref.at[:, i] for i in range(n_grp)],
        sems,
    )
    g = lax.axis_index("grp")
    t = lax.axis_index("tile")
    rows = ext_ref.shape[1]
    span = rows + 2 * HALO
    groups = span // STRIPS
    lane = lanes()

    even = lax.rem(g, 2) == 0

    def above(first, size):
        at = pl.ds(first, size)
        got = jnp.where(even, odd_ref[at, :].astype(F32), even_ref[at, :].astype(F32))
        return jnp.where(g > 0, got, 0.0)

    def below(first, size):
        at = pl.ds(first, size)
        got = jnp.where(even, even_ref[at, :].astype(F32), odd_ref[at, :].astype(F32))
        return jnp.where(g < n_grp - 1, got, 0.0)

    first_lane = lane == 0
    last_lane = lane == 127

    band = lanes((HALO, 128))
    for f in range(FIELDS):
        for h in range(2):
            plane_ref[f, h, HALO : HALO + rows, :] = ext_ref[f, :, h * 128 : (h + 1) * 128]
        for load, at in ((above, 0), (below, HALO + rows)):
            plane_ref[f, 0, at : at + HALO, :] = load(f * HALO, HALO)
            edge = pltpu.roll(load(FIELDS * HALO, HALO), (0 - (2 * f + 1) * HALO) % 128, 1)
            plane_ref[f, 1, at : at + HALO, :] = jnp.where((band < HALO) | (band >= 128 - HALO), edge, 0.0)

    def strided(f, h, v):
        return plane_ref[f, h, pl.ds(v, STRIPS, stride=groups), :]

    def beside(pair):
        a, b = pair
        ra, rb = pltpu.roll(a, 1, 1), pltpu.roll(b, 1, 1)
        before = (jnp.where(first_lane, rb, ra), jnp.where(first_lane, ra, rb))
        ra, rb = pltpu.roll(a, 127, 1), pltpu.roll(b, 127, 1)
        after = (jnp.where(last_lane, rb, ra), jnp.where(last_lane, ra, rb))
        return before, pair, after

    def row(load, v):
        if v < 0:
            return beside(tuple(pltpu.roll(load(h, groups - 1), 1, 0) for h in range(2)))
        if v == groups:
            return beside(tuple(pltpu.roll(load(h, 0), STRIPS - 1, 0) for h in range(2)))
        return beside(tuple(load(h, v) for h in range(2)))

    strip = lax.broadcasted_iota(jnp.int32, (8, 128), 0)
    col_in = [
        None,
        ((lane < HALO) & (t < n_tile - 1)) | ((lane >= 128 - HALO) & (t > 0)),
    ]
    load_visc = functools.partial(strided, 2)
    prev, cur = row(load_visc, -1), row(load_visc, 0)
    for v in range(groups):
        nxt = row(load_visc, v + 1)
        place = g * rows - HALO + strip * groups + v
        row_in = (place >= 0) & (place < n_grp * rows)
        at = pl.ds(v * 8, 8)
        for h in range(2):
            centre = cur[1][h]
            east = 0.5 * (centre + nxt[1][h])
            west = 0.5 * (centre + prev[1][h])
            north = 0.5 * (centre + cur[2][h])
            south = 0.5 * (centre + cur[0][h])
            node_pp = 0.25 * (centre + nxt[1][h] + cur[2][h] + nxt[2][h])
            node_mm = 0.25 * (centre + prev[1][h] + cur[0][h] + prev[0][h])
            node_pm = 0.25 * (centre + nxt[1][h] + cur[0][h] + nxt[0][h])
            node_mp = 0.25 * (centre + prev[1][h] + cur[2][h] + prev[2][h])
            fric = strided(3, h, v)
            diag_x = fric + 2.0 * (east + west) + (north + south)
            diag_y = fric + (east + west) + 2.0 * (north + south)
            inside = row_in if col_in[h] is None else row_in & col_in[h]
            inv_x = jnp.where(inside, RELAX / jnp.where(inside, diag_x, 1.0), 0.0)
            inv_y = jnp.where(inside, RELAX / jnp.where(inside, diag_y, 1.0), 0.0)
            cols = pl.ds(h * 128, 128)
            for i, plane in enumerate(
                (east, west, north, south, 0.25 * node_pp, 0.25 * node_mm, 0.25 * node_pm, 0.25 * node_mp, inv_x, inv_y)
            ):
                coef_ref[i, at, cols] = plane
            src_ref[0, at, cols] = inv_x * strided(0, h, v)
            src_ref[1, at, cols] = inv_y * strided(1, h, v)
        prev, cur = cur, nxt

    def natural(h, v):
        return (h, pl.ds(v, STRIPS, stride=groups), slice(None))

    def relax():
        w_ref[0] = src_ref[...]

        def sweep(now, later, start):
            rows_seen = {}

            def both(v):
                if v not in rows_seen:
                    rows_seen[v] = tuple(
                        row(lambda h, u, c=c: now[c, pl.ds(u * 8, 8), pl.ds(h * 128, 128)], v) for c in range(2)
                    )
                return rows_seen[v]

            for p in range(groups):
                v = (p + start) % groups
                prev, cur, nxt = both(v - 1), both(v), both(v + 1)
                at = pl.ds(v * 8, 8)
                for h in range(2):
                    cols = pl.ds(h * 128, 128)
                    east, west, north, south, pp, mm, pm, mp, inv_x, inv_y = (
                        coef_ref[i, at, cols] for i in range(10)
                    )

                    def along(c):
                        return (
                            east * nxt[c][1][h] + west * prev[c][1][h],
                            north * cur[c][2][h] + south * cur[c][0][h],
                        )

                    def cross(c):
                        return (
                            pp * nxt[c][2][h] + mm * prev[c][0][h] - pm * nxt[c][0][h] - mp * prev[c][2][h]
                        )

                    one, two = along(0)
                    sum_x = 2.0 * one + two + cross(1)
                    one, two = along(1)
                    sum_y = one + 2.0 * two + cross(0)
                    for c, new in ((0, inv_x * sum_x), (1, inv_y * sum_y)):
                        new = (1.0 - RELAX) * cur[c][1][h] + src_ref[c, at, cols] + new
                        if later is None:
                            nat_ref[(c,) + natural(h, v)] = new
                        else:
                            later[c, at, cols] = new

        def three_sweeps(_, carry):
            for k in range(3):
                sweep(w_ref.at[k], w_ref.at[(k + 1) % 3], k)
            return carry

        lax.fori_loop(0, (SWEEPS - 2) // 3, three_sweeps, 0)
        sweep(w_ref.at[0], None, 0)

    def solve(phase, carry):
        relax()

        @pl.when(phase == 0)
        def _():
            for c in range(2):
                inc_ref[c] = nat_ref[c, 0, HALO : HALO + rows, :]
            pltpu.make_async_copy(inc_ref, inc_hbm, inc_sem).start()
            misfit()

        return carry

    def misfit():
        n_near, n_all = n_tile // 2, 3 * n_tile // 2
        low = lanes((n_tile, 128)) < CAP
        spans = ((0, HALO, rows), (-1, HALO - EDGE, EDGE), (1, HALO + rows, EDGE))
        rim_lane = lanes((2 * rows, 128))
        jobs = []
        for delta, first, size in spans:
            if delta == 0:
                values = pix_ref[...]
            else:
                base = (FIELDS + 1) * HALO
                values = (above if delta < 0 else below)(base, 4 * n_all)
            los_x, los_y, r, c = (values[q * n_all : (q + 1) * n_all] for q in range(4))
            if delta < 0:
                r = r - (rows - EDGE)
            in_rim = c[n_near:] + jnp.where(low, float(EDGE) - 128.0, float(EDGE))
            for h, begin, count, lane_of in ((0, 0, n_near, c[0:n_near]), (1, n_near, n_tile, in_rim)):
                parts = []
                for comp in range(2):
                    part = nat_ref[comp, h, first : first + size, :]
                    parts.append(part if h == 0 else pltpu.roll(part, EDGE, 1))
                field = jnp.concatenate(parts, axis=0)
                high = field.astype(BF16).astype(F32)
                rest = field - high
                if h == 0:
                    stacked = jnp.concatenate([high.astype(BF16), rest.astype(BF16)], axis=1)
                else:
                    lane_here = rim_lane[0 : 2 * size]
                    stacked = jnp.where(lane_here < 2 * EDGE, high, pltpu.roll(rest, 2 * EDGE, 1))
                    stacked = jnp.where(lane_here < 4 * EDGE, stacked, 0.0).astype(BF16)
                jobs.append((h, first, size, begin, count, lane_of, los_x, los_y, r, stacked))

        nat_ref[...] = jnp.zeros_like(nat_ref)
        for h, first, size, begin, count, lane_of, los_x, los_y, r, stacked in jobs:
            chunk = 4 if h == 0 else 8
            depth = 128 if h == 0 else 2 * EDGE
            wide = chunk * 128
            row_id = lax.broadcasted_iota(jnp.int32, (size, wide), 0).astype(F32)
            lane_id = lax.broadcasted_iota(jnp.int32, (depth, wide), 0).astype(F32)
            total = jnp.zeros((4 * size, 128), F32)
            for j in range(0, count, chunk):

                def line(table, offset):
                    return jnp.concatenate([table[offset + i : offset + i + 1] for i in range(j, j + chunk)], axis=1)

                line_x, line_y = line(los_x, begin), line(los_y, begin)
                hot = jnp.where(lane_id == line(lane_of, 0), 1.0, 0.0).astype(BF16)
                here = row_id == line(r, begin)
                twice = [hot, hot]
                if h == 1:
                    twice.append(jnp.zeros((128 - 2 * depth, wide), BF16))
                    hot = jnp.concatenate([hot, jnp.zeros((128 - depth, wide), BF16)], axis=0)
                got = jnp.dot(stacked, jnp.concatenate(twice, axis=0), preferred_element_type=F32)
                got_x = jnp.sum(jnp.where(here, got[0:size], 0.0), axis=0, keepdims=True)
                got_y = jnp.sum(jnp.where(here, got[size:], 0.0), axis=0, keepdims=True)
                amount = line_x * got_x + line_y * got_y
                terms = [amount * line_x, amount * line_y]
                highs = [p.astype(BF16).astype(F32) for p in terms]
                terms = highs + [p - q for p, q in zip(terms, highs)]
                spread = jnp.concatenate([jnp.where(here, p, 0.0) for p in terms], axis=0).astype(BF16)
                total = total + lax.dot_general(spread, hot, (((1,), (1,)), ((), ())), preferred_element_type=F32)
            total = total[0 : 2 * size] + total[2 * size :]
            if h == 1:
                total = pltpu.roll(total, 128 - EDGE, 1)
            for c in range(2):
                nat_ref[c, h, first : first + size, :] = total[c * size : (c + 1) * size]

        for v in range(groups):
            at = pl.ds(v * 8, 8)
            for h in range(2):
                cols = pl.ds(h * 128, 128)
                for c in range(2):
                    src_ref[c, at, cols] = coef_ref[8 + c, at, cols] * nat_ref[(c,) + natural(h, v)]

    lax.fori_loop(0, 2, solve, 0)
    for copy in copies:
        copy.wait()
    pltpu.make_async_copy(inc_ref, inc_hbm, inc_sem).wait()
    hess = -(bv_ref[0] * nat_ref[0, 0, HALO : HALO + rows, :] + bv_ref[1] * nat_ref[1, 0, HALO : HALO + rows, :])
    hess_ref[...] = hess
    low_ref[...] = hess.astype(BF16)


def project_block(panels_ref, probe_ref, k, distance):
    count, n_grp, rows, columns = panels_ref.shape
    product = panels_ref[k, lax.axis_index("grp") ^ distance].astype(F32) * probe_ref[...].astype(F32)
    return jnp.sum(product.reshape(-1, 8, columns), axis=0)


def project_kernel(panels_ref, hess_ref, *refs):
    blocks, (sums_ref, hess_hbm, sem) = refs[:-3], refs[-3:]
    copy = pltpu.make_async_copy(hess_ref, hess_hbm, sem)
    copy.start()
    for k in range(panels_ref.shape[0]):
        sums_ref[k] = sum(project_block(panels_ref, block, k, i) for i, block in enumerate(blocks))
    copy.wait()


def project_last_kernel(panels_ref, block_ref, sums_ref, out_ref):
    count, n_grp = panels_ref.shape[:2]
    sums = []
    for k in range(count):
        total = sums_ref[k] + project_block(panels_ref, block_ref, k, n_grp - 1)
        sums.append(jnp.sum(total, axis=0, keepdims=True))
    sums.append(jnp.zeros((128 - count, 128), F32))
    table = jnp.concatenate(sums, axis=0)
    line = lax.dot_general(
        jnp.ones((8, 128), F32), table, (((1,), (1,)), ((), ())),
        precision=lax.Precision.HIGHEST, preferred_element_type=F32,
    )
    line = pltpu.roll(line, lax.axis_index("grp") * count, 1)[0:1]
    out_ref[...] = jnp.broadcast_to(line[None], out_ref.shape)


def add_lines_kernel(lines_ref, out_ref):
    out_ref[...] = jnp.sum(lines_ref[...], axis=0)


def vmem(n):
    return [pl.BlockSpec(memory_space=pltpu.VMEM)] * n


def on_device(
    base_velocity, viscosity, friction, friction_probe, pixel_los, pixel_weight, pixel_cell, pixel_count, panels
):
    n_grp, n_tile = lax.axis_size("grp"), lax.axis_size("tile")
    rows, columns = viscosity.shape
    half = rows // 2
    span = rows + 2 * HALO
    params = pltpu.CompilerParams(vmem_limit_bytes=32 * 2**20)

    inputs = [
        pltpu.with_memory_space_constraint(x, pltpu.HBM)
        for x in (
            base_velocity, viscosity, friction, friction_probe, pixel_los, pixel_weight, pixel_cell, pixel_count
        )
    ]
    slots, fields = pl.pallas_call(
        functools.partial(pack_tiles_kernel, n_tile),
        out_shape=(
            jax.ShapeDtypeStruct((n_tile, half + 16, 128), BF16),
            jax.ShapeDtypeStruct((FIELDS, rows, columns), F32),
        ),
        in_specs=[pl.BlockSpec(memory_space=pltpu.HBM)] * len(inputs),
        out_specs=tuple(vmem(2)),
        scratch_shapes=[pltpu.VMEM(x.shape, x.dtype) for x in inputs] + [pltpu.SemaphoreType.DMA((len(inputs),))],
        compiler_params=params,
        name="pack_tiles",
    )(*inputs)
    got = lax.all_to_all(slots, "tile", split_axis=0, concat_axis=0, tiled=True)

    packet = (FIELDS + 1) * HALO + 6 * n_tile
    ext, pix, even, odd = pl.pallas_call(
        functools.partial(pack_rows_kernel, n_tile),
        out_shape=(
            jax.ShapeDtypeStruct((FIELDS, rows, 256), F32),
            jax.ShapeDtypeStruct((6 * n_tile, 128), F32),
            jax.ShapeDtypeStruct((packet, 128), BF16),
            jax.ShapeDtypeStruct((packet, 128), BF16),
        ),
        in_specs=vmem(2),
        out_specs=tuple(vmem(4)),
        compiler_params=params,
        name="pack_rows",
    )(fields, got)
    even = lax.ppermute(even, "grp", [(i, i ^ 1) for i in range(n_grp)])
    odd = lax.ppermute(odd, "grp", [(i, (i - 1 + 2 * (i % 2)) % n_grp) for i in range(n_grp)])

    increment, hess, probe_low, panels_near = pl.pallas_call(
        functools.partial(solve_kernel, n_grp, n_tile),
        out_shape=(
            jax.ShapeDtypeStruct((2, rows, columns), F32),
            jax.ShapeDtypeStruct((rows, columns), F32),
            jax.ShapeDtypeStruct((rows, columns), BF16),
            jax.ShapeDtypeStruct((panels.shape[0], n_grp, rows, columns), BF16),
        ),
        in_specs=vmem(4) + [pl.BlockSpec(memory_space=pltpu.HBM)] * 2,
        out_specs=tuple([pl.BlockSpec(memory_space=pltpu.HBM)] + vmem(3)),
        scratch_shapes=[
            pltpu.VMEM((FIELDS, 2, span, 128), F32),
            pltpu.VMEM((10, span, 256), F32),
            pltpu.VMEM((2, span, 256), F32),
            pltpu.VMEM((3, 2, span, 256), F32),
            pltpu.VMEM((2, 2, span, 128), F32),
            pltpu.VMEM(base_velocity.shape, F32),
            pltpu.VMEM(base_velocity.shape, F32),
            pltpu.SemaphoreType.DMA((1 + n_grp,)),
            pltpu.SemaphoreType.DMA,
        ],
        compiler_params=params,
        name="solve",
    )(ext, pix, odd, even, inputs[0], pltpu.with_memory_space_constraint(panels, pltpu.HBM))

    column = [probe_low]
    while len(column) < n_grp:
        swap = [(i, i ^ len(column)) for i in range(n_grp)]
        column += [lax.ppermute(block, "grp", swap) for block in column]
    sums, hessian_probe = pl.pallas_call(
        project_kernel,
        out_shape=(
            jax.ShapeDtypeStruct((panels.shape[0], 8, 128), F32),
            jax.ShapeDtypeStruct((rows, columns), F32),
        ),
        in_specs=vmem(1 + n_grp),
        out_specs=(pl.BlockSpec(memory_space=pltpu.VMEM), pl.BlockSpec(memory_space=pltpu.HBM)),
        scratch_shapes=[pltpu.SemaphoreType.DMA],
        compiler_params=params,
        cost_estimate=pl.CostEstimate(
            flops=2 * panels.size * (n_grp - 1) // n_grp, bytes_accessed=2 * panels.size, transcendentals=0
        ),
        name="project",
    )(panels_near, hess, *column[:-1])
    partial = pl.pallas_call(
        project_last_kernel,
        out_shape=jax.ShapeDtypeStruct((n_grp * n_tile, 1, 128), F32),
        in_specs=vmem(3),
        out_specs=pl.BlockSpec(memory_space=pltpu.VMEM),
        compiler_params=params,
        name="project_last",
    )(panels_near, column[-1], sums)
    everyone = lax.all_to_all(partial, ("grp", "tile"), split_axis=0, concat_axis=0, tiled=True)
    coefficients = pl.pallas_call(
        add_lines_kernel,
        out_shape=jax.ShapeDtypeStruct((1, 128), F32),
        in_specs=vmem(1),
        out_specs=pl.BlockSpec(memory_space=pltpu.VMEM),
        compiler_params=params,
        name="add_lines",
    )(everyone)
    return increment, hessian_probe, coefficients.reshape(128)


def solution(mesh):
    in_specs = (
        P(None, "grp", "tile"),
        P("grp", "tile"),
        P("grp", "tile"),
        P("grp", "tile"),
        P("grp", "tile", None, None),
        P("grp", "tile", None, None),
        P("grp", "tile", None, None),
        P("grp", "tile", None, None),
        P("grp", None, "tile"),
    )
    out_specs = (P(None, "grp", "tile"), P("grp", "tile"), P())
    return jax.shard_map(
        on_device, mesh=mesh, in_specs=in_specs, out_specs=out_specs, check_vma=False
    )
```

```python
import functools

import jax
import jax.numpy as jnp
from jax import lax
from jax.experimental import pallas as pl
from jax.experimental.pallas import tpu as pltpu
from jax.sharding import PartitionSpec as P

SWEEPS = 8
RELAX = 0.8
CAP = 64
HALO = 16
EDGE = 8
FIELDS = 4
STRIPS = 8
F32 = jnp.float32
BF16 = jnp.bfloat16


def lanes(shape=(8, 128)):
    return lax.broadcasted_iota(jnp.int32, shape, len(shape) - 1)


def fetch(sources, targets, sems):
    copies = [pltpu.make_async_copy(s, d, sems.at[i]) for i, (s, d) in enumerate(zip(sources, targets))]
    for copy in copies:
        copy.start()
    return copies


def pack_tiles_kernel(n_tile, *refs):
    sources, (out_ref, fields_ref), targets, sems = refs[:8], refs[8:10], refs[10:18], refs[18]
    copies = fetch(sources, targets, sems)
    bv_ref, visc_ref, fric_ref, fp_ref, los_ref, weight_ref, cell_ref, count_ref = targets
    t = lax.axis_index("tile")
    parity = lax.rem(t, 2)
    rows = visc_ref.shape[0]
    half = rows // 2
    for copy in copies[4:]:
        copy.wait()
    row_lane = lanes((1, 128))
    low = lanes() < CAP
    straight, turned = [], []
    for j in range(n_tile // 2):
        at = pl.ds(j * 128, 128)
        count = jnp.where(
            row_lane < CAP, count_ref[0, 0, :, 2 * j : 2 * j + 1], count_ref[0, 0, :, 2 * j + 1 : 2 * j + 2]
        )
        live = (row_lane & (CAP - 1)) < count
        weight = jnp.where(live, weight_ref[0, 0, :, at], 0.0)
        scaled = jnp.sqrt(weight) * los_ref[0, 0, :, at]
        high = scaled.astype(BF16).astype(F32)
        cell = cell_ref[0, 0, :, at]
        block = jnp.concatenate(
            [
                high, scaled - high,
                lax.shift_right_logical(cell, 7).astype(F32), (cell & 127).astype(F32), jnp.zeros((2, 128), F32),
            ],
            axis=0,
        )
        straight.append(block)
        turned.append(pltpu.roll(block, CAP, 1))
    nothing = jnp.zeros((8, 128), F32)
    in_half = (lanes() // CAP) == parity

    def placed(owner, side):
        if owner < 0 or owner >= n_tile:
            return nothing
        return (straight if owner % 2 == side else turned)[owner // 2]

    for d in range(n_tile):
        solo = jnp.where(parity == d % 2, straight[d // 2], turned[d // 2])
        solo = jnp.where(in_half, solo, 0.0)
        pair = jnp.where(low, placed(d - 1, 0), placed(d + 1, 1))
        out_ref[d, half : half + 16, :] = jnp.concatenate([solo, pair], axis=0).astype(BF16)

    for copy in copies[:4]:
        copy.wait()
    probe = fp_ref[...]
    fields = [-(probe * bv_ref[0]), -(probe * bv_ref[1]), visc_ref[...], fric_ref[...]]
    for f, field in enumerate(fields):
        fields_ref[f] = field
    lane = lanes((half, 128))

    def fold(first_lane):
        packed = jnp.zeros((half, 128), F32)
        for part in range(2):
            for f, field in enumerate(fields):
                start = part * 64 + f * HALO
                piece = field[part * half : (part + 1) * half]
                piece = pltpu.roll(piece, (start - first_lane) % 128, 1)
                packed = jnp.where((lane >= start) & (lane < start + HALO), piece, packed)
        return packed

    @pl.when(t < n_tile - 1)
    def _():
        out_ref[t + 1, 0:half, :] = fold(128 - HALO).astype(BF16)

    @pl.when(t > 0)
    def _():
        out_ref[t - 1, 0:half, :] = fold(0).astype(BF16)


def pack_rows_kernel(n_tile, fields_ref, got_ref, ext_ref, pix_ref, even_ref, odd_ref):
    g = lax.axis_index("grp")
    t = lax.axis_index("tile")
    rows = fields_ref.shape[1]
    half = rows // 2
    fields = [fields_ref[f] for f in range(FIELDS)]
    lane = lanes((half, 128))
    right = jnp.where(t < n_tile - 1, got_ref[jnp.minimum(t + 1, n_tile - 1), 0:half, :].astype(F32), 0.0)
    left = jnp.where(t > 0, got_ref[jnp.maximum(t - 1, 0), 0:half, :].astype(F32), 0.0)
    band = lanes((HALO, 128))
    edge_up = jnp.zeros((HALO, 128), F32)
    edge_down = jnp.zeros((HALO, 128), F32)
    for f, field in enumerate(fields):
        ext_ref[f, :, 0:128] = field
        edges = []
        for part in range(2):
            start = part * 64 + f * HALO
            edge = jnp.where(
                lane < HALO,
                pltpu.roll(right, (0 - start) % 128, 1),
                jnp.where(lane >= 128 - HALO, pltpu.roll(left, (128 - HALO - start) % 128, 1), 0.0),
            )
            ext_ref[f, part * half : (part + 1) * half, 128:256] = edge
            edges.append(edge)
        here = (band >= 2 * f * HALO) & (band < 2 * (f + 1) * HALO)
        turn = (2 * f + 1) * HALO % 128
        edge_up = jnp.where(here, pltpu.roll(edges[0][0:HALO], turn, 1), edge_up)
        edge_down = jnp.where(here, pltpu.roll(edges[1][half - HALO :], turn, 1), edge_down)
    low = lanes() < CAP
    near, far = [], []
    for s in range(0, n_tile, 2):
        one = got_ref[s, half : half + 16, :].astype(F32)
        two = got_ref[s + 1, half : half + 16, :].astype(F32)
        near.append(jnp.where(low, one[0:8], two[0:8]))
        far += [one[8:16], two[8:16]]
    blocks = near + far
    pixels = jnp.concatenate(
        [b[0:1] + b[2:3] for b in blocks]
        + [b[1:2] + b[3:4] for b in blocks]
        + [b[4:5] for b in blocks]
        + [b[5:6] for b in blocks],
        axis=0,
    )
    pix_ref[...] = pixels
    pixels = pixels.astype(BF16)

    even = lax.rem(g, 2) == 0

    def choose(one, two):
        even_ref_value, odd_ref_value = jnp.where(even, one, two), jnp.where(even, two, one)
        return even_ref_value.astype(BF16), odd_ref_value.astype(BF16)

    for f, field in enumerate(fields):
        at = pl.ds(f * HALO, HALO)
        even_ref[at, :], odd_ref[at, :] = choose(field[rows - HALO :], field[0:HALO])
    at = pl.ds(FIELDS * HALO, HALO)
    even_ref[at, :], odd_ref[at, :] = choose(edge_down, edge_up)
    for ref in (even_ref, odd_ref):
        ref[(FIELDS + 1) * HALO :, :] = pixels


def solve_kernel(
    n_grp, n_tile, ext_ref, pix_ref, odd_ref, even_ref, bv_hbm, panels_hbm,
    inc_hbm, hess_ref, low_ref, panels_ref,
    plane_ref, coef_ref, src_ref, w_ref, nat_ref, bv_ref, inc_ref, sems, inc_sem,
):
    size = panels_ref.shape[2]
    copies = fetch(
        [bv_hbm] + [panels_hbm.at[:, pl.ds(i * size, size), :] for i in range(n_grp)],
        [bv_ref] + [panels_ref.at[:, i] for i in range(n_grp)],
        sems,
    )
    g = lax.axis_index("grp")
    t = lax.axis_index("tile")
    rows = ext_ref.shape[1]
    span = rows + 2 * HALO
    groups = span // STRIPS
    lane = lanes()

    even = lax.rem(g, 2) == 0

    def above(first, size):
        at = pl.ds(first, size)
        got = jnp.where(even, odd_ref[at, :].astype(F32), even_ref[at, :].astype(F32))
        return jnp.where(g > 0, got, 0.0)

    def below(first, size):
        at = pl.ds(first, size)
        got = jnp.where(even, even_ref[at, :].astype(F32), odd_ref[at, :].astype(F32))
        return jnp.where(g < n_grp - 1, got, 0.0)

    first_lane = lane == 0
    last_lane = lane == 127

    band = lanes((HALO, 128))
    for f in range(FIELDS):
        for h in range(2):
            plane_ref[f, h, HALO : HALO + rows, :] = ext_ref[f, :, h * 128 : (h + 1) * 128]
        for load, at in ((above, 0), (below, HALO + rows)):
            plane_ref[f, 0, at : at + HALO, :] = load(f * HALO, HALO)
            edge = pltpu.roll(load(FIELDS * HALO, HALO), (0 - (2 * f + 1) * HALO) % 128, 1)
            plane_ref[f, 1, at : at + HALO, :] = jnp.where((band < HALO) | (band >= 128 - HALO), edge, 0.0)

    def strided(f, h, v):
        return plane_ref[f, h, pl.ds(v, STRIPS, stride=groups), :]

    def beside(pair):
        a, b = pair
        ra, rb = pltpu.roll(a, 1, 1), pltpu.roll(b, 1, 1)
        before = (jnp.where(first_lane, rb, ra), jnp.where(first_lane, ra, rb))
        ra, rb = pltpu.roll(a, 127, 1), pltpu.roll(b, 127, 1)
        after = (jnp.where(last_lane, rb, ra), jnp.where(last_lane, ra, rb))
        return before, pair, after

    def row(load, v):
        if v < 0:
            return beside(tuple(pltpu.roll(load(h, groups - 1), 1, 0) for h in range(2)))
        if v == groups:
            return beside(tuple(pltpu.roll(load(h, 0), STRIPS - 1, 0) for h in range(2)))
        return beside(tuple(load(h, v) for h in range(2)))

    strip = lax.broadcasted_iota(jnp.int32, (8, 128), 0)
    col_in = [
        None,
        ((lane < HALO) & (t < n_tile - 1)) | ((lane >= 128 - HALO) & (t > 0)),
    ]
    load_visc = functools.partial(strided, 2)
    prev, cur = row(load_visc, -1), row(load_visc, 0)
    for v in range(groups):
        nxt = row(load_visc, v + 1)
        place = g * rows - HALO + strip * groups + v
        row_in = (place >= 0) & (place < n_grp * rows)
        at = pl.ds(v * 8, 8)
        for h in range(2):
            centre = cur[1][h]
            east = 0.5 * (centre + nxt[1][h])
            west = 0.5 * (centre + prev[1][h])
            north = 0.5 * (centre + cur[2][h])
            south = 0.5 * (centre + cur[0][h])
            node_pp = 0.25 * (centre + nxt[1][h] + cur[2][h] + nxt[2][h])
            node_mm = 0.25 * (centre + prev[1][h] + cur[0][h] + prev[0][h])
            node_pm = 0.25 * (centre + nxt[1][h] + cur[0][h] + nxt[0][h])
            node_mp = 0.25 * (centre + prev[1][h] + cur[2][h] + prev[2][h])
            fric = strided(3, h, v)
            diag_x = fric + 2.0 * (east + west) + (north + south)
            diag_y = fric + (east + west) + 2.0 * (north + south)
            inside = row_in if col_in[h] is None else row_in & col_in[h]
            inv_x = jnp.where(inside, RELAX / jnp.where(inside, diag_x, 1.0), 0.0)
            inv_y = jnp.where(inside, RELAX / jnp.where(inside, diag_y, 1.0), 0.0)
            cols = pl.ds(h * 128, 128)
            for i, plane in enumerate(
                (east, west, north, south, 0.25 * node_pp, 0.25 * node_mm, 0.25 * node_pm, 0.25 * node_mp, inv_x, inv_y)
            ):
                coef_ref[i, at, cols] = plane
            src_ref[0, at, cols] = inv_x * strided(0, h, v)
            src_ref[1, at, cols] = inv_y * strided(1, h, v)
        prev, cur = cur, nxt

    def natural(h, v):
        return (h, pl.ds(v, STRIPS, stride=groups), slice(None))

    def relax():
        w_ref[0] = src_ref[...]

        def sweep(now, later, start):
            rows_seen = {}

            def both(v):
                if v not in rows_seen:
                    rows_seen[v] = tuple(
                        row(lambda h, u, c=c: now[c, pl.ds(u * 8, 8), pl.ds(h * 128, 128)], v) for c in range(2)
                    )
                return rows_seen[v]

            for p in range(groups):
                v = (p + start) % groups
                prev, cur, nxt = both(v - 1), both(v), both(v + 1)
                at = pl.ds(v * 8, 8)
                for h in range(2):
                    cols = pl.ds(h * 128, 128)
                    east, west, north, south, pp, mm, pm, mp, inv_x, inv_y = (
                        coef_ref[i, at, cols] for i in range(10)
                    )

                    def along(c):
                        return (
                            east * nxt[c][1][h] + west * prev[c][1][h],
                            north * cur[c][2][h] + south * cur[c][0][h],
                        )

                    def cross(c):
                        return (
                            pp * nxt[c][2][h] + mm * prev[c][0][h] - pm * nxt[c][0][h] - mp * prev[c][2][h]
                        )

                    one, two = along(0)
                    sum_x = 2.0 * one + two + cross(1)
                    one, two = along(1)
                    sum_y = one + 2.0 * two + cross(0)
                    for c, new in ((0, inv_x * sum_x), (1, inv_y * sum_y)):
                        new = (1.0 - RELAX) * cur[c][1][h] + src_ref[c, at, cols] + new
                        if later is None:
                            nat_ref[(c,) + natural(h, v)] = new
                        else:
                            later[c, at, cols] = new

        def three_sweeps(_, carry):
            for k in range(3):
                sweep(w_ref.at[k], w_ref.at[(k + 1) % 3], k)
            return carry

        lax.fori_loop(0, (SWEEPS - 2) // 3, three_sweeps, 0)
        sweep(w_ref.at[0], None, 0)

    def solve(phase, carry):
        relax()

        @pl.when(phase == 0)
        def _():
            for c in range(2):
                inc_ref[c] = nat_ref[c, 0, HALO : HALO + rows, :]
            pltpu.make_async_copy(inc_ref, inc_hbm, inc_sem).start()
            misfit()

        return carry

    def misfit():
        n_near, n_all = n_tile // 2, 3 * n_tile // 2
        low = lanes((n_tile, 128)) < CAP
        spans = ((0, HALO, rows), (-1, HALO - EDGE, EDGE), (1, HALO + rows, EDGE))

        def exact(h, delta):
            return h == 0 and delta == 0

        jobs = []
        for delta, first, size in spans:
            if delta == 0:
                values = pix_ref[...]
            else:
                base = (FIELDS + 1) * HALO
                values = (above if delta < 0 else below)(base, 4 * n_all)
            los_x, los_y, r, c = (values[q * n_all : (q + 1) * n_all] for q in range(4))
            if delta < 0:
                r = r - (rows - EDGE)
            in_rim = c[n_near:] + jnp.where(low, float(EDGE) - 128.0, float(EDGE))
            for h, begin, count, lane_of in ((0, 0, n_near, c[0:n_near]), (1, n_near, n_tile, in_rim)):
                parts = []
                for comp in range(2):
                    part = nat_ref[comp, h, first : first + size, :]
                    parts.append(part if h == 0 else pltpu.roll(part, EDGE, 1))
                field = jnp.concatenate(parts, axis=0)
                stacked = field.astype(BF16)
                if exact(h, delta):
                    rest = (field - stacked.astype(F32)).astype(BF16)
                    stacked = jnp.concatenate([stacked, rest], axis=1)
                jobs.append((exact(h, delta), h, first, size, begin, count, lane_of, los_x, los_y, r, stacked))

        nat_ref[...] = jnp.zeros_like(nat_ref)
        for two_parts, h, first, size, begin, count, lane_of, los_x, los_y, r, stacked in jobs:
            chunk = 4 if h == 0 else 8
            depth = 128 if h == 0 else 2 * EDGE
            wide = chunk * 128
            row_id = lax.broadcasted_iota(jnp.int32, (size, wide), 0).astype(F32)
            lane_id = lax.broadcasted_iota(jnp.int32, (depth, wide), 0).astype(F32)
            total = jnp.zeros(((4 if two_parts else 2) * size, 128), F32)
            for j in range(0, count, chunk):

                def line(table, offset):
                    return jnp.concatenate([table[offset + i : offset + i + 1] for i in range(j, j + chunk)], axis=1)

                line_x, line_y = line(los_x, begin), line(los_y, begin)
                hot = jnp.where(lane_id == line(lane_of, 0), 1.0, 0.0).astype(BF16)
                here = row_id == line(r, begin)
                if h == 1:
                    hot = jnp.concatenate([hot, jnp.zeros((128 - depth, wide), BF16)], axis=0)
                twice = jnp.concatenate([hot, hot], axis=0) if two_parts else hot
                got = jnp.dot(stacked, twice, preferred_element_type=F32)
                got_x = jnp.sum(jnp.where(here, got[0:size], 0.0), axis=0, keepdims=True)
                got_y = jnp.sum(jnp.where(here, got[size:], 0.0), axis=0, keepdims=True)
                amount = line_x * got_x + line_y * got_y
                terms = [amount * line_x, amount * line_y]
                if two_parts:
                    highs = [p.astype(BF16).astype(F32) for p in terms]
                    terms = highs + [p - q for p, q in zip(terms, highs)]
                spread = jnp.concatenate([jnp.where(here, p, 0.0) for p in terms], axis=0).astype(BF16)
                total = total + lax.dot_general(spread, hot, (((1,), (1,)), ((), ())), preferred_element_type=F32)
            if two_parts:
                total = total[0 : 2 * size] + total[2 * size :]
            if h == 1:
                total = pltpu.roll(total, 128 - EDGE, 1)
            for c in range(2):
                nat_ref[c, h, first : first + size, :] = total[c * size : (c + 1) * size]

        for v in range(groups):
            at = pl.ds(v * 8, 8)
            for h in range(2):
                cols = pl.ds(h * 128, 128)
                for c in range(2):
                    src_ref[c, at, cols] = coef_ref[8 + c, at, cols] * nat_ref[(c,) + natural(h, v)]

    lax.fori_loop(0, 2, solve, 0)
    for copy in copies:
        copy.wait()
    pltpu.make_async_copy(inc_ref, inc_hbm, inc_sem).wait()
    hess = -(bv_ref[0] * nat_ref[0, 0, HALO : HALO + rows, :] + bv_ref[1] * nat_ref[1, 0, HALO : HALO + rows, :])
    hess_ref[...] = hess
    low_ref[...] = hess.astype(BF16)


def distances(n_grp):
    return [0] + list(range(2, n_grp)) + [1]


def project_block(panels_ref, probe_ref, k, distance):
    count, n_grp, rows, columns = panels_ref.shape
    product = panels_ref[k, lax.axis_index("grp") ^ distance].astype(F32) * probe_ref[...].astype(F32)
    return jnp.sum(product.reshape(-1, 8, columns), axis=0)


def project_kernel(panels_ref, hess_ref, *refs):
    blocks, (sums_ref, hess_hbm, sem) = refs[:-3], refs[-3:]
    copy = pltpu.make_async_copy(hess_ref, hess_hbm, sem)
    copy.start()
    order = distances(panels_ref.shape[1])
    for k in range(panels_ref.shape[0]):
        sums_ref[k] = sum(project_block(panels_ref, block, k, i) for i, block in zip(order, blocks))
    copy.wait()


def project_last_kernel(panels_ref, block_ref, sums_ref, out_ref):
    count, n_grp = panels_ref.shape[:2]
    sums = []
    for k in range(count):
        total = sums_ref[k] + project_block(panels_ref, block_ref, k, distances(n_grp)[-1])
        sums.append(jnp.sum(total, axis=0, keepdims=True))
    sums.append(jnp.zeros((128 - count, 128), F32))
    table = jnp.concatenate(sums, axis=0)
    high = table.astype(BF16)
    parts = jnp.concatenate([high, (table - high.astype(F32)).astype(BF16)], axis=1)
    line = lax.dot_general(
        jnp.ones((16, 256), BF16), parts, (((1,), (1,)), ((), ())), preferred_element_type=F32
    )
    line = pltpu.roll(line, lax.axis_index("grp") * count, 1)[0:1]
    out_ref[...] = jnp.broadcast_to(line[None], out_ref.shape)


def add_lines_kernel(lines_ref, out_ref):
    out_ref[...] = jnp.sum(lines_ref[...], axis=0)


def vmem(n):
    return [pl.BlockSpec(memory_space=pltpu.VMEM)] * n


def on_device(
    base_velocity, viscosity, friction, friction_probe, pixel_los, pixel_weight, pixel_cell, pixel_count, panels
):
    n_grp, n_tile = lax.axis_size("grp"), lax.axis_size("tile")
    rows, columns = viscosity.shape
    half = rows // 2
    span = rows + 2 * HALO
    params = pltpu.CompilerParams(vmem_limit_bytes=32 * 2**20)

    inputs = [
        pltpu.with_memory_space_constraint(x, pltpu.HBM)
        for x in (
            base_velocity, viscosity, friction, friction_probe, pixel_los, pixel_weight, pixel_cell, pixel_count
        )
    ]
    slots, fields = pl.pallas_call(
        functools.partial(pack_tiles_kernel, n_tile),
        out_shape=(
            jax.ShapeDtypeStruct((n_tile, half + 16, 128), BF16),
            jax.ShapeDtypeStruct((FIELDS, rows, columns), F32),
        ),
        in_specs=[pl.BlockSpec(memory_space=pltpu.HBM)] * len(inputs),
        out_specs=tuple(vmem(2)),
        scratch_shapes=[pltpu.VMEM(x.shape, x.dtype) for x in inputs] + [pltpu.SemaphoreType.DMA((len(inputs),))],
        compiler_params=params,
        name="pack_tiles",
    )(*inputs)
    got = lax.all_to_all(slots, "tile", split_axis=0, concat_axis=0, tiled=True)

    packet = (FIELDS + 1) * HALO + 6 * n_tile
    ext, pix, even, odd = pl.pallas_call(
        functools.partial(pack_rows_kernel, n_tile),
        out_shape=(
            jax.ShapeDtypeStruct((FIELDS, rows, 256), F32),
            jax.ShapeDtypeStruct((6 * n_tile, 128), F32),
            jax.ShapeDtypeStruct((packet, 128), BF16),
            jax.ShapeDtypeStruct((packet, 128), BF16),
        ),
        in_specs=vmem(2),
        out_specs=tuple(vmem(4)),
        compiler_params=params,
        name="pack_rows",
    )(fields, got)
    even = lax.ppermute(even, "grp", [(i, i ^ 1) for i in range(n_grp)])
    odd = lax.ppermute(odd, "grp", [(i, (i - 1 + 2 * (i % 2)) % n_grp) for i in range(n_grp)])

    increment, hess, probe_low, panels_near = pl.pallas_call(
        functools.partial(solve_kernel, n_grp, n_tile),
        out_shape=(
            jax.ShapeDtypeStruct((2, rows, columns), F32),
            jax.ShapeDtypeStruct((rows, columns), F32),
            jax.ShapeDtypeStruct((rows, columns), BF16),
            jax.ShapeDtypeStruct((panels.shape[0], n_grp, rows, columns), BF16),
        ),
        in_specs=vmem(4) + [pl.BlockSpec(memory_space=pltpu.HBM)] * 2,
        out_specs=tuple([pl.BlockSpec(memory_space=pltpu.HBM)] + vmem(3)),
        scratch_shapes=[
            pltpu.VMEM((FIELDS, 2, span, 128), F32),
            pltpu.VMEM((10, span, 256), F32),
            pltpu.VMEM((2, span, 256), F32),
            pltpu.VMEM((3, 2, span, 256), F32),
            pltpu.VMEM((2, 2, span, 128), F32),
            pltpu.VMEM(base_velocity.shape, F32),
            pltpu.VMEM(base_velocity.shape, F32),
            pltpu.SemaphoreType.DMA((1 + n_grp,)),
            pltpu.SemaphoreType.DMA,
        ],
        compiler_params=params,
        name="solve",
    )(ext, pix, odd, even, inputs[0], pltpu.with_memory_space_constraint(panels, pltpu.HBM))

    column = [probe_low] + [
        lax.ppermute(probe_low, "grp", [(i, i ^ k) for i in range(n_grp)]) for k in distances(n_grp)[1:]
    ]
    sums, hessian_probe = pl.pallas_call(
        project_kernel,
        out_shape=(
            jax.ShapeDtypeStruct((panels.shape[0], 8, 128), F32),
            jax.ShapeDtypeStruct((rows, columns), F32),
        ),
        in_specs=vmem(1 + n_grp),
        out_specs=(pl.BlockSpec(memory_space=pltpu.VMEM), pl.BlockSpec(memory_space=pltpu.HBM)),
        scratch_shapes=[pltpu.SemaphoreType.DMA],
        compiler_params=params,
        cost_estimate=pl.CostEstimate(
            flops=2 * panels.size * (n_grp - 1) // n_grp, bytes_accessed=2 * panels.size, transcendentals=0
        ),
        name="project",
    )(panels_near, hess, *column[:-1])
    partial = pl.pallas_call(
        project_last_kernel,
        out_shape=jax.ShapeDtypeStruct((n_grp * n_tile, 1, 128), F32),
        in_specs=vmem(3),
        out_specs=pl.BlockSpec(memory_space=pltpu.VMEM),
        compiler_params=params,
        name="project_last",
    )(panels_near, column[-1], sums)
    everyone = lax.all_to_all(partial, ("grp", "tile"), split_axis=0, concat_axis=0, tiled=True)
    coefficients = pl.pallas_call(
        add_lines_kernel,
        out_shape=jax.ShapeDtypeStruct((1, 128), F32),
        in_specs=vmem(1),
        out_specs=pl.BlockSpec(memory_space=pltpu.VMEM),
        compiler_params=params,
        name="add_lines",
    )(everyone)
    return increment, hessian_probe, coefficients.reshape(128)


def solution(mesh):
    in_specs = (
        P(None, "grp", "tile"),
        P("grp", "tile"),
        P("grp", "tile"),
        P("grp", "tile"),
        P("grp", "tile", None, None),
        P("grp", "tile", None, None),
        P("grp", "tile", None, None),
        P("grp", "tile", None, None),
        P("grp", None, "tile"),
    )
    out_specs = (P(None, "grp", "tile"), P("grp", "tile"), P())
    return jax.shard_map(
        on_device, mesh=mesh, in_specs=in_specs, out_specs=out_specs, check_vma=False
    )
```

```python
import functools

import jax
import jax.numpy as jnp
from jax import lax
from jax.experimental import pallas as pl
from jax.experimental.pallas import tpu as pltpu
from jax.sharding import PartitionSpec as P

SWEEPS = 8
RELAX = 0.8
CAP = 64
HALO = 16
EDGE = 8
FIELDS = 4
STRIPS = 8
F32 = jnp.float32
BF16 = jnp.bfloat16


def lanes(shape=(8, 128)):
    return lax.broadcasted_iota(jnp.int32, shape, len(shape) - 1)


def fetch(sources, targets, sems):
    copies = [pltpu.make_async_copy(s, d, sems.at[i]) for i, (s, d) in enumerate(zip(sources, targets))]
    for copy in copies:
        copy.start()
    return copies


def pack_tiles_kernel(n_tile, *refs):
    sources, (out_ref, fields_ref), targets, sems = refs[:8], refs[8:10], refs[10:18], refs[18]
    copies = fetch(sources, targets, sems)
    bv_ref, visc_ref, fric_ref, fp_ref, los_ref, weight_ref, cell_ref, count_ref = targets
    t = lax.axis_index("tile")
    parity = lax.rem(t, 2)
    rows = visc_ref.shape[0]
    half = rows // 2
    for copy in copies[4:]:
        copy.wait()
    row_lane = lanes((1, 128))
    low = lanes() < CAP
    straight, turned = [], []
    for j in range(n_tile // 2):
        at = pl.ds(j * 128, 128)
        count = jnp.where(
            row_lane < CAP, count_ref[0, 0, :, 2 * j : 2 * j + 1], count_ref[0, 0, :, 2 * j + 1 : 2 * j + 2]
        )
        live = (row_lane & (CAP - 1)) < count
        weight = jnp.where(live, weight_ref[0, 0, :, at], 0.0)
        scaled = jnp.sqrt(weight) * los_ref[0, 0, :, at]
        high = scaled.astype(BF16).astype(F32)
        cell = cell_ref[0, 0, :, at]
        block = jnp.concatenate(
            [
                high, scaled - high,
                lax.shift_right_logical(cell, 7).astype(F32), (cell & 127).astype(F32), jnp.zeros((2, 128), F32),
            ],
            axis=0,
        )
        straight.append(block)
        turned.append(pltpu.roll(block, CAP, 1))
    nothing = jnp.zeros((8, 128), F32)
    in_half = (lanes() // CAP) == parity

    def placed(owner, side):
        if owner < 0 or owner >= n_tile:
            return nothing
        return (straight if owner % 2 == side else turned)[owner // 2]

    for d in range(n_tile):
        solo = jnp.where(parity == d % 2, straight[d // 2], turned[d // 2])
        solo = jnp.where(in_half, solo, 0.0)
        pair = jnp.where(low, placed(d - 1, 0), placed(d + 1, 1))
        out_ref[d, half : half + 16, :] = jnp.concatenate([solo, pair], axis=0).astype(BF16)

    for copy in copies[:4]:
        copy.wait()
    probe = fp_ref[...]
    fields = [-(probe * bv_ref[0]), -(probe * bv_ref[1]), visc_ref[...], fric_ref[...]]
    for f, field in enumerate(fields):
        fields_ref[f] = field
    lane = lanes((half, 128))

    def fold(first_lane):
        packed = jnp.zeros((half, 128), F32)
        for part in range(2):
            for f, field in enumerate(fields):
                start = part * 64 + f * HALO
                piece = field[part * half : (part + 1) * half]
                piece = pltpu.roll(piece, (start - first_lane) % 128, 1)
                packed = jnp.where((lane >= start) & (lane < start + HALO), piece, packed)
        return packed

    @pl.when(t < n_tile - 1)
    def _():
        out_ref[t + 1, 0:half, :] = fold(128 - HALO).astype(BF16)

    @pl.when(t > 0)
    def _():
        out_ref[t - 1, 0:half, :] = fold(0).astype(BF16)


def pack_rows_kernel(n_tile, fields_ref, got_ref, ext_ref, pix_ref, up_ref, down_ref):
    t = lax.axis_index("tile")
    rows = fields_ref.shape[1]
    half = rows // 2
    fields = [fields_ref[f] for f in range(FIELDS)]
    lane = lanes((half, 128))
    right = jnp.where(t < n_tile - 1, got_ref[jnp.minimum(t + 1, n_tile - 1), 0:half, :].astype(F32), 0.0)
    left = jnp.where(t > 0, got_ref[jnp.maximum(t - 1, 0), 0:half, :].astype(F32), 0.0)
    band = lanes((HALO, 128))
    edge_up = jnp.zeros((HALO, 128), F32)
    edge_down = jnp.zeros((HALO, 128), F32)
    for f, field in enumerate(fields):
        ext_ref[f, :, 0:128] = field
        edges = []
        for part in range(2):
            start = part * 64 + f * HALO
            edge = jnp.where(
                lane < HALO,
                pltpu.roll(right, (0 - start) % 128, 1),
                jnp.where(lane >= 128 - HALO, pltpu.roll(left, (128 - HALO - start) % 128, 1), 0.0),
            )
            ext_ref[f, part * half : (part + 1) * half, 128:256] = edge
            edges.append(edge)
        here = (band >= 2 * f * HALO) & (band < 2 * (f + 1) * HALO)
        turn = (2 * f + 1) * HALO % 128
        edge_up = jnp.where(here, pltpu.roll(edges[0][0:HALO], turn, 1), edge_up)
        edge_down = jnp.where(here, pltpu.roll(edges[1][half - HALO :], turn, 1), edge_down)
    low = lanes() < CAP
    near, far = [], []
    for s in range(0, n_tile, 2):
        one = got_ref[s, half : half + 16, :].astype(F32)
        two = got_ref[s + 1, half : half + 16, :].astype(F32)
        near.append(jnp.where(low, one[0:8], two[0:8]))
        far += [one[8:16], two[8:16]]
    blocks = near + far
    pixels = jnp.concatenate(
        [b[0:1] + b[2:3] for b in blocks]
        + [b[1:2] + b[3:4] for b in blocks]
        + [b[4:5] for b in blocks]
        + [b[5:6] for b in blocks],
        axis=0,
    )
    pix_ref[...] = pixels
    pixels = pixels.astype(BF16)

    for ref, first, edge in ((up_ref, 0, edge_up), (down_ref, rows - HALO, edge_down)):
        for f, field in enumerate(fields):
            ref[f * HALO : (f + 1) * HALO, :] = field[first : first + HALO].astype(BF16)
        base = FIELDS * HALO
        ref[base : base + HALO, :] = edge.astype(BF16)
        ref[base + HALO :, :] = pixels


def solve_kernel(
    n_grp, n_tile, ext_ref, pix_ref, above_ref, below_ref, bv_hbm, panels_hbm,
    inc_hbm, hess_ref, low_ref, panels_ref,
    plane_ref, coef_ref, src_ref, w_ref, nat_ref, bv_ref, inc_ref, sems, inc_sem,
):
    size = panels_ref.shape[2]
    copies = fetch(
        [bv_hbm] + [panels_hbm.at[:, pl.ds(i * size, size), :] for i in range(n_grp)],
        [bv_ref] + [panels_ref.at[:, i] for i in range(n_grp)],
        sems,
    )
    g = lax.axis_index("grp")
    t = lax.axis_index("tile")
    rows = ext_ref.shape[1]
    span = rows + 2 * HALO
    groups = span // STRIPS
    lane = lanes()

    def above(first, size):
        return jnp.where(g > 0, above_ref[first : first + size, :].astype(F32), 0.0)

    def below(first, size):
        return jnp.where(g < n_grp - 1, below_ref[first : first + size, :].astype(F32), 0.0)

    first_lane = lane == 0
    last_lane = lane == 127

    band = lanes((HALO, 128))
    for f in range(FIELDS):
        for h in range(2):
            plane_ref[f, h, HALO : HALO + rows, :] = ext_ref[f, :, h * 128 : (h + 1) * 128]
        for load, at in ((above, 0), (below, HALO + rows)):
            plane_ref[f, 0, at : at + HALO, :] = load(f * HALO, HALO)
            edge = pltpu.roll(load(FIELDS * HALO, HALO), (0 - (2 * f + 1) * HALO) % 128, 1)
            plane_ref[f, 1, at : at + HALO, :] = jnp.where((band < HALO) | (band >= 128 - HALO), edge, 0.0)

    def strided(f, h, v):
        return plane_ref[f, h, pl.ds(v, STRIPS, stride=groups), :]

    def beside(pair):
        a, b = pair
        ra, rb = pltpu.roll(a, 1, 1), pltpu.roll(b, 1, 1)
        before = (jnp.where(first_lane, rb, ra), jnp.where(first_lane, ra, rb))
        ra, rb = pltpu.roll(a, 127, 1), pltpu.roll(b, 127, 1)
        after = (jnp.where(last_lane, rb, ra), jnp.where(last_lane, ra, rb))
        return before, pair, after

    def row(load, v):
        if v < 0:
            return beside(tuple(pltpu.roll(load(h, groups - 1), 1, 0) for h in range(2)))
        if v == groups:
            return beside(tuple(pltpu.roll(load(h, 0), STRIPS - 1, 0) for h in range(2)))
        return beside(tuple(load(h, v) for h in range(2)))

    strip = lax.broadcasted_iota(jnp.int32, (8, 128), 0)
    col_in = [
        None,
        ((lane < HALO) & (t < n_tile - 1)) | ((lane >= 128 - HALO) & (t > 0)),
    ]
    load_visc = functools.partial(strided, 2)
    prev, cur = row(load_visc, -1), row(load_visc, 0)
    for v in range(groups):
        nxt = row(load_visc, v + 1)
        place = g * rows - HALO + strip * groups + v
        row_in = (place >= 0) & (place < n_grp * rows)
        at = pl.ds(v * 8, 8)
        for h in range(2):
            centre = cur[1][h]
            east = 0.5 * (centre + nxt[1][h])
            west = 0.5 * (centre + prev[1][h])
            north = 0.5 * (centre + cur[2][h])
            south = 0.5 * (centre + cur[0][h])
            node_pp = 0.25 * (centre + nxt[1][h] + cur[2][h] + nxt[2][h])
            node_mm = 0.25 * (centre + prev[1][h] + cur[0][h] + prev[0][h])
            node_pm = 0.25 * (centre + nxt[1][h] + cur[0][h] + nxt[0][h])
            node_mp = 0.25 * (centre + prev[1][h] + cur[2][h] + prev[2][h])
            fric = strided(3, h, v)
            diag_x = fric + 2.0 * (east + west) + (north + south)
            diag_y = fric + (east + west) + 2.0 * (north + south)
            inside = row_in if col_in[h] is None else row_in & col_in[h]
            inv_x = jnp.where(inside, RELAX / jnp.where(inside, diag_x, 1.0), 0.0)
            inv_y = jnp.where(inside, RELAX / jnp.where(inside, diag_y, 1.0), 0.0)
            cols = pl.ds(h * 128, 128)
            for i, plane in enumerate(
                (east, west, north, south, 0.25 * node_pp, 0.25 * node_mm, 0.25 * node_pm, 0.25 * node_mp, inv_x, inv_y)
            ):
                coef_ref[i, at, cols] = plane
            src_ref[0, at, cols] = inv_x * strided(0, h, v)
            src_ref[1, at, cols] = inv_y * strided(1, h, v)
        prev, cur = cur, nxt

    def natural(h, v):
        return (h, pl.ds(v, STRIPS, stride=groups), slice(None))

    def relax():
        w_ref[0] = src_ref[...]

        def sweep(now, later, start):
            rows_seen = {}

            def both(v):
                if v not in rows_seen:
                    rows_seen[v] = tuple(
                        row(lambda h, u, c=c: now[c, pl.ds(u * 8, 8), pl.ds(h * 128, 128)], v) for c in range(2)
                    )
                return rows_seen[v]

            for p in range(groups):
                v = (p + start) % groups
                prev, cur, nxt = both(v - 1), both(v), both(v + 1)
                at = pl.ds(v * 8, 8)
                for h in range(2):
                    cols = pl.ds(h * 128, 128)
                    east, west, north, south, pp, mm, pm, mp, inv_x, inv_y = (
                        coef_ref[i, at, cols] for i in range(10)
                    )

                    def along(c):
                        return (
                            east * nxt[c][1][h] + west * prev[c][1][h],
                            north * cur[c][2][h] + south * cur[c][0][h],
                        )

                    def cross(c):
                        return (
                            pp * nxt[c][2][h] + mm * prev[c][0][h] - pm * nxt[c][0][h] - mp * prev[c][2][h]
                        )

                    one, two = along(0)
                    sum_x = 2.0 * one + two + cross(1)
                    one, two = along(1)
                    sum_y = one + 2.0 * two + cross(0)
                    for c, new in ((0, inv_x * sum_x), (1, inv_y * sum_y)):
                        new = (1.0 - RELAX) * cur[c][1][h] + src_ref[c, at, cols] + new
                        if later is None:
                            nat_ref[(c,) + natural(h, v)] = new
                        else:
                            later[c, at, cols] = new

        def three_sweeps(_, carry):
            for k in range(3):
                sweep(w_ref.at[k], w_ref.at[(k + 1) % 3], k)
            return carry

        lax.fori_loop(0, (SWEEPS - 2) // 3, three_sweeps, 0)
        sweep(w_ref.at[0], None, 0)

    def solve(phase, carry):
        relax()

        @pl.when(phase == 0)
        def _():
            for c in range(2):
                inc_ref[c] = nat_ref[c, 0, HALO : HALO + rows, :]
            pltpu.make_async_copy(inc_ref, inc_hbm, inc_sem).start()
            misfit()

        return carry

    def misfit():
        n_near, n_all = n_tile // 2, 3 * n_tile // 2
        low = lanes((n_tile, 128)) < CAP
        spans = ((0, HALO, rows), (-1, HALO - EDGE, EDGE), (1, HALO + rows, EDGE))

        def exact(h, delta):
            return h == 0 and delta == 0

        jobs = []
        for delta, first, size in spans:
            if delta == 0:
                values = pix_ref[...]
            else:
                base = (FIELDS + 1) * HALO
                values = (above if delta < 0 else below)(base, 4 * n_all)
            los_x, los_y, r, c = (values[q * n_all : (q + 1) * n_all] for q in range(4))
            if delta < 0:
                r = r - (rows - EDGE)
            in_rim = c[n_near:] + jnp.where(low, float(EDGE) - 128.0, float(EDGE))
            for h, begin, count, lane_of in ((0, 0, n_near, c[0:n_near]), (1, n_near, n_tile, in_rim)):
                parts = []
                for comp in range(2):
                    part = nat_ref[comp, h, first : first + size, :]
                    parts.append(part if h == 0 else pltpu.roll(part, EDGE, 1))
                field = jnp.concatenate(parts, axis=0)
                stacked = field.astype(BF16)
                if exact(h, delta):
                    rest = (field - stacked.astype(F32)).astype(BF16)
                    stacked = jnp.concatenate([stacked, rest], axis=1)
                jobs.append((exact(h, delta), h, first, size, begin, count, lane_of, los_x, los_y, r, stacked))

        nat_ref[...] = jnp.zeros_like(nat_ref)
        for two_parts, h, first, size, begin, count, lane_of, los_x, los_y, r, stacked in jobs:
            chunk = 4 if h == 0 else 8
            depth = 128 if h == 0 else 2 * EDGE
            wide = chunk * 128
            row_id = lax.broadcasted_iota(jnp.int32, (size, wide), 0).astype(F32)
            lane_id = lax.broadcasted_iota(jnp.int32, (depth, wide), 0).astype(F32)
            total = jnp.zeros(((4 if two_parts else 2) * size, 128), F32)
            for j in range(0, count, chunk):

                def line(table, offset):
                    return jnp.concatenate([table[offset + i : offset + i + 1] for i in range(j, j + chunk)], axis=1)

                line_x, line_y = line(los_x, begin), line(los_y, begin)
                hot = jnp.where(lane_id == line(lane_of, 0), 1.0, 0.0).astype(BF16)
                here = row_id == line(r, begin)
                if h == 1:
                    hot = jnp.concatenate([hot, jnp.zeros((128 - depth, wide), BF16)], axis=0)
                twice = jnp.concatenate([hot, hot], axis=0) if two_parts else hot
                got = jnp.dot(stacked, twice, preferred_element_type=F32)
                got_x = jnp.sum(jnp.where(here, got[0:size], 0.0), axis=0, keepdims=True)
                got_y = jnp.sum(jnp.where(here, got[size:], 0.0), axis=0, keepdims=True)
                amount = line_x * got_x + line_y * got_y
                terms = [amount * line_x, amount * line_y]
                if two_parts:
                    highs = [p.astype(BF16).astype(F32) for p in terms]
                    terms = highs + [p - q for p, q in zip(terms, highs)]
                spread = jnp.concatenate([jnp.where(here, p, 0.0) for p in terms], axis=0).astype(BF16)
                total = total + lax.dot_general(spread, hot, (((1,), (1,)), ((), ())), preferred_element_type=F32)
            if two_parts:
                total = total[0 : 2 * size] + total[2 * size :]
            if h == 1:
                total = pltpu.roll(total, 128 - EDGE, 1)
            for c in range(2):
                nat_ref[c, h, first : first + size, :] = total[c * size : (c + 1) * size]

        for v in range(groups):
            at = pl.ds(v * 8, 8)
            for h in range(2):
                cols = pl.ds(h * 128, 128)
                for c in range(2):
                    src_ref[c, at, cols] = coef_ref[8 + c, at, cols] * nat_ref[(c,) + natural(h, v)]

    lax.fori_loop(0, 2, solve, 0)
    for copy in copies:
        copy.wait()
    pltpu.make_async_copy(inc_ref, inc_hbm, inc_sem).wait()
    hess = -(bv_ref[0] * nat_ref[0, 0, HALO : HALO + rows, :] + bv_ref[1] * nat_ref[1, 0, HALO : HALO + rows, :])
    hess_ref[...] = hess
    low_ref[...] = hess.astype(BF16)


def distances(n_grp):
    return [0] + list(range(2, n_grp)) + [1]


def project_block(panels_ref, probe_ref, k, distance):
    count, n_grp, rows, columns = panels_ref.shape
    product = panels_ref[k, lax.axis_index("grp") ^ distance].astype(F32) * probe_ref[...].astype(F32)
    return jnp.sum(product.reshape(-1, 8, columns), axis=0)


def project_kernel(panels_ref, hess_ref, *refs):
    blocks, (sums_ref, hess_hbm, sem) = refs[:-3], refs[-3:]
    copy = pltpu.make_async_copy(hess_ref, hess_hbm, sem)
    copy.start()
    order = distances(panels_ref.shape[1])
    for k in range(panels_ref.shape[0]):
        sums_ref[k] = sum(project_block(panels_ref, block, k, i) for i, block in zip(order, blocks))
    copy.wait()


def project_last_kernel(panels_ref, block_ref, sums_ref, out_ref):
    count, n_grp = panels_ref.shape[:2]
    sums = []
    for k in range(count):
        total = sums_ref[k] + project_block(panels_ref, block_ref, k, distances(n_grp)[-1])
        sums.append(jnp.sum(total, axis=0, keepdims=True))
    sums.append(jnp.zeros((128 - count, 128), F32))
    table = jnp.concatenate(sums, axis=0)
    high = table.astype(BF16)
    parts = jnp.concatenate([high, (table - high.astype(F32)).astype(BF16)], axis=1)
    line = lax.dot_general(
        jnp.ones((16, 256), BF16), parts, (((1,), (1,)), ((), ())), preferred_element_type=F32
    )
    line = pltpu.roll(line, lax.axis_index("grp") * count, 1)[0:1]
    out_ref[...] = jnp.broadcast_to(line[None], out_ref.shape)


def add_lines_kernel(lines_ref, out_ref):
    out_ref[...] = jnp.sum(lines_ref[...], axis=0)


def vmem(n):
    return [pl.BlockSpec(memory_space=pltpu.VMEM)] * n


def on_device(
    base_velocity, viscosity, friction, friction_probe, pixel_los, pixel_weight, pixel_cell, pixel_count, panels
):
    n_grp, n_tile = lax.axis_size("grp"), lax.axis_size("tile")
    rows, columns = viscosity.shape
    half = rows // 2
    span = rows + 2 * HALO
    params = pltpu.CompilerParams(vmem_limit_bytes=32 * 2**20)

    inputs = [
        pltpu.with_memory_space_constraint(x, pltpu.HBM)
        for x in (
            base_velocity, viscosity, friction, friction_probe, pixel_los, pixel_weight, pixel_cell, pixel_count
        )
    ]
    slots, fields = pl.pallas_call(
        functools.partial(pack_tiles_kernel, n_tile),
        out_shape=(
            jax.ShapeDtypeStruct((n_tile, half + 16, 128), BF16),
            jax.ShapeDtypeStruct((FIELDS, rows, columns), F32),
        ),
        in_specs=[pl.BlockSpec(memory_space=pltpu.HBM)] * len(inputs),
        out_specs=tuple(vmem(2)),
        scratch_shapes=[pltpu.VMEM(x.shape, x.dtype) for x in inputs] + [pltpu.SemaphoreType.DMA((len(inputs),))],
        compiler_params=params,
        name="pack_tiles",
    )(*inputs)
    got = lax.all_to_all(slots, "tile", split_axis=0, concat_axis=0, tiled=True)

    packet = (FIELDS + 1) * HALO + 6 * n_tile
    ext, pix, up, down = pl.pallas_call(
        functools.partial(pack_rows_kernel, n_tile),
        out_shape=(
            jax.ShapeDtypeStruct((FIELDS, rows, 256), F32),
            jax.ShapeDtypeStruct((6 * n_tile, 128), F32),
            jax.ShapeDtypeStruct((packet, 128), BF16),
            jax.ShapeDtypeStruct((packet, 128), BF16),
        ),
        in_specs=vmem(2),
        out_specs=tuple(vmem(4)),
        compiler_params=params,
        name="pack_rows",
    )(fields, got)
    above = lax.ppermute(down, "grp", [(i, (i + 1) % n_grp) for i in range(n_grp)])
    below = lax.ppermute(up, "grp", [((i + 1) % n_grp, i) for i in range(n_grp)])

    increment, hess, probe_low, panels_near = pl.pallas_call(
        functools.partial(solve_kernel, n_grp, n_tile),
        out_shape=(
            jax.ShapeDtypeStruct((2, rows, columns), F32),
            jax.ShapeDtypeStruct((rows, columns), F32),
            jax.ShapeDtypeStruct((rows, columns), BF16),
            jax.ShapeDtypeStruct((panels.shape[0], n_grp, rows, columns), BF16),
        ),
        in_specs=vmem(4) + [pl.BlockSpec(memory_space=pltpu.HBM)] * 2,
        out_specs=tuple([pl.BlockSpec(memory_space=pltpu.HBM)] + vmem(3)),
        scratch_shapes=[
            pltpu.VMEM((FIELDS, 2, span, 128), F32),
            pltpu.VMEM((10, span, 256), F32),
            pltpu.VMEM((2, span, 256), F32),
            pltpu.VMEM((3, 2, span, 256), F32),
            pltpu.VMEM((2, 2, span, 128), F32),
            pltpu.VMEM(base_velocity.shape, F32),
            pltpu.VMEM(base_velocity.shape, F32),
            pltpu.SemaphoreType.DMA((1 + n_grp,)),
            pltpu.SemaphoreType.DMA,
        ],
        compiler_params=params,
        name="solve",
    )(ext, pix, above, below, inputs[0], pltpu.with_memory_space_constraint(panels, pltpu.HBM))

    column = [probe_low] + [
        lax.ppermute(probe_low, "grp", [(i, i ^ k) for i in range(n_grp)]) for k in distances(n_grp)[1:]
    ]
    sums, hessian_probe = pl.pallas_call(
        project_kernel,
        out_shape=(
            jax.ShapeDtypeStruct((panels.shape[0], 8, 128), F32),
            jax.ShapeDtypeStruct((rows, columns), F32),
        ),
        in_specs=vmem(1 + n_grp),
        out_specs=(pl.BlockSpec(memory_space=pltpu.VMEM), pl.BlockSpec(memory_space=pltpu.HBM)),
        scratch_shapes=[pltpu.SemaphoreType.DMA],
        compiler_params=params,
        cost_estimate=pl.CostEstimate(
            flops=2 * panels.size * (n_grp - 1) // n_grp, bytes_accessed=2 * panels.size, transcendentals=0
        ),
        name="project",
    )(panels_near, hess, *column[:-1])
    partial = pl.pallas_call(
        project_last_kernel,
        out_shape=jax.ShapeDtypeStruct((n_grp * n_tile, 1, 128), F32),
        in_specs=vmem(3),
        out_specs=pl.BlockSpec(memory_space=pltpu.VMEM),
        compiler_params=params,
        name="project_last",
    )(panels_near, column[-1], sums)
    everyone = lax.all_to_all(partial, ("grp", "tile"), split_axis=0, concat_axis=0, tiled=True)
    coefficients = pl.pallas_call(
        add_lines_kernel,
        out_shape=jax.ShapeDtypeStruct((1, 128), F32),
        in_specs=vmem(1),
        out_specs=pl.BlockSpec(memory_space=pltpu.VMEM),
        compiler_params=params,
        name="add_lines",
    )(everyone)
    return increment, hessian_probe, coefficients.reshape(128)


def solution(mesh):
    in_specs = (
        P(None, "grp", "tile"),
        P("grp", "tile"),
        P("grp", "tile"),
        P("grp", "tile"),
        P("grp", "tile", None, None),
        P("grp", "tile", None, None),
        P("grp", "tile", None, None),
        P("grp", "tile", None, None),
        P("grp", None, "tile"),
    )
    out_specs = (P(None, "grp", "tile"), P("grp", "tile"), P())
    return jax.shard_map(
        on_device, mesh=mesh, in_specs=in_specs, out_specs=out_specs, check_vma=False
    )
```

```python
import functools

import jax
import jax.numpy as jnp
from jax import lax
from jax.experimental import pallas as pl
from jax.experimental.pallas import tpu as pltpu
from jax.sharding import PartitionSpec as P

SWEEPS = 8
RELAX = 0.8
CAP = 64
HALO = 16
EDGE = 8
FIELDS = 4
STRIPS = 8
F32 = jnp.float32
BF16 = jnp.bfloat16


def lanes(shape=(8, 128)):
    return lax.broadcasted_iota(jnp.int32, shape, len(shape) - 1)


def fetch(sources, targets, sems):
    copies = [pltpu.make_async_copy(s, d, sems.at[i]) for i, (s, d) in enumerate(zip(sources, targets))]
    for copy in copies:
        copy.start()
    return copies


def pack_tiles_kernel(n_tile, *refs):
    sources, (out_ref, fields_ref), targets, sems = refs[:8], refs[8:10], refs[10:18], refs[18]
    copies = fetch(sources, targets, sems)
    bv_ref, visc_ref, fric_ref, fp_ref, los_ref, weight_ref, cell_ref, count_ref = targets
    t = lax.axis_index("tile")
    parity = lax.rem(t, 2)
    rows = visc_ref.shape[0]
    half = rows // 2
    for copy in copies[4:]:
        copy.wait()
    row_lane = lanes((1, 128))
    low = lanes() < CAP
    straight, turned = [], []
    for j in range(n_tile // 2):
        at = pl.ds(j * 128, 128)
        count = jnp.where(
            row_lane < CAP, count_ref[0, 0, :, 2 * j : 2 * j + 1], count_ref[0, 0, :, 2 * j + 1 : 2 * j + 2]
        )
        live = (row_lane & (CAP - 1)) < count
        weight = jnp.where(live, weight_ref[0, 0, :, at], 0.0)
        scaled = jnp.sqrt(weight) * los_ref[0, 0, :, at]
        high = scaled.astype(BF16).astype(F32)
        cell = cell_ref[0, 0, :, at]
        block = jnp.concatenate(
            [
                high, scaled - high,
                lax.shift_right_logical(cell, 7).astype(F32), (cell & 127).astype(F32), jnp.zeros((2, 128), F32),
            ],
            axis=0,
        )
        straight.append(block)
        turned.append(pltpu.roll(block, CAP, 1))
    nothing = jnp.zeros((8, 128), F32)
    in_half = (lanes() // CAP) == parity

    def placed(owner, side):
        if owner < 0 or owner >= n_tile:
            return nothing
        return (straight if owner % 2 == side else turned)[owner // 2]

    for d in range(n_tile):
        solo = jnp.where(parity == d % 2, straight[d // 2], turned[d // 2])
        solo = jnp.where(in_half, solo, 0.0)
        pair = jnp.where(low, placed(d - 1, 0), placed(d + 1, 1))
        out_ref[d, half : half + 16, :] = jnp.concatenate([solo, pair], axis=0).astype(BF16)

    for copy in copies[:4]:
        copy.wait()
    probe = fp_ref[...]
    fields = [-(probe * bv_ref[0]), -(probe * bv_ref[1]), visc_ref[...], fric_ref[...]]
    for f, field in enumerate(fields):
        fields_ref[f] = field
    lane = lanes((half, 128))

    def fold(first_lane):
        packed = jnp.zeros((half, 128), F32)
        for part in range(2):
            for f, field in enumerate(fields):
                start = part * 64 + f * HALO
                piece = field[part * half : (part + 1) * half]
                piece = pltpu.roll(piece, (start - first_lane) % 128, 1)
                packed = jnp.where((lane >= start) & (lane < start + HALO), piece, packed)
        return packed

    out_ref[jnp.minimum(t + 1, n_tile - 1), 0:half, :] = fold(128 - HALO).astype(BF16)
    out_ref[jnp.maximum(t - 1, 0), 0:half, :] = fold(0).astype(BF16)


def pack_rows_kernel(n_tile, fields_ref, got_ref, ext_ref, pix_ref, even_ref, odd_ref):
    g = lax.axis_index("grp")
    t = lax.axis_index("tile")
    rows = fields_ref.shape[1]
    half = rows // 2
    fields = [fields_ref[f] for f in range(FIELDS)]
    lane = lanes((half, 128))
    right = jnp.where(t < n_tile - 1, got_ref[jnp.minimum(t + 1, n_tile - 1), 0:half, :].astype(F32), 0.0)
    left = jnp.where(t > 0, got_ref[jnp.maximum(t - 1, 0), 0:half, :].astype(F32), 0.0)
    band = lanes((HALO, 128))
    edge_up = jnp.zeros((HALO, 128), F32)
    edge_down = jnp.zeros((HALO, 128), F32)
    for f, field in enumerate(fields):
        ext_ref[f, :, 0:128] = field
        edges = []
        for part in range(2):
            start = part * 64 + f * HALO
            edge = jnp.where(
                lane < HALO,
                pltpu.roll(right, (0 - start) % 128, 1),
                jnp.where(lane >= 128 - HALO, pltpu.roll(left, (128 - HALO - start) % 128, 1), 0.0),
            )
            ext_ref[f, part * half : (part + 1) * half, 128:256] = edge
            edges.append(edge)
        here = (band >= 2 * f * HALO) & (band < 2 * (f + 1) * HALO)
        turn = (2 * f + 1) * HALO % 128
        edge_up = jnp.where(here, pltpu.roll(edges[0][0:HALO], turn, 1), edge_up)
        edge_down = jnp.where(here, pltpu.roll(edges[1][half - HALO :], turn, 1), edge_down)
    low = lanes() < CAP
    near, far = [], []
    for s in range(0, n_tile, 2):
        one = got_ref[s, half : half + 16, :].astype(F32)
        two = got_ref[s + 1, half : half + 16, :].astype(F32)
        near.append(jnp.where(low, one[0:8], two[0:8]))
        far += [one[8:16], two[8:16]]
    blocks = near + far
    pixels = jnp.concatenate(
        [b[0:1] + b[2:3] for b in blocks]
        + [b[1:2] + b[3:4] for b in blocks]
        + [b[4:5] for b in blocks]
        + [b[5:6] for b in blocks],
        axis=0,
    )
    pix_ref[...] = pixels
    pixels = pixels.astype(BF16)

    even = lax.rem(g, 2) == 0

    def choose(one, two):
        even_ref_value, odd_ref_value = jnp.where(even, one, two), jnp.where(even, two, one)
        return even_ref_value.astype(BF16), odd_ref_value.astype(BF16)

    for f, field in enumerate(fields):
        at = pl.ds(f * HALO, HALO)
        even_ref[at, :], odd_ref[at, :] = choose(field[rows - HALO :], field[0:HALO])
    at = pl.ds(FIELDS * HALO, HALO)
    even_ref[at, :], odd_ref[at, :] = choose(edge_down, edge_up)
    for ref in (even_ref, odd_ref):
        ref[(FIELDS + 1) * HALO :, :] = pixels


def solve_kernel(
    n_grp, n_tile, ext_ref, pix_ref, odd_ref, even_ref, bv_hbm, panels_hbm,
    inc_hbm, hess_ref, low_ref, panels_ref,
    plane_ref, coef_ref, src_ref, w_ref, nat_ref, bv_ref, inc_ref, sems, inc_sem,
):
    size = panels_ref.shape[2]
    copies = fetch(
        [bv_hbm] + [panels_hbm.at[:, pl.ds(i * size, size), :] for i in range(n_grp)],
        [bv_ref] + [panels_ref.at[:, i] for i in range(n_grp)],
        sems,
    )
    g = lax.axis_index("grp")
    t = lax.axis_index("tile")
    rows = ext_ref.shape[1]
    span = rows + 2 * HALO
    groups = span // STRIPS
    lane = lanes()

    even = lax.rem(g, 2) == 0

    def above(first, size):
        at = pl.ds(first, size)
        got = jnp.where(even, odd_ref[at, :].astype(F32), even_ref[at, :].astype(F32))
        return jnp.where(g > 0, got, 0.0)

    def below(first, size):
        at = pl.ds(first, size)
        got = jnp.where(even, even_ref[at, :].astype(F32), odd_ref[at, :].astype(F32))
        return jnp.where(g < n_grp - 1, got, 0.0)

    first_lane = lane == 0
    last_lane = lane == 127

    band = lanes((HALO, 128))
    for f in range(FIELDS):
        for h in range(2):
            plane_ref[f, h, HALO : HALO + rows, :] = ext_ref[f, :, h * 128 : (h + 1) * 128]
        for load, at in ((above, 0), (below, HALO + rows)):
            plane_ref[f, 0, at : at + HALO, :] = load(f * HALO, HALO)
            edge = pltpu.roll(load(FIELDS * HALO, HALO), (0 - (2 * f + 1) * HALO) % 128, 1)
            plane_ref[f, 1, at : at + HALO, :] = jnp.where((band < HALO) | (band >= 128 - HALO), edge, 0.0)

    def strided(f, h, v):
        return plane_ref[f, h, pl.ds(v, STRIPS, stride=groups), :]

    def beside(pair):
        a, b = pair
        ra, rb = pltpu.roll(a, 1, 1), pltpu.roll(b, 1, 1)
        before = (jnp.where(first_lane, rb, ra), jnp.where(first_lane, ra, rb))
        ra, rb = pltpu.roll(a, 127, 1), pltpu.roll(b, 127, 1)
        after = (jnp.where(last_lane, rb, ra), jnp.where(last_lane, ra, rb))
        return before, pair, after

    def row(load, v):
        if v < 0:
            return beside(tuple(pltpu.roll(load(h, groups - 1), 1, 0) for h in range(2)))
        if v == groups:
            return beside(tuple(pltpu.roll(load(h, 0), STRIPS - 1, 0) for h in range(2)))
        return beside(tuple(load(h, v) for h in range(2)))

    strip = lax.broadcasted_iota(jnp.int32, (8, 128), 0)
    col_in = [
        None,
        ((lane < HALO) & (t < n_tile - 1)) | ((lane >= 128 - HALO) & (t > 0)),
    ]
    load_visc = functools.partial(strided, 2)
    prev, cur = row(load_visc, -1), row(load_visc, 0)
    for v in range(groups):
        nxt = row(load_visc, v + 1)
        place = g * rows - HALO + strip * groups + v
        row_in = (place >= 0) & (place < n_grp * rows)
        at = pl.ds(v * 8, 8)
        for h in range(2):
            centre = cur[1][h]
            east = 0.5 * (centre + nxt[1][h])
            west = 0.5 * (centre + prev[1][h])
            north = 0.5 * (centre + cur[2][h])
            south = 0.5 * (centre + cur[0][h])
            node_pp = 0.25 * (centre + nxt[1][h] + cur[2][h] + nxt[2][h])
            node_mm = 0.25 * (centre + prev[1][h] + cur[0][h] + prev[0][h])
            node_pm = 0.25 * (centre + nxt[1][h] + cur[0][h] + nxt[0][h])
            node_mp = 0.25 * (centre + prev[1][h] + cur[2][h] + prev[2][h])
            fric = strided(3, h, v)
            diag_x = fric + 2.0 * (east + west) + (north + south)
            diag_y = fric + (east + west) + 2.0 * (north + south)
            inside = row_in if col_in[h] is None else row_in & col_in[h]
            inv_x = jnp.where(inside, RELAX / jnp.where(inside, diag_x, 1.0), 0.0)
            inv_y = jnp.where(inside, RELAX / jnp.where(inside, diag_y, 1.0), 0.0)
            cols = pl.ds(h * 128, 128)
            for i, plane in enumerate(
                (east, west, north, south, 0.25 * node_pp, 0.25 * node_mm, 0.25 * node_pm, 0.25 * node_mp, inv_x, inv_y)
            ):
                coef_ref[i, at, cols] = plane
            src_ref[0, at, cols] = inv_x * strided(0, h, v)
            src_ref[1, at, cols] = inv_y * strided(1, h, v)
        prev, cur = cur, nxt

    def natural(h, v):
        return (h, pl.ds(v, STRIPS, stride=groups), slice(None))

    def relax():
        w_ref[0] = src_ref[...]

        def sweep(now, later, start):
            rows_seen = {}

            def both(v):
                if v not in rows_seen:
                    rows_seen[v] = tuple(
                        row(lambda h, u, c=c: now[c, pl.ds(u * 8, 8), pl.ds(h * 128, 128)], v) for c in range(2)
                    )
                return rows_seen[v]

            for p in range(groups):
                v = (p + start) % groups
                prev, cur, nxt = both(v - 1), both(v), both(v + 1)
                at = pl.ds(v * 8, 8)
                for h in range(2):
                    cols = pl.ds(h * 128, 128)
                    east, west, north, south, pp, mm, pm, mp, inv_x, inv_y = (
                        coef_ref[i, at, cols] for i in range(10)
                    )

                    def along(c):
                        return (
                            east * nxt[c][1][h] + west * prev[c][1][h],
                            north * cur[c][2][h] + south * cur[c][0][h],
                        )

                    def cross(c):
                        return (
                            pp * nxt[c][2][h] + mm * prev[c][0][h] - pm * nxt[c][0][h] - mp * prev[c][2][h]
                        )

                    one, two = along(0)
                    sum_x = 2.0 * one + two + cross(1)
                    one, two = along(1)
                    sum_y = one + 2.0 * two + cross(0)
                    for c, new in ((0, inv_x * sum_x), (1, inv_y * sum_y)):
                        new = (1.0 - RELAX) * cur[c][1][h] + src_ref[c, at, cols] + new
                        if later is None:
                            nat_ref[(c,) + natural(h, v)] = new
                        else:
                            later[c, at, cols] = new

        def three_sweeps(_, carry):
            for k in range(3):
                sweep(w_ref.at[k], w_ref.at[(k + 1) % 3], k)
            return carry

        lax.fori_loop(0, (SWEEPS - 2) // 3, three_sweeps, 0)
        sweep(w_ref.at[0], None, 0)

    def solve(phase, carry):
        relax()

        @pl.when(phase == 0)
        def _():
            for c in range(2):
                inc_ref[c] = nat_ref[c, 0, HALO : HALO + rows, :]
            pltpu.make_async_copy(inc_ref, inc_hbm, inc_sem).start()
            misfit()

        return carry

    def misfit():
        n_near, n_all = n_tile // 2, 3 * n_tile // 2
        low = lanes((n_tile, 128)) < CAP
        spans = ((0, HALO, rows), (-1, HALO - EDGE, EDGE), (1, HALO + rows, EDGE))

        def exact(h, delta):
            return h == 0 and delta == 0

        jobs = []
        for delta, first, size in spans:
            if delta == 0:
                values = pix_ref[...]
            else:
                base = (FIELDS + 1) * HALO
                values = (above if delta < 0 else below)(base, 4 * n_all)
            los_x, los_y, r, c = (values[q * n_all : (q + 1) * n_all] for q in range(4))
            if delta < 0:
                r = r - (rows - EDGE)
            in_rim = c[n_near:] + jnp.where(low, float(EDGE) - 128.0, float(EDGE))
            for h, begin, count, lane_of in ((0, 0, n_near, c[0:n_near]), (1, n_near, n_tile, in_rim)):
                parts = []
                for comp in range(2):
                    part = nat_ref[comp, h, first : first + size, :]
                    parts.append(part if h == 0 else pltpu.roll(part, EDGE, 1))
                field = jnp.concatenate(parts, axis=0)
                stacked = field.astype(BF16)
                if exact(h, delta):
                    rest = (field - stacked.astype(F32)).astype(BF16)
                    stacked = jnp.concatenate([stacked, rest], axis=1)
                jobs.append((exact(h, delta), h, first, size, begin, count, lane_of, los_x, los_y, r, stacked))

        nat_ref[...] = jnp.zeros_like(nat_ref)
        for two_parts, h, first, size, begin, count, lane_of, los_x, los_y, r, stacked in jobs:
            chunk = 4 if h == 0 else 8
            depth = 128 if h == 0 else 2 * EDGE
            wide = chunk * 128
            row_id = lax.broadcasted_iota(jnp.int32, (size, wide), 0).astype(F32)
            lane_id = lax.broadcasted_iota(jnp.int32, (depth, wide), 0).astype(F32)
            total = jnp.zeros(((4 if two_parts else 2) * size, 128), F32)
            for j in range(0, count, chunk):

                def line(table, offset):
                    return jnp.concatenate([table[offset + i : offset + i + 1] for i in range(j, j + chunk)], axis=1)

                line_x, line_y = line(los_x, begin), line(los_y, begin)
                hot = jnp.where(lane_id == line(lane_of, 0), 1.0, 0.0).astype(BF16)
                here = row_id == line(r, begin)
                if h == 1:
                    hot = jnp.concatenate([hot, jnp.zeros((128 - depth, wide), BF16)], axis=0)
                twice = jnp.concatenate([hot, hot], axis=0) if two_parts else hot
                got = jnp.dot(stacked, twice, preferred_element_type=F32)
                got_x = jnp.sum(jnp.where(here, got[0:size], 0.0), axis=0, keepdims=True)
                got_y = jnp.sum(jnp.where(here, got[size:], 0.0), axis=0, keepdims=True)
                amount = line_x * got_x + line_y * got_y
                terms = [amount * line_x, amount * line_y]
                if two_parts:
                    highs = [p.astype(BF16).astype(F32) for p in terms]
                    terms = highs + [p - q for p, q in zip(terms, highs)]
                spread = jnp.concatenate([jnp.where(here, p, 0.0) for p in terms], axis=0).astype(BF16)
                total = total + lax.dot_general(spread, hot, (((1,), (1,)), ((), ())), preferred_element_type=F32)
            if two_parts:
                total = total[0 : 2 * size] + total[2 * size :]
            if h == 1:
                total = pltpu.roll(total, 128 - EDGE, 1)
            for c in range(2):
                nat_ref[c, h, first : first + size, :] = total[c * size : (c + 1) * size]

        for v in range(groups):
            at = pl.ds(v * 8, 8)
            for h in range(2):
                cols = pl.ds(h * 128, 128)
                for c in range(2):
                    src_ref[c, at, cols] = coef_ref[8 + c, at, cols] * nat_ref[(c,) + natural(h, v)]

    lax.fori_loop(0, 2, solve, 0)
    for copy in copies:
        copy.wait()
    pltpu.make_async_copy(inc_ref, inc_hbm, inc_sem).wait()
    hess = -(bv_ref[0] * nat_ref[0, 0, HALO : HALO + rows, :] + bv_ref[1] * nat_ref[1, 0, HALO : HALO + rows, :])
    hess_ref[...] = hess
    low_ref[...] = hess.astype(BF16)


def distances(n_grp):
    return [0] + list(range(2, n_grp)) + [1]


def project_block(panels_ref, probe_ref, k, distance):
    count, n_grp, rows, columns = panels_ref.shape
    product = panels_ref[k, lax.axis_index("grp") ^ distance].astype(F32) * probe_ref[...].astype(F32)
    return jnp.sum(product.reshape(-1, 8, columns), axis=0)


def project_kernel(panels_ref, hess_ref, *refs):
    blocks, (sums_ref, hess_hbm, sem) = refs[:-3], refs[-3:]
    copy = pltpu.make_async_copy(hess_ref, hess_hbm, sem)
    copy.start()
    order = distances(panels_ref.shape[1])
    for k in range(panels_ref.shape[0]):
        sums_ref[k] = sum(project_block(panels_ref, block, k, i) for i, block in zip(order, blocks))
    copy.wait()


def project_last_kernel(panels_ref, block_ref, sums_ref, out_ref):
    count, n_grp = panels_ref.shape[:2]
    sums = []
    for k in range(count):
        total = sums_ref[k] + project_block(panels_ref, block_ref, k, distances(n_grp)[-1])
        sums.append(jnp.sum(total, axis=0, keepdims=True))
    sums.append(jnp.zeros((128 - count, 128), F32))
    table = jnp.concatenate(sums, axis=0)
    high = table.astype(BF16)
    parts = jnp.concatenate([high, (table - high.astype(F32)).astype(BF16)], axis=1)
    line = lax.dot_general(
        jnp.ones((16, 256), BF16), parts, (((1,), (1,)), ((), ())), preferred_element_type=F32
    )
    line = pltpu.roll(line, lax.axis_index("grp") * count, 1)[0:1]
    out_ref[...] = jnp.broadcast_to(line[None], out_ref.shape)


def add_lines_kernel(lines_ref, out_ref):
    out_ref[...] = jnp.sum(lines_ref[...], axis=0)


def vmem(n):
    return [pl.BlockSpec(memory_space=pltpu.VMEM)] * n


def on_device(
    base_velocity, viscosity, friction, friction_probe, pixel_los, pixel_weight, pixel_cell, pixel_count, panels
):
    n_grp, n_tile = lax.axis_size("grp"), lax.axis_size("tile")
    rows, columns = viscosity.shape
    half = rows // 2
    span = rows + 2 * HALO
    params = pltpu.CompilerParams(vmem_limit_bytes=32 * 2**20)

    inputs = [
        pltpu.with_memory_space_constraint(x, pltpu.HBM)
        for x in (
            base_velocity, viscosity, friction, friction_probe, pixel_los, pixel_weight, pixel_cell, pixel_count
        )
    ]
    slots, fields = pl.pallas_call(
        functools.partial(pack_tiles_kernel, n_tile),
        out_shape=(
            jax.ShapeDtypeStruct((n_tile, half + 16, 128), BF16),
            jax.ShapeDtypeStruct((FIELDS, rows, columns), F32),
        ),
        in_specs=[pl.BlockSpec(memory_space=pltpu.HBM)] * len(inputs),
        out_specs=tuple(vmem(2)),
        scratch_shapes=[pltpu.VMEM(x.shape, x.dtype) for x in inputs] + [pltpu.SemaphoreType.DMA((len(inputs),))],
        compiler_params=params,
        name="pack_tiles",
    )(*inputs)
    got = lax.all_to_all(slots, "tile", split_axis=0, concat_axis=0, tiled=True)

    packet = (FIELDS + 1) * HALO + 6 * n_tile
    ext, pix, even, odd = pl.pallas_call(
        functools.partial(pack_rows_kernel, n_tile),
        out_shape=(
            jax.ShapeDtypeStruct((FIELDS, rows, 256), F32),
            jax.ShapeDtypeStruct((6 * n_tile, 128), F32),
            jax.ShapeDtypeStruct((packet, 128), BF16),
            jax.ShapeDtypeStruct((packet, 128), BF16),
        ),
        in_specs=vmem(2),
        out_specs=tuple(vmem(4)),
        compiler_params=params,
        name="pack_rows",
    )(fields, got)
    even = lax.ppermute(even, "grp", [(i, i ^ 1) for i in range(n_grp)])
    odd = lax.ppermute(odd, "grp", [(i, (i - 1 + 2 * (i % 2)) % n_grp) for i in range(n_grp)])

    increment, hess, probe_low, panels_near = pl.pallas_call(
        functools.partial(solve_kernel, n_grp, n_tile),
        out_shape=(
            jax.ShapeDtypeStruct((2, rows, columns), F32),
            jax.ShapeDtypeStruct((rows, columns), F32),
            jax.ShapeDtypeStruct((rows, columns), BF16),
            jax.ShapeDtypeStruct((panels.shape[0], n_grp, rows, columns), BF16),
        ),
        in_specs=vmem(4) + [pl.BlockSpec(memory_space=pltpu.HBM)] * 2,
        out_specs=tuple([pl.BlockSpec(memory_space=pltpu.HBM)] + vmem(3)),
        scratch_shapes=[
            pltpu.VMEM((FIELDS, 2, span, 128), F32),
            pltpu.VMEM((10, span, 256), F32),
            pltpu.VMEM((2, span, 256), F32),
            pltpu.VMEM((3, 2, span, 256), F32),
            pltpu.VMEM((2, 2, span, 128), F32),
            pltpu.VMEM(base_velocity.shape, F32),
            pltpu.VMEM(base_velocity.shape, F32),
            pltpu.SemaphoreType.DMA((1 + n_grp,)),
            pltpu.SemaphoreType.DMA,
        ],
        compiler_params=params,
        name="solve",
    )(ext, pix, odd, even, inputs[0], pltpu.with_memory_space_constraint(panels, pltpu.HBM))

    column = [probe_low] + [
        lax.ppermute(probe_low, "grp", [(i, i ^ k) for i in range(n_grp)]) for k in distances(n_grp)[1:]
    ]
    sums, hessian_probe = pl.pallas_call(
        project_kernel,
        out_shape=(
            jax.ShapeDtypeStruct((panels.shape[0], 8, 128), F32),
            jax.ShapeDtypeStruct((rows, columns), F32),
        ),
        in_specs=vmem(1 + n_grp),
        out_specs=(pl.BlockSpec(memory_space=pltpu.VMEM), pl.BlockSpec(memory_space=pltpu.HBM)),
        scratch_shapes=[pltpu.SemaphoreType.DMA],
        compiler_params=params,
        cost_estimate=pl.CostEstimate(
            flops=2 * panels.size * (n_grp - 1) // n_grp, bytes_accessed=2 * panels.size, transcendentals=0
        ),
        name="project",
    )(panels_near, hess, *column[:-1])
    partial = pl.pallas_call(
        project_last_kernel,
        out_shape=jax.ShapeDtypeStruct((n_grp * n_tile, 1, 128), F32),
        in_specs=vmem(3),
        out_specs=pl.BlockSpec(memory_space=pltpu.VMEM),
        compiler_params=params,
        name="project_last",
    )(panels_near, column[-1], sums)
    everyone = lax.all_to_all(partial, ("grp", "tile"), split_axis=0, concat_axis=0, tiled=True)
    coefficients = pl.pallas_call(
        add_lines_kernel,
        out_shape=jax.ShapeDtypeStruct((1, 128), F32),
        in_specs=vmem(1),
        out_specs=pl.BlockSpec(memory_space=pltpu.VMEM),
        compiler_params=params,
        name="add_lines",
    )(everyone)
    return increment, hessian_probe, coefficients.reshape(128)


def solution(mesh):
    in_specs = (
        P(None, "grp", "tile"),
        P("grp", "tile"),
        P("grp", "tile"),
        P("grp", "tile"),
        P("grp", "tile", None, None),
        P("grp", "tile", None, None),
        P("grp", "tile", None, None),
        P("grp", "tile", None, None),
        P("grp", None, "tile"),
    )
    out_specs = (P(None, "grp", "tile"), P("grp", "tile"), P())
    return jax.shard_map(
        on_device, mesh=mesh, in_specs=in_specs, out_specs=out_specs, check_vma=False
    )
```

```python
import functools

import jax
import jax.numpy as jnp
from jax import lax
from jax.experimental import pallas as pl
from jax.experimental.pallas import tpu as pltpu
from jax.sharding import PartitionSpec as P

SWEEPS = 8
RELAX = 0.8
CAP = 64
HALO = 16
EDGE = 8
FIELDS = 4
STRIPS = 8
F32 = jnp.float32
BF16 = jnp.bfloat16


def lanes(shape=(8, 128)):
    return lax.broadcasted_iota(jnp.int32, shape, len(shape) - 1)


def fetch(sources, targets, sems):
    copies = [pltpu.make_async_copy(s, d, sems.at[i]) for i, (s, d) in enumerate(zip(sources, targets))]
    for copy in copies:
        copy.start()
    return copies


def pack_tiles_kernel(n_tile, *refs):
    sources, (out_ref, fields_ref), targets, sems = refs[:8], refs[8:10], refs[10:18], refs[18]
    copies = fetch(sources, targets, sems)
    bv_ref, visc_ref, fric_ref, fp_ref, los_ref, weight_ref, cell_ref, count_ref = targets
    t = lax.axis_index("tile")
    parity = lax.rem(t, 2)
    rows = visc_ref.shape[0]
    half = rows // 2
    for copy in copies[4:]:
        copy.wait()
    row_lane = lanes((1, 128))
    low = lanes() < CAP
    straight, turned = [], []
    for j in range(n_tile // 2):
        at = pl.ds(j * 128, 128)
        count = jnp.where(
            row_lane < CAP, count_ref[0, 0, :, 2 * j : 2 * j + 1], count_ref[0, 0, :, 2 * j + 1 : 2 * j + 2]
        )
        live = (row_lane & (CAP - 1)) < count
        weight = jnp.where(live, weight_ref[0, 0, :, at], 0.0)
        scaled = jnp.sqrt(weight) * los_ref[0, 0, :, at]
        high = scaled.astype(BF16).astype(F32)
        cell = cell_ref[0, 0, :, at]
        block = jnp.concatenate(
            [
                high, scaled - high,
                lax.shift_right_logical(cell, 7).astype(F32), (cell & 127).astype(F32), jnp.zeros((2, 128), F32),
            ],
            axis=0,
        )
        straight.append(block)
        turned.append(pltpu.roll(block, CAP, 1))
    nothing = jnp.zeros((8, 128), F32)
    in_half = (lanes() // CAP) == parity

    def placed(owner, side):
        if owner < 0 or owner >= n_tile:
            return nothing
        return (straight if owner % 2 == side else turned)[owner // 2]

    for d in range(n_tile):
        solo = jnp.where(parity == d % 2, straight[d // 2], turned[d // 2])
        solo = jnp.where(in_half, solo, 0.0)
        pair = jnp.where(low, placed(d - 1, 0), placed(d + 1, 1))
        out_ref[d, half : half + 16, :] = jnp.concatenate([solo, pair], axis=0).astype(BF16)

    for copy in copies[:4]:
        copy.wait()
    probe = fp_ref[...]
    fields = [-(probe * bv_ref[0]), -(probe * bv_ref[1]), visc_ref[...], fric_ref[...]]
    for f, field in enumerate(fields):
        fields_ref[f] = field
    lane = lanes((half, 128))

    def fold(first_lane):
        packed = jnp.zeros((half, 128), F32)
        for part in range(2):
            for f, field in enumerate(fields):
                start = part * 64 + f * HALO
                piece = field[part * half : (part + 1) * half]
                piece = pltpu.roll(piece, (start - first_lane) % 128, 1)
                packed = jnp.where((lane >= start) & (lane < start + HALO), piece, packed)
        return packed

    out_ref[jnp.minimum(t + 1, n_tile - 1), 0:half, :] = fold(128 - HALO).astype(BF16)
    out_ref[jnp.maximum(t - 1, 0), 0:half, :] = fold(0).astype(BF16)


def pack_rows_kernel(n_tile, fields_ref, got_ref, ext_ref, pix_ref, up_ref, down_ref):
    t = lax.axis_index("tile")
    rows = fields_ref.shape[1]
    half = rows // 2
    fields = [fields_ref[f] for f in range(FIELDS)]
    lane = lanes((half, 128))
    right = jnp.where(t < n_tile - 1, got_ref[jnp.minimum(t + 1, n_tile - 1), 0:half, :].astype(F32), 0.0)
    left = jnp.where(t > 0, got_ref[jnp.maximum(t - 1, 0), 0:half, :].astype(F32), 0.0)
    band = lanes((HALO, 128))
    edge_up = jnp.zeros((HALO, 128), F32)
    edge_down = jnp.zeros((HALO, 128), F32)
    for f, field in enumerate(fields):
        ext_ref[f, :, 0:128] = field
        edges = []
        for part in range(2):
            start = part * 64 + f * HALO
            edge = jnp.where(
                lane < HALO,
                pltpu.roll(right, (0 - start) % 128, 1),
                jnp.where(lane >= 128 - HALO, pltpu.roll(left, (128 - HALO - start) % 128, 1), 0.0),
            )
            ext_ref[f, part * half : (part + 1) * half, 128:256] = edge
            edges.append(edge)
        here = (band >= 2 * f * HALO) & (band < 2 * (f + 1) * HALO)
        turn = (2 * f + 1) * HALO % 128
        edge_up = jnp.where(here, pltpu.roll(edges[0][0:HALO], turn, 1), edge_up)
        edge_down = jnp.where(here, pltpu.roll(edges[1][half - HALO :], turn, 1), edge_down)
    low = lanes() < CAP
    near, far = [], []
    for s in range(0, n_tile, 2):
        one = got_ref[s, half : half + 16, :].astype(F32)
        two = got_ref[s + 1, half : half + 16, :].astype(F32)
        near.append(jnp.where(low, one[0:8], two[0:8]))
        far += [one[8:16], two[8:16]]
    blocks = near + far
    pixels = jnp.concatenate(
        [b[0:1] + b[2:3] for b in blocks]
        + [b[1:2] + b[3:4] for b in blocks]
        + [b[4:5] for b in blocks]
        + [b[5:6] for b in blocks],
        axis=0,
    )
    pix_ref[...] = pixels
    pixels = pixels.astype(BF16)

    for ref, first, edge in ((up_ref, 0, edge_up), (down_ref, rows - HALO, edge_down)):
        for f, field in enumerate(fields):
            ref[f * HALO : (f + 1) * HALO, :] = field[first : first + HALO].astype(BF16)
        base = FIELDS * HALO
        ref[base : base + HALO, :] = edge.astype(BF16)
        ref[base + HALO :, :] = pixels


def solve_kernel(
    n_grp, n_tile, ext_ref, pix_ref, above_ref, below_ref, bv_hbm, panels_hbm,
    inc_hbm, hess_ref, low_ref, panels_ref,
    plane_ref, coef_ref, src_ref, w_ref, nat_ref, bv_ref, inc_ref, sems, inc_sem,
):
    size = panels_ref.shape[2]
    copies = fetch(
        [bv_hbm] + [panels_hbm.at[:, pl.ds(i * size, size), :] for i in range(n_grp)],
        [bv_ref] + [panels_ref.at[:, i] for i in range(n_grp)],
        sems,
    )
    g = lax.axis_index("grp")
    t = lax.axis_index("tile")
    rows = ext_ref.shape[1]
    span = rows + 2 * HALO
    groups = span // STRIPS
    lane = lanes()

    def above(first, size):
        return jnp.where(g > 0, above_ref[first : first + size, :].astype(F32), 0.0)

    def below(first, size):
        return jnp.where(g < n_grp - 1, below_ref[first : first + size, :].astype(F32), 0.0)

    first_lane = lane == 0
    last_lane = lane == 127

    band = lanes((HALO, 128))
    for f in range(FIELDS):
        for h in range(2):
            plane_ref[f, h, HALO : HALO + rows, :] = ext_ref[f, :, h * 128 : (h + 1) * 128]
        for load, at in ((above, 0), (below, HALO + rows)):
            plane_ref[f, 0, at : at + HALO, :] = load(f * HALO, HALO)
            edge = pltpu.roll(load(FIELDS * HALO, HALO), (0 - (2 * f + 1) * HALO) % 128, 1)
            plane_ref[f, 1, at : at + HALO, :] = jnp.where((band < HALO) | (band >= 128 - HALO), edge, 0.0)

    def strided(f, h, v):
        return plane_ref[f, h, pl.ds(v, STRIPS, stride=groups), :]

    def beside(pair):
        a, b = pair
        ra, rb = pltpu.roll(a, 1, 1), pltpu.roll(b, 1, 1)
        before = (jnp.where(first_lane, rb, ra), jnp.where(first_lane, ra, rb))
        ra, rb = pltpu.roll(a, 127, 1), pltpu.roll(b, 127, 1)
        after = (jnp.where(last_lane, rb, ra), jnp.where(last_lane, ra, rb))
        return before, pair, after

    def row(load, v):
        if v < 0:
            return beside(tuple(pltpu.roll(load(h, groups - 1), 1, 0) for h in range(2)))
        if v == groups:
            return beside(tuple(pltpu.roll(load(h, 0), STRIPS - 1, 0) for h in range(2)))
        return beside(tuple(load(h, v) for h in range(2)))

    strip = lax.broadcasted_iota(jnp.int32, (8, 128), 0)
    col_in = [
        None,
        ((lane < HALO) & (t < n_tile - 1)) | ((lane >= 128 - HALO) & (t > 0)),
    ]
    load_visc = functools.partial(strided, 2)
    prev, cur = row(load_visc, -1), row(load_visc, 0)
    for v in range(groups):
        nxt = row(load_visc, v + 1)
        place = g * rows - HALO + strip * groups + v
        row_in = (place >= 0) & (place < n_grp * rows)
        at = pl.ds(v * 8, 8)
        for h in range(2):
            centre = cur[1][h]
            east = 0.5 * (centre + nxt[1][h])
            west = 0.5 * (centre + prev[1][h])
            north = 0.5 * (centre + cur[2][h])
            south = 0.5 * (centre + cur[0][h])
            node_pp = 0.25 * (centre + nxt[1][h] + cur[2][h] + nxt[2][h])
            node_mm = 0.25 * (centre + prev[1][h] + cur[0][h] + prev[0][h])
            node_pm = 0.25 * (centre + nxt[1][h] + cur[0][h] + nxt[0][h])
            node_mp = 0.25 * (centre + prev[1][h] + cur[2][h] + prev[2][h])
            fric = strided(3, h, v)
            diag_x = fric + 2.0 * (east + west) + (north + south)
            diag_y = fric + (east + west) + 2.0 * (north + south)
            inside = row_in if col_in[h] is None else row_in & col_in[h]
            inv_x = jnp.where(inside, RELAX / jnp.where(inside, diag_x, 1.0), 0.0)
            inv_y = jnp.where(inside, RELAX / jnp.where(inside, diag_y, 1.0), 0.0)
            cols = pl.ds(h * 128, 128)
            for i, plane in enumerate(
                (east, west, north, south, 0.25 * node_pp, 0.25 * node_mm, 0.25 * node_pm, 0.25 * node_mp, inv_x, inv_y)
            ):
                coef_ref[i, at, cols] = plane
            src_ref[0, at, cols] = inv_x * strided(0, h, v)
            src_ref[1, at, cols] = inv_y * strided(1, h, v)
        prev, cur = cur, nxt

    def natural(h, v):
        return (h, pl.ds(v, STRIPS, stride=groups), slice(None))

    def relax():
        w_ref[0] = src_ref[...]

        def sweep(now, later, start):
            rows_seen = {}

            def both(v):
                if v not in rows_seen:
                    rows_seen[v] = tuple(
                        row(lambda h, u, c=c: now[c, pl.ds(u * 8, 8), pl.ds(h * 128, 128)], v) for c in range(2)
                    )
                return rows_seen[v]

            for p in range(groups):
                v = (p + start) % groups
                prev, cur, nxt = both(v - 1), both(v), both(v + 1)
                at = pl.ds(v * 8, 8)
                for h in range(2):
                    cols = pl.ds(h * 128, 128)
                    east, west, north, south, pp, mm, pm, mp, inv_x, inv_y = (
                        coef_ref[i, at, cols] for i in range(10)
                    )

                    def along(c):
                        return (
                            east * nxt[c][1][h] + west * prev[c][1][h],
                            north * cur[c][2][h] + south * cur[c][0][h],
                        )

                    def cross(c):
                        return (
                            pp * nxt[c][2][h] + mm * prev[c][0][h] - pm * nxt[c][0][h] - mp * prev[c][2][h]
                        )

                    one, two = along(0)
                    sum_x = 2.0 * one + two + cross(1)
                    one, two = along(1)
                    sum_y = one + 2.0 * two + cross(0)
                    for c, new in ((0, inv_x * sum_x), (1, inv_y * sum_y)):
                        new = (1.0 - RELAX) * cur[c][1][h] + src_ref[c, at, cols] + new
                        if later is None:
                            nat_ref[(c,) + natural(h, v)] = new
                        else:
                            later[c, at, cols] = new

        def three_sweeps(_, carry):
            for k in range(3):
                sweep(w_ref.at[k], w_ref.at[(k + 1) % 3], k)
            return carry

        lax.fori_loop(0, (SWEEPS - 2) // 3, three_sweeps, 0)
        sweep(w_ref.at[0], None, 0)

    def solve(phase, carry):
        relax()

        @pl.when(phase == 0)
        def _():
            for c in range(2):
                inc_ref[c] = nat_ref[c, 0, HALO : HALO + rows, :]
            pltpu.make_async_copy(inc_ref, inc_hbm, inc_sem).start()
            misfit()

        return carry

    def misfit():
        n_near, n_all = n_tile // 2, 3 * n_tile // 2
        low = lanes((n_tile, 128)) < CAP
        spans = ((0, HALO, rows), (-1, HALO - EDGE, EDGE), (1, HALO + rows, EDGE))

        def exact(h, delta):
            return h == 0 and delta == 0

        jobs = []
        for delta, first, size in spans:
            if delta == 0:
                values = pix_ref[...]
            else:
                base = (FIELDS + 1) * HALO
                values = (above if delta < 0 else below)(base, 4 * n_all)
            los_x, los_y, r, c = (values[q * n_all : (q + 1) * n_all] for q in range(4))
            if delta < 0:
                r = r - (rows - EDGE)
            in_rim = c[n_near:] + jnp.where(low, float(EDGE) - 128.0, float(EDGE))
            for h, begin, count, lane_of in ((0, 0, n_near, c[0:n_near]), (1, n_near, n_tile, in_rim)):
                parts = []
                for comp in range(2):
                    part = nat_ref[comp, h, first : first + size, :]
                    parts.append(part if h == 0 else pltpu.roll(part, EDGE, 1))
                field = jnp.concatenate(parts, axis=0)
                stacked = field.astype(BF16)
                if exact(h, delta):
                    rest = (field - stacked.astype(F32)).astype(BF16)
                    stacked = jnp.concatenate([stacked, rest], axis=1)
                jobs.append((exact(h, delta), h, first, size, begin, count, lane_of, los_x, los_y, r, stacked))

        nat_ref[...] = jnp.zeros_like(nat_ref)
        for two_parts, h, first, size, begin, count, lane_of, los_x, los_y, r, stacked in jobs:
            chunk = 4 if h == 0 else 8
            depth = 128 if h == 0 else 2 * EDGE
            wide = chunk * 128
            row_id = lax.broadcasted_iota(jnp.int32, (size, wide), 0).astype(F32)
            lane_id = lax.broadcasted_iota(jnp.int32, (depth, wide), 0).astype(F32)
            total = jnp.zeros(((4 if two_parts else 2) * size, 128), F32)
            for j in range(0, count, chunk):

                def line(table, offset):
                    return jnp.concatenate([table[offset + i : offset + i + 1] for i in range(j, j + chunk)], axis=1)

                line_x, line_y = line(los_x, begin), line(los_y, begin)
                hot = jnp.where(lane_id == line(lane_of, 0), 1.0, 0.0).astype(BF16)
                here = row_id == line(r, begin)
                if h == 1:
                    hot = jnp.concatenate([hot, jnp.zeros((128 - depth, wide), BF16)], axis=0)
                twice = jnp.concatenate([hot, hot], axis=0) if two_parts else hot
                got = jnp.dot(stacked, twice, preferred_element_type=F32)
                got_x = jnp.sum(jnp.where(here, got[0:size], 0.0), axis=0, keepdims=True)
                got_y = jnp.sum(jnp.where(here, got[size:], 0.0), axis=0, keepdims=True)
                amount = line_x * got_x + line_y * got_y
                terms = [amount * line_x, amount * line_y]
                if two_parts:
                    highs = [p.astype(BF16).astype(F32) for p in terms]
                    terms = highs + [p - q for p, q in zip(terms, highs)]
                spread = jnp.concatenate([jnp.where(here, p, 0.0) for p in terms], axis=0).astype(BF16)
                total = total + lax.dot_general(spread, hot, (((1,), (1,)), ((), ())), preferred_element_type=F32)
            if two_parts:
                total = total[0 : 2 * size] + total[2 * size :]
            if h == 1:
                total = pltpu.roll(total, 128 - EDGE, 1)
            for c in range(2):
                nat_ref[c, h, first : first + size, :] = total[c * size : (c + 1) * size]

        for v in range(groups):
            at = pl.ds(v * 8, 8)
            for h in range(2):
                cols = pl.ds(h * 128, 128)
                for c in range(2):
                    src_ref[c, at, cols] = coef_ref[8 + c, at, cols] * nat_ref[(c,) + natural(h, v)]

    lax.fori_loop(0, 2, solve, 0)
    for copy in copies:
        copy.wait()
    pltpu.make_async_copy(inc_ref, inc_hbm, inc_sem).wait()
    hess = -(bv_ref[0] * nat_ref[0, 0, HALO : HALO + rows, :] + bv_ref[1] * nat_ref[1, 0, HALO : HALO + rows, :])
    hess_ref[...] = hess
    low_ref[...] = hess.astype(BF16)


def distances(n_grp):
    return [0, 1] + list(range(3, n_grp)) + [2]


def project_block(panels_ref, probe_ref, k, distance):
    count, n_grp, rows, columns = panels_ref.shape
    product = panels_ref[k, lax.axis_index("grp") ^ distance].astype(F32) * probe_ref[...].astype(F32)
    return jnp.sum(product.reshape(-1, 8, columns), axis=0)


def project_kernel(panels_ref, hess_ref, *refs):
    blocks, (sums_ref, hess_hbm, sem) = refs[:-3], refs[-3:]
    copy = pltpu.make_async_copy(hess_ref, hess_hbm, sem)
    copy.start()
    order = distances(panels_ref.shape[1])
    for k in range(panels_ref.shape[0]):
        sums_ref[k] = sum(project_block(panels_ref, block, k, i) for i, block in zip(order, blocks))
    copy.wait()


def project_last_kernel(panels_ref, block_ref, sums_ref, out_ref):
    count, n_grp = panels_ref.shape[:2]
    sums = []
    for k in range(count):
        total = sums_ref[k] + project_block(panels_ref, block_ref, k, distances(n_grp)[-1])
        sums.append(jnp.sum(total, axis=0, keepdims=True))
    sums.append(jnp.zeros((128 - count, 128), F32))
    table = jnp.concatenate(sums, axis=0)
    high = table.astype(BF16)
    parts = jnp.concatenate([high, (table - high.astype(F32)).astype(BF16)], axis=1)
    line = lax.dot_general(
        jnp.ones((16, 256), BF16), parts, (((1,), (1,)), ((), ())), preferred_element_type=F32
    )
    line = pltpu.roll(line, lax.axis_index("grp") * count, 1)[0:1]
    out_ref[...] = jnp.broadcast_to(line[None], out_ref.shape)


def add_lines_kernel(lines_ref, out_ref):
    out_ref[...] = jnp.sum(lines_ref[...], axis=0)


def vmem(n):
    return [pl.BlockSpec(memory_space=pltpu.VMEM)] * n


def on_device(
    base_velocity, viscosity, friction, friction_probe, pixel_los, pixel_weight, pixel_cell, pixel_count, panels
):
    n_grp, n_tile = lax.axis_size("grp"), lax.axis_size("tile")
    rows, columns = viscosity.shape
    half = rows // 2
    span = rows + 2 * HALO
    params = pltpu.CompilerParams(vmem_limit_bytes=32 * 2**20)

    inputs = [
        pltpu.with_memory_space_constraint(x, pltpu.HBM)
        for x in (
            base_velocity, viscosity, friction, friction_probe, pixel_los, pixel_weight, pixel_cell, pixel_count
        )
    ]
    slots, fields = pl.pallas_call(
        functools.partial(pack_tiles_kernel, n_tile),
        out_shape=(
            jax.ShapeDtypeStruct((n_tile, half + 16, 128), BF16),
            jax.ShapeDtypeStruct((FIELDS, rows, columns), F32),
        ),
        in_specs=[pl.BlockSpec(memory_space=pltpu.HBM)] * len(inputs),
        out_specs=tuple(vmem(2)),
        scratch_shapes=[pltpu.VMEM(x.shape, x.dtype) for x in inputs] + [pltpu.SemaphoreType.DMA((len(inputs),))],
        compiler_params=params,
        name="pack_tiles",
    )(*inputs)
    got = lax.all_to_all(slots, "tile", split_axis=0, concat_axis=0, tiled=True)

    packet = (FIELDS + 1) * HALO + 6 * n_tile
    ext, pix, up, down = pl.pallas_call(
        functools.partial(pack_rows_kernel, n_tile),
        out_shape=(
            jax.ShapeDtypeStruct((FIELDS, rows, 256), F32),
            jax.ShapeDtypeStruct((6 * n_tile, 128), F32),
            jax.ShapeDtypeStruct((packet, 128), BF16),
            jax.ShapeDtypeStruct((packet, 128), BF16),
        ),
        in_specs=vmem(2),
        out_specs=tuple(vmem(4)),
        compiler_params=params,
        name="pack_rows",
    )(fields, got)
    above = lax.ppermute(down, "grp", [(i, (i + 1) % n_grp) for i in range(n_grp)])
    below = lax.ppermute(up, "grp", [((i + 1) % n_grp, i) for i in range(n_grp)])

    increment, hess, probe_low, panels_near = pl.pallas_call(
        functools.partial(solve_kernel, n_grp, n_tile),
        out_shape=(
            jax.ShapeDtypeStruct((2, rows, columns), F32),
            jax.ShapeDtypeStruct((rows, columns), F32),
            jax.ShapeDtypeStruct((rows, columns), BF16),
            jax.ShapeDtypeStruct((panels.shape[0], n_grp, rows, columns), BF16),
        ),
        in_specs=vmem(4) + [pl.BlockSpec(memory_space=pltpu.HBM)] * 2,
        out_specs=tuple([pl.BlockSpec(memory_space=pltpu.HBM)] + vmem(3)),
        scratch_shapes=[
            pltpu.VMEM((FIELDS, 2, span, 128), F32),
            pltpu.VMEM((10, span, 256), F32),
            pltpu.VMEM((2, span, 256), F32),
            pltpu.VMEM((3, 2, span, 256), F32),
            pltpu.VMEM((2, 2, span, 128), F32),
            pltpu.VMEM(base_velocity.shape, F32),
            pltpu.VMEM(base_velocity.shape, F32),
            pltpu.SemaphoreType.DMA((1 + n_grp,)),
            pltpu.SemaphoreType.DMA,
        ],
        compiler_params=params,
        name="solve",
    )(ext, pix, above, below, inputs[0], pltpu.with_memory_space_constraint(panels, pltpu.HBM))

    column = [probe_low] + [
        lax.ppermute(probe_low, "grp", [(i, i ^ k) for i in range(n_grp)]) for k in distances(n_grp)[1:]
    ]
    sums, hessian_probe = pl.pallas_call(
        project_kernel,
        out_shape=(
            jax.ShapeDtypeStruct((panels.shape[0], 8, 128), F32),
            jax.ShapeDtypeStruct((rows, columns), F32),
        ),
        in_specs=vmem(1 + n_grp),
        out_specs=(pl.BlockSpec(memory_space=pltpu.VMEM), pl.BlockSpec(memory_space=pltpu.HBM)),
        scratch_shapes=[pltpu.SemaphoreType.DMA],
        compiler_params=params,
        cost_estimate=pl.CostEstimate(
            flops=2 * panels.size * (n_grp - 1) // n_grp, bytes_accessed=2 * panels.size, transcendentals=0
        ),
        name="project",
    )(panels_near, hess, *column[:-1])
    partial = pl.pallas_call(
        project_last_kernel,
        out_shape=jax.ShapeDtypeStruct((n_grp * n_tile, 1, 128), F32),
        in_specs=vmem(3),
        out_specs=pl.BlockSpec(memory_space=pltpu.VMEM),
        compiler_params=params,
        name="project_last",
    )(panels_near, column[-1], sums)
    everyone = lax.all_to_all(partial, ("grp", "tile"), split_axis=0, concat_axis=0, tiled=True)
    coefficients = pl.pallas_call(
        add_lines_kernel,
        out_shape=jax.ShapeDtypeStruct((1, 128), F32),
        in_specs=vmem(1),
        out_specs=pl.BlockSpec(memory_space=pltpu.VMEM),
        compiler_params=params,
        name="add_lines",
    )(everyone)
    return increment, hessian_probe, coefficients.reshape(128)


def solution(mesh):
    in_specs = (
        P(None, "grp", "tile"),
        P("grp", "tile"),
        P("grp", "tile"),
        P("grp", "tile"),
        P("grp", "tile", None, None),
        P("grp", "tile", None, None),
        P("grp", "tile", None, None),
        P("grp", "tile", None, None),
        P("grp", None, "tile"),
    )
    out_specs = (P(None, "grp", "tile"), P("grp", "tile"), P())
    return jax.shard_map(
        on_device, mesh=mesh, in_specs=in_specs, out_specs=out_specs, check_vma=False
    )
```

```python
import functools

import jax
import jax.numpy as jnp
from jax import lax
from jax.experimental import pallas as pl
from jax.experimental.pallas import tpu as pltpu
from jax.sharding import PartitionSpec as P

SWEEPS = 8
RELAX = 0.8
CAP = 64
HALO = 16
EDGE = 8
FIELDS = 4
STRIPS = 8
F32 = jnp.float32
BF16 = jnp.bfloat16


def lanes(shape=(8, 128)):
    return lax.broadcasted_iota(jnp.int32, shape, len(shape) - 1)


def fetch(sources, targets, sems):
    copies = [pltpu.make_async_copy(s, d, sems.at[i]) for i, (s, d) in enumerate(zip(sources, targets))]
    for copy in copies:
        copy.start()
    return copies


def pack_tiles_kernel(n_tile, *refs):
    sources, (out_ref, fields_ref), targets, sems = refs[:8], refs[8:10], refs[10:18], refs[18]
    copies = fetch(sources, targets, sems)
    bv_ref, visc_ref, fric_ref, fp_ref, los_ref, weight_ref, cell_ref, count_ref = targets
    t = lax.axis_index("tile")
    parity = lax.rem(t, 2)
    rows = visc_ref.shape[0]
    half = rows // 2
    for copy in copies[4:]:
        copy.wait()
    row_lane = lanes((1, 128))
    low = lanes() < CAP
    straight, turned = [], []
    for j in range(n_tile // 2):
        at = pl.ds(j * 128, 128)
        count = jnp.where(
            row_lane < CAP, count_ref[0, 0, :, 2 * j : 2 * j + 1], count_ref[0, 0, :, 2 * j + 1 : 2 * j + 2]
        )
        live = (row_lane & (CAP - 1)) < count
        weight = jnp.where(live, weight_ref[0, 0, :, at], 0.0)
        scaled = jnp.sqrt(weight) * los_ref[0, 0, :, at]
        high = scaled.astype(BF16).astype(F32)
        cell = cell_ref[0, 0, :, at]
        block = jnp.concatenate(
            [
                high, scaled - high,
                lax.shift_right_logical(cell, 7).astype(F32), (cell & 127).astype(F32), jnp.zeros((2, 128), F32),
            ],
            axis=0,
        )
        straight.append(block)
        turned.append(pltpu.roll(block, CAP, 1))
    nothing = jnp.zeros((8, 128), F32)
    in_half = (lanes() // CAP) == parity

    def placed(owner, side):
        if owner < 0 or owner >= n_tile:
            return nothing
        return (straight if owner % 2 == side else turned)[owner // 2]

    for d in range(n_tile):
        solo = jnp.where(parity == d % 2, straight[d // 2], turned[d // 2])
        solo = jnp.where(in_half, solo, 0.0)
        pair = jnp.where(low, placed(d - 1, 0), placed(d + 1, 1))
        out_ref[d, half : half + 16, :] = jnp.concatenate([solo, pair], axis=0).astype(BF16)

    for copy in copies[:4]:
        copy.wait()
    probe = fp_ref[...]
    fields = [-(probe * bv_ref[0]), -(probe * bv_ref[1]), visc_ref[...], fric_ref[...]]
    for f, field in enumerate(fields):
        fields_ref[f] = field
    lane = lanes((half, 128))

    def fold(first_lane):
        packed = jnp.zeros((half, 128), F32)
        for part in range(2):
            for f, field in enumerate(fields):
                start = part * 64 + f * HALO
                piece = field[part * half : (part + 1) * half]
                piece = pltpu.roll(piece, (start - first_lane) % 128, 1)
                packed = jnp.where((lane >= start) & (lane < start + HALO), piece, packed)
        return packed

    out_ref[jnp.minimum(t + 1, n_tile - 1), 0:half, :] = fold(128 - HALO).astype(BF16)
    out_ref[jnp.maximum(t - 1, 0), 0:half, :] = fold(0).astype(BF16)


def pack_rows_kernel(n_tile, fields_ref, got_ref, ext_ref, pix_ref, even_ref, odd_ref):
    g = lax.axis_index("grp")
    t = lax.axis_index("tile")
    rows = fields_ref.shape[1]
    half = rows // 2
    fields = [fields_ref[f] for f in range(FIELDS)]
    lane = lanes((half, 128))
    right = jnp.where(t < n_tile - 1, got_ref[jnp.minimum(t + 1, n_tile - 1), 0:half, :].astype(F32), 0.0)
    left = jnp.where(t > 0, got_ref[jnp.maximum(t - 1, 0), 0:half, :].astype(F32), 0.0)
    band = lanes((HALO, 128))
    edge_up = jnp.zeros((HALO, 128), F32)
    edge_down = jnp.zeros((HALO, 128), F32)
    for f, field in enumerate(fields):
        ext_ref[f, :, 0:128] = field
        edges = []
        for part in range(2):
            start = part * 64 + f * HALO
            edge = jnp.where(
                lane < HALO,
                pltpu.roll(right, (0 - start) % 128, 1),
                jnp.where(lane >= 128 - HALO, pltpu.roll(left, (128 - HALO - start) % 128, 1), 0.0),
            )
            ext_ref[f, part * half : (part + 1) * half, 128:256] = edge
            edges.append(edge)
        here = (band >= 2 * f * HALO) & (band < 2 * (f + 1) * HALO)
        turn = (2 * f + 1) * HALO % 128
        edge_up = jnp.where(here, pltpu.roll(edges[0][0:HALO], turn, 1), edge_up)
        edge_down = jnp.where(here, pltpu.roll(edges[1][half - HALO :], turn, 1), edge_down)
    low = lanes() < CAP
    near, far = [], []
    for s in range(0, n_tile, 2):
        one = got_ref[s, half : half + 16, :].astype(F32)
        two = got_ref[s + 1, half : half + 16, :].astype(F32)
        near.append(jnp.where(low, one[0:8], two[0:8]))
        far += [one[8:16], two[8:16]]
    blocks = near + far
    pixels = jnp.concatenate(
        [b[0:1] + b[2:3] for b in blocks]
        + [b[1:2] + b[3:4] for b in blocks]
        + [b[4:5] for b in blocks]
        + [b[5:6] for b in blocks],
        axis=0,
    )
    pix_ref[...] = pixels
    pixels = pixels.astype(BF16)

    even = lax.rem(g, 2) == 0

    def choose(one, two):
        even_ref_value, odd_ref_value = jnp.where(even, one, two), jnp.where(even, two, one)
        return even_ref_value.astype(BF16), odd_ref_value.astype(BF16)

    for f, field in enumerate(fields):
        at = pl.ds(f * HALO, HALO)
        even_ref[at, :], odd_ref[at, :] = choose(field[rows - HALO :], field[0:HALO])
    at = pl.ds(FIELDS * HALO, HALO)
    even_ref[at, :], odd_ref[at, :] = choose(edge_down, edge_up)
    for ref in (even_ref, odd_ref):
        ref[(FIELDS + 1) * HALO :, :] = pixels


def solve_kernel(
    n_grp, n_tile, ext_ref, pix_ref, odd_ref, even_ref, bv_hbm, panels_hbm,
    inc_hbm, hess_ref, low_ref, panels_ref,
    plane_ref, coef_ref, src_ref, w_ref, nat_ref, bv_ref, inc_ref, sems, inc_sem,
):
    size = panels_ref.shape[2]
    copies = fetch(
        [bv_hbm] + [panels_hbm.at[:, pl.ds(i * size, size), :] for i in range(n_grp)],
        [bv_ref] + [panels_ref.at[:, i] for i in range(n_grp)],
        sems,
    )
    g = lax.axis_index("grp")
    t = lax.axis_index("tile")
    rows = ext_ref.shape[1]
    span = rows + 2 * HALO
    groups = span // STRIPS
    lane = lanes()

    even = lax.rem(g, 2) == 0

    def above(first, size):
        at = pl.ds(first, size)
        got = jnp.where(even, odd_ref[at, :].astype(F32), even_ref[at, :].astype(F32))
        return jnp.where(g > 0, got, 0.0)

    def below(first, size):
        at = pl.ds(first, size)
        got = jnp.where(even, even_ref[at, :].astype(F32), odd_ref[at, :].astype(F32))
        return jnp.where(g < n_grp - 1, got, 0.0)

    first_lane = lane == 0
    last_lane = lane == 127

    band = lanes((HALO, 128))
    for f in range(FIELDS):
        for h in range(2):
            plane_ref[f, h, HALO : HALO + rows, :] = ext_ref[f, :, h * 128 : (h + 1) * 128]
        for load, at in ((above, 0), (below, HALO + rows)):
            plane_ref[f, 0, at : at + HALO, :] = load(f * HALO, HALO)
            edge = pltpu.roll(load(FIELDS * HALO, HALO), (0 - (2 * f + 1) * HALO) % 128, 1)
            plane_ref[f, 1, at : at + HALO, :] = jnp.where((band < HALO) | (band >= 128 - HALO), edge, 0.0)

    def strided(f, h, v):
        return plane_ref[f, h, pl.ds(v, STRIPS, stride=groups), :]

    def beside(pair):
        a, b = pair
        ra, rb = pltpu.roll(a, 1, 1), pltpu.roll(b, 1, 1)
        before = (jnp.where(first_lane, rb, ra), jnp.where(first_lane, ra, rb))
        ra, rb = pltpu.roll(a, 127, 1), pltpu.roll(b, 127, 1)
        after = (jnp.where(last_lane, rb, ra), jnp.where(last_lane, ra, rb))
        return before, pair, after

    def row(load, v):
        if v < 0:
            return beside(tuple(pltpu.roll(load(h, groups - 1), 1, 0) for h in range(2)))
        if v == groups:
            return beside(tuple(pltpu.roll(load(h, 0), STRIPS - 1, 0) for h in range(2)))
        return beside(tuple(load(h, v) for h in range(2)))

    strip = lax.broadcasted_iota(jnp.int32, (8, 128), 0)
    col_in = [
        None,
        ((lane < HALO) & (t < n_tile - 1)) | ((lane >= 128 - HALO) & (t > 0)),
    ]
    load_visc = functools.partial(strided, 2)
    prev, cur = row(load_visc, -1), row(load_visc, 0)
    for v in range(groups):
        nxt = row(load_visc, v + 1)
        place = g * rows - HALO + strip * groups + v
        row_in = (place >= 0) & (place < n_grp * rows)
        at = pl.ds(v * 8, 8)
        for h in range(2):
            centre = cur[1][h]
            east = 0.5 * (centre + nxt[1][h])
            west = 0.5 * (centre + prev[1][h])
            north = 0.5 * (centre + cur[2][h])
            south = 0.5 * (centre + cur[0][h])
            node_pp = 0.25 * (centre + nxt[1][h] + cur[2][h] + nxt[2][h])
            node_mm = 0.25 * (centre + prev[1][h] + cur[0][h] + prev[0][h])
            node_pm = 0.25 * (centre + nxt[1][h] + cur[0][h] + nxt[0][h])
            node_mp = 0.25 * (centre + prev[1][h] + cur[2][h] + prev[2][h])
            fric = strided(3, h, v)
            diag_x = fric + 2.0 * (east + west) + (north + south)
            diag_y = fric + (east + west) + 2.0 * (north + south)
            inside = row_in if col_in[h] is None else row_in & col_in[h]
            inv_x = jnp.where(inside, RELAX / jnp.where(inside, diag_x, 1.0), 0.0)
            inv_y = jnp.where(inside, RELAX / jnp.where(inside, diag_y, 1.0), 0.0)
            cols = pl.ds(h * 128, 128)
            for i, plane in enumerate(
                (east, west, north, south, 0.25 * node_pp, 0.25 * node_mm, 0.25 * node_pm, 0.25 * node_mp, inv_x, inv_y)
            ):
                coef_ref[i, at, cols] = plane
            for c, inv in ((0, inv_x), (1, inv_y)):
                scaled = inv * strided(c, h, v)
                src_ref[c, at, cols] = scaled
                w_ref[0, c, at, cols] = scaled
        prev, cur = cur, nxt

    def natural(h, v):
        return (h, pl.ds(v, STRIPS, stride=groups), slice(None))

    def relax():
        def sweep(now, later, start):
            rows_seen = {}

            def both(v):
                if v not in rows_seen:
                    rows_seen[v] = tuple(
                        row(lambda h, u, c=c: now[c, pl.ds(u * 8, 8), pl.ds(h * 128, 128)], v) for c in range(2)
                    )
                return rows_seen[v]

            for p in range(groups):
                v = (p + start) % groups
                prev, cur, nxt = both(v - 1), both(v), both(v + 1)
                at = pl.ds(v * 8, 8)
                for h in range(2):
                    cols = pl.ds(h * 128, 128)
                    east, west, north, south, pp, mm, pm, mp, inv_x, inv_y = (
                        coef_ref[i, at, cols] for i in range(10)
                    )

                    def along(c):
                        return (
                            east * nxt[c][1][h] + west * prev[c][1][h],
                            north * cur[c][2][h] + south * cur[c][0][h],
                        )

                    def cross(c):
                        return (
                            pp * nxt[c][2][h] + mm * prev[c][0][h] - pm * nxt[c][0][h] - mp * prev[c][2][h]
                        )

                    one, two = along(0)
                    sum_x = 2.0 * one + two + cross(1)
                    one, two = along(1)
                    sum_y = one + 2.0 * two + cross(0)
                    for c, new in ((0, inv_x * sum_x), (1, inv_y * sum_y)):
                        new = (1.0 - RELAX) * cur[c][1][h] + src_ref[c, at, cols] + new
                        if later is None:
                            nat_ref[(c,) + natural(h, v)] = new
                        else:
                            later[c, at, cols] = new

        def three_sweeps(_, carry):
            for k in range(3):
                sweep(w_ref.at[k], w_ref.at[(k + 1) % 3], k)
            return carry

        lax.fori_loop(0, (SWEEPS - 2) // 3, three_sweeps, 0)
        sweep(w_ref.at[0], None, 0)

    def solve(phase, carry):
        relax()

        @pl.when(phase == 0)
        def _():
            for c in range(2):
                inc_ref[c] = nat_ref[c, 0, HALO : HALO + rows, :]
            pltpu.make_async_copy(inc_ref, inc_hbm, inc_sem).start()
            misfit()

        return carry

    def misfit():
        n_near, n_all = n_tile // 2, 3 * n_tile // 2
        low = lanes((n_tile, 128)) < CAP
        spans = ((0, HALO, rows), (-1, HALO - EDGE, EDGE), (1, HALO + rows, EDGE))

        def exact(h, delta):
            return h == 0 and delta == 0

        jobs = []
        for delta, first, size in spans:
            if delta == 0:
                values = pix_ref[...]
            else:
                base = (FIELDS + 1) * HALO
                values = (above if delta < 0 else below)(base, 4 * n_all)
            los_x, los_y, r, c = (values[q * n_all : (q + 1) * n_all] for q in range(4))
            if delta < 0:
                r = r - (rows - EDGE)
            in_rim = c[n_near:] + jnp.where(low, float(EDGE) - 128.0, float(EDGE))
            for h, begin, count, lane_of in ((0, 0, n_near, c[0:n_near]), (1, n_near, n_tile, in_rim)):
                parts = []
                for comp in range(2):
                    part = nat_ref[comp, h, first : first + size, :]
                    parts.append(part if h == 0 else pltpu.roll(part, EDGE, 1))
                field = jnp.concatenate(parts, axis=0)
                stacked = field.astype(BF16)
                if exact(h, delta):
                    rest = (field - stacked.astype(F32)).astype(BF16)
                    stacked = jnp.concatenate([stacked, rest], axis=1)
                jobs.append((exact(h, delta), h, first, size, begin, count, lane_of, los_x, los_y, r, stacked))

        nat_ref[...] = jnp.zeros_like(nat_ref)
        for two_parts, h, first, size, begin, count, lane_of, los_x, los_y, r, stacked in jobs:
            chunk = 4 if h == 0 else 8
            depth = 128 if h == 0 else 2 * EDGE
            wide = chunk * 128
            row_id = lax.broadcasted_iota(jnp.int32, (size, wide), 0).astype(F32)
            lane_id = lax.broadcasted_iota(jnp.int32, (depth, wide), 0).astype(F32)
            total = jnp.zeros(((4 if two_parts else 2) * size, 128), F32)
            for j in range(0, count, chunk):

                def line(table, offset):
                    return jnp.concatenate([table[offset + i : offset + i + 1] for i in range(j, j + chunk)], axis=1)

                line_x, line_y = line(los_x, begin), line(los_y, begin)
                hot = jnp.where(lane_id == line(lane_of, 0), 1.0, 0.0).astype(BF16)
                here = row_id == line(r, begin)
                if h == 1:
                    hot = jnp.concatenate([hot, jnp.zeros((128 - depth, wide), BF16)], axis=0)
                twice = jnp.concatenate([hot, hot], axis=0) if two_parts else hot
                got = jnp.dot(stacked, twice, preferred_element_type=F32)
                got_x = jnp.sum(jnp.where(here, got[0:size], 0.0), axis=0, keepdims=True)
                got_y = jnp.sum(jnp.where(here, got[size:], 0.0), axis=0, keepdims=True)
                amount = line_x * got_x + line_y * got_y
                terms = [amount * line_x, amount * line_y]
                if two_parts:
                    highs = [p.astype(BF16).astype(F32) for p in terms]
                    terms = highs + [p - q for p, q in zip(terms, highs)]
                spread = jnp.concatenate([jnp.where(here, p, 0.0) for p in terms], axis=0).astype(BF16)
                total = total + lax.dot_general(spread, hot, (((1,), (1,)), ((), ())), preferred_element_type=F32)
            if two_parts:
                total = total[0 : 2 * size] + total[2 * size :]
            if h == 1:
                total = pltpu.roll(total, 128 - EDGE, 1)
            for c in range(2):
                nat_ref[c, h, first : first + size, :] = total[c * size : (c + 1) * size]

        for v in range(groups):
            at = pl.ds(v * 8, 8)
            for h in range(2):
                cols = pl.ds(h * 128, 128)
                for c in range(2):
                    scaled = coef_ref[8 + c, at, cols] * nat_ref[(c,) + natural(h, v)]
                    src_ref[c, at, cols] = scaled
                    w_ref[0, c, at, cols] = scaled

    lax.fori_loop(0, 2, solve, 0)
    for copy in copies:
        copy.wait()
    pltpu.make_async_copy(inc_ref, inc_hbm, inc_sem).wait()
    hess = -(bv_ref[0] * nat_ref[0, 0, HALO : HALO + rows, :] + bv_ref[1] * nat_ref[1, 0, HALO : HALO + rows, :])
    hess_ref[...] = hess
    low_ref[...] = hess.astype(BF16)


def distances(n_grp):
    return [0] + list(range(2, n_grp)) + [1]


def project_block(panels_ref, probe_ref, k, distance):
    count, n_grp, rows, columns = panels_ref.shape
    product = panels_ref[k, lax.axis_index("grp") ^ distance].astype(F32) * probe_ref[...].astype(F32)
    return jnp.sum(product.reshape(-1, 8, columns), axis=0)


def project_kernel(panels_ref, hess_ref, *refs):
    blocks, (sums_ref, hess_hbm, sem) = refs[:-3], refs[-3:]
    copy = pltpu.make_async_copy(hess_ref, hess_hbm, sem)
    copy.start()
    order = distances(panels_ref.shape[1])
    for k in range(panels_ref.shape[0]):
        sums_ref[k] = sum(project_block(panels_ref, block, k, i) for i, block in zip(order, blocks))
    copy.wait()


def project_last_kernel(panels_ref, block_ref, sums_ref, out_ref):
    count, n_grp = panels_ref.shape[:2]
    sums = []
    for k in range(count):
        total = sums_ref[k] + project_block(panels_ref, block_ref, k, distances(n_grp)[-1])
        sums.append(jnp.sum(total, axis=0, keepdims=True))
    sums.append(jnp.zeros((128 - count, 128), F32))
    table = jnp.concatenate(sums, axis=0)
    high = table.astype(BF16)
    parts = jnp.concatenate([high, (table - high.astype(F32)).astype(BF16)], axis=1)
    line = lax.dot_general(
        jnp.ones((16, 256), BF16), parts, (((1,), (1,)), ((), ())), preferred_element_type=F32
    )
    line = pltpu.roll(line, lax.axis_index("grp") * count, 1)[0:1]
    out_ref[...] = jnp.broadcast_to(line[None], out_ref.shape)


def add_lines_kernel(lines_ref, out_ref):
    out_ref[...] = jnp.sum(lines_ref[...], axis=0)


def vmem(n):
    return [pl.BlockSpec(memory_space=pltpu.VMEM)] * n


def on_device(
    base_velocity, viscosity, friction, friction_probe, pixel_los, pixel_weight, pixel_cell, pixel_count, panels
):
    n_grp, n_tile = lax.axis_size("grp"), lax.axis_size("tile")
    rows, columns = viscosity.shape
    half = rows // 2
    span = rows + 2 * HALO
    params = pltpu.CompilerParams(vmem_limit_bytes=32 * 2**20)

    inputs = [
        pltpu.with_memory_space_constraint(x, pltpu.HBM)
        for x in (
            base_velocity, viscosity, friction, friction_probe, pixel_los, pixel_weight, pixel_cell, pixel_count
        )
    ]
    slots, fields = pl.pallas_call(
        functools.partial(pack_tiles_kernel, n_tile),
        out_shape=(
            jax.ShapeDtypeStruct((n_tile, half + 16, 128), BF16),
            jax.ShapeDtypeStruct((FIELDS, rows, columns), F32),
        ),
        in_specs=[pl.BlockSpec(memory_space=pltpu.HBM)] * len(inputs),
        out_specs=tuple(vmem(2)),
        scratch_shapes=[pltpu.VMEM(x.shape, x.dtype) for x in inputs] + [pltpu.SemaphoreType.DMA((len(inputs),))],
        compiler_params=params,
        name="pack_tiles",
    )(*inputs)
    got = lax.all_to_all(slots, "tile", split_axis=0, concat_axis=0, tiled=True)

    packet = (FIELDS + 1) * HALO + 6 * n_tile
    ext, pix, even, odd = pl.pallas_call(
        functools.partial(pack_rows_kernel, n_tile),
        out_shape=(
            jax.ShapeDtypeStruct((FIELDS, rows, 256), F32),
            jax.ShapeDtypeStruct((6 * n_tile, 128), F32),
            jax.ShapeDtypeStruct((packet, 128), BF16),
            jax.ShapeDtypeStruct((packet, 128), BF16),
        ),
        in_specs=vmem(2),
        out_specs=tuple(vmem(4)),
        compiler_params=params,
        name="pack_rows",
    )(fields, got)
    even = lax.ppermute(even, "grp", [(i, i ^ 1) for i in range(n_grp)])
    odd = lax.ppermute(odd, "grp", [(i, (i - 1 + 2 * (i % 2)) % n_grp) for i in range(n_grp)])

    increment, hess, probe_low, panels_near = pl.pallas_call(
        functools.partial(solve_kernel, n_grp, n_tile),
        out_shape=(
            jax.ShapeDtypeStruct((2, rows, columns), F32),
            jax.ShapeDtypeStruct((rows, columns), F32),
            jax.ShapeDtypeStruct((rows, columns), BF16),
            jax.ShapeDtypeStruct((panels.shape[0], n_grp, rows, columns), BF16),
        ),
        in_specs=vmem(4) + [pl.BlockSpec(memory_space=pltpu.HBM)] * 2,
        out_specs=tuple([pl.BlockSpec(memory_space=pltpu.HBM)] + vmem(3)),
        scratch_shapes=[
            pltpu.VMEM((FIELDS, 2, span, 128), F32),
            pltpu.VMEM((10, span, 256), F32),
            pltpu.VMEM((2, span, 256), F32),
            pltpu.VMEM((3, 2, span, 256), F32),
            pltpu.VMEM((2, 2, span, 128), F32),
            pltpu.VMEM(base_velocity.shape, F32),
            pltpu.VMEM(base_velocity.shape, F32),
            pltpu.SemaphoreType.DMA((1 + n_grp,)),
            pltpu.SemaphoreType.DMA,
        ],
        compiler_params=params,
        name="solve",
    )(ext, pix, odd, even, inputs[0], pltpu.with_memory_space_constraint(panels, pltpu.HBM))

    column = [probe_low] + [
        lax.ppermute(probe_low, "grp", [(i, i ^ k) for i in range(n_grp)]) for k in distances(n_grp)[1:]
    ]
    sums, hessian_probe = pl.pallas_call(
        project_kernel,
        out_shape=(
            jax.ShapeDtypeStruct((panels.shape[0], 8, 128), F32),
            jax.ShapeDtypeStruct((rows, columns), F32),
        ),
        in_specs=vmem(1 + n_grp),
        out_specs=(pl.BlockSpec(memory_space=pltpu.VMEM), pl.BlockSpec(memory_space=pltpu.HBM)),
        scratch_shapes=[pltpu.SemaphoreType.DMA],
        compiler_params=params,
        cost_estimate=pl.CostEstimate(
            flops=2 * panels.size * (n_grp - 1) // n_grp, bytes_accessed=2 * panels.size, transcendentals=0
        ),
        name="project",
    )(panels_near, hess, *column[:-1])
    partial = pl.pallas_call(
        project_last_kernel,
        out_shape=jax.ShapeDtypeStruct((n_grp * n_tile, 1, 128), F32),
        in_specs=vmem(3),
        out_specs=pl.BlockSpec(memory_space=pltpu.VMEM),
        compiler_params=params,
        name="project_last",
    )(panels_near, column[-1], sums)
    everyone = lax.all_to_all(partial, ("grp", "tile"), split_axis=0, concat_axis=0, tiled=True)
    coefficients = pl.pallas_call(
        add_lines_kernel,
        out_shape=jax.ShapeDtypeStruct((1, 128), F32),
        in_specs=vmem(1),
        out_specs=pl.BlockSpec(memory_space=pltpu.VMEM),
        compiler_params=params,
        name="add_lines",
    )(everyone)
    return increment, hessian_probe, coefficients.reshape(128)


def solution(mesh):
    in_specs = (
        P(None, "grp", "tile"),
        P("grp", "tile"),
        P("grp", "tile"),
        P("grp", "tile"),
        P("grp", "tile", None, None),
        P("grp", "tile", None, None),
        P("grp", "tile", None, None),
        P("grp", "tile", None, None),
        P("grp", None, "tile"),
    )
    out_specs = (P(None, "grp", "tile"), P("grp", "tile"), P())
    return jax.shard_map(
        on_device, mesh=mesh, in_specs=in_specs, out_specs=out_specs, check_vma=False
    )
```

```python
import functools

import jax
import jax.numpy as jnp
from jax import lax
from jax.experimental import pallas as pl
from jax.experimental.pallas import tpu as pltpu
from jax.sharding import PartitionSpec as P

SWEEPS = 8
RELAX = 0.8
CAP = 64
HALO = 16
EDGE = 8
FIELDS = 4
STRIPS = 8
F32 = jnp.float32
BF16 = jnp.bfloat16


def lanes(shape=(8, 128)):
    return lax.broadcasted_iota(jnp.int32, shape, len(shape) - 1)


def fetch(sources, targets, sems):
    copies = [pltpu.make_async_copy(s, d, sems.at[i]) for i, (s, d) in enumerate(zip(sources, targets))]
    for copy in copies:
        copy.start()
    return copies


def pack_tiles_kernel(n_tile, *refs):
    sources, (out_ref, fields_ref), targets, sems = refs[:8], refs[8:10], refs[10:18], refs[18]
    copies = fetch(sources, targets, sems)
    bv_ref, visc_ref, fric_ref, fp_ref, los_ref, weight_ref, cell_ref, count_ref = targets
    t = lax.axis_index("tile")
    parity = lax.rem(t, 2)
    rows = visc_ref.shape[0]
    half = rows // 2
    for copy in copies[4:]:
        copy.wait()
    row_lane = lanes((1, 128))
    low = lanes() < CAP
    straight, turned = [], []
    for j in range(n_tile // 2):
        at = pl.ds(j * 128, 128)
        count = jnp.where(
            row_lane < CAP, count_ref[0, 0, :, 2 * j : 2 * j + 1], count_ref[0, 0, :, 2 * j + 1 : 2 * j + 2]
        )
        live = (row_lane & (CAP - 1)) < count
        weight = jnp.where(live, weight_ref[0, 0, :, at], 0.0)
        scaled = jnp.sqrt(weight) * los_ref[0, 0, :, at]
        high = scaled.astype(BF16).astype(F32)
        cell = cell_ref[0, 0, :, at]
        block = jnp.concatenate(
            [
                high, scaled - high,
                lax.shift_right_logical(cell, 7).astype(F32), (cell & 127).astype(F32), jnp.zeros((2, 128), F32),
            ],
            axis=0,
        )
        straight.append(block)
        turned.append(pltpu.roll(block, CAP, 1))
    nothing = jnp.zeros((8, 128), F32)
    in_half = (lanes() // CAP) == parity

    def placed(owner, side):
        if owner < 0 or owner >= n_tile:
            return nothing
        return (straight if owner % 2 == side else turned)[owner // 2]

    for d in range(n_tile):
        solo = jnp.where(parity == d % 2, straight[d // 2], turned[d // 2])
        solo = jnp.where(in_half, solo, 0.0)
        pair = jnp.where(low, placed(d - 1, 0), placed(d + 1, 1))
        out_ref[d, half : half + 16, :] = jnp.concatenate([solo, pair], axis=0).astype(BF16)

    for copy in copies[:4]:
        copy.wait()
    probe = fp_ref[...]
    fields = [-(probe * bv_ref[0]), -(probe * bv_ref[1]), visc_ref[...], fric_ref[...]]
    for f, field in enumerate(fields):
        fields_ref[f] = field
    lane = lanes((half, 128))

    def fold(first_lane):
        packed = jnp.zeros((half, 128), F32)
        for part in range(2):
            for f, field in enumerate(fields):
                start = part * 64 + f * HALO
                piece = field[part * half : (part + 1) * half]
                piece = pltpu.roll(piece, (start - first_lane) % 128, 1)
                packed = jnp.where((lane >= start) & (lane < start + HALO), piece, packed)
        return packed

    out_ref[jnp.minimum(t + 1, n_tile - 1), 0:half, :] = fold(128 - HALO).astype(BF16)
    out_ref[jnp.maximum(t - 1, 0), 0:half, :] = fold(0).astype(BF16)


def pack_rows_kernel(n_tile, fields_ref, got_ref, ext_ref, pix_ref, even_ref, odd_ref):
    g = lax.axis_index("grp")
    t = lax.axis_index("tile")
    rows = fields_ref.shape[1]
    half = rows // 2
    fields = [fields_ref[f] for f in range(FIELDS)]
    lane = lanes((half, 128))
    right = jnp.where(t < n_tile - 1, got_ref[jnp.minimum(t + 1, n_tile - 1), 0:half, :].astype(F32), 0.0)
    left = jnp.where(t > 0, got_ref[jnp.maximum(t - 1, 0), 0:half, :].astype(F32), 0.0)
    band = lanes((HALO, 128))
    edge_up = jnp.zeros((HALO, 128), F32)
    edge_down = jnp.zeros((HALO, 128), F32)
    for f, field in enumerate(fields):
        ext_ref[f, :, 0:128] = field
        edges = []
        for part in range(2):
            start = part * 64 + f * HALO
            edge = jnp.where(
                lane < HALO,
                pltpu.roll(right, (0 - start) % 128, 1),
                jnp.where(lane >= 128 - HALO, pltpu.roll(left, (128 - HALO - start) % 128, 1), 0.0),
            )
            ext_ref[f, part * half : (part + 1) * half, 128:256] = edge
            edges.append(edge)
        here = (band >= 2 * f * HALO) & (band < 2 * (f + 1) * HALO)
        turn = (2 * f + 1) * HALO % 128
        edge_up = jnp.where(here, pltpu.roll(edges[0][0:HALO], turn, 1), edge_up)
        edge_down = jnp.where(here, pltpu.roll(edges[1][half - HALO :], turn, 1), edge_down)
    low = lanes() < CAP
    near, far = [], []
    for s in range(0, n_tile, 2):
        one = got_ref[s, half : half + 16, :].astype(F32)
        two = got_ref[s + 1, half : half + 16, :].astype(F32)
        near.append(jnp.where(low, one[0:8], two[0:8]))
        far += [one[8:16], two[8:16]]
    blocks = near + far
    pixels = jnp.concatenate(
        [b[0:1] + b[2:3] for b in blocks]
        + [b[1:2] + b[3:4] for b in blocks]
        + [b[4:5] for b in blocks]
        + [b[5:6] for b in blocks],
        axis=0,
    )
    pix_ref[...] = pixels
    pixels = pixels.astype(BF16)

    even = lax.rem(g, 2) == 0

    def choose(one, two):
        even_ref_value, odd_ref_value = jnp.where(even, one, two), jnp.where(even, two, one)
        return even_ref_value.astype(BF16), odd_ref_value.astype(BF16)

    for f, field in enumerate(fields):
        at = pl.ds(f * HALO, HALO)
        even_ref[at, :], odd_ref[at, :] = choose(field[rows - HALO :], field[0:HALO])
    at = pl.ds(FIELDS * HALO, HALO)
    even_ref[at, :], odd_ref[at, :] = choose(edge_down, edge_up)
    for ref in (even_ref, odd_ref):
        ref[(FIELDS + 1) * HALO :, :] = pixels


def solve_kernel(
    n_grp, n_tile, ext_ref, pix_ref, odd_ref, even_ref, bv_hbm, panels_hbm,
    inc_hbm, hess_ref, low_ref, panels_ref,
    plane_ref, coef_ref, src_ref, w_ref, nat_ref, bv_ref, inc_ref, sems, inc_sem,
):
    size = panels_ref.shape[2]
    copies = fetch(
        [bv_hbm] + [panels_hbm.at[:, pl.ds(i * size, size), :] for i in range(n_grp)],
        [bv_ref] + [panels_ref.at[:, i] for i in range(n_grp)],
        sems,
    )
    g = lax.axis_index("grp")
    t = lax.axis_index("tile")
    rows = ext_ref.shape[1]
    span = rows + 2 * HALO
    groups = span // STRIPS
    lane = lanes()

    even = lax.rem(g, 2) == 0

    def above(first, size):
        at = pl.ds(first, size)
        got = jnp.where(even, odd_ref[at, :].astype(F32), even_ref[at, :].astype(F32))
        return jnp.where(g > 0, got, 0.0)

    def below(first, size):
        at = pl.ds(first, size)
        got = jnp.where(even, even_ref[at, :].astype(F32), odd_ref[at, :].astype(F32))
        return jnp.where(g < n_grp - 1, got, 0.0)

    first_lane = lane == 0
    last_lane = lane == 127

    band = lanes((HALO, 128))
    for f in range(FIELDS):
        for h in range(2):
            plane_ref[f, h, HALO : HALO + rows, :] = ext_ref[f, :, h * 128 : (h + 1) * 128]
        for load, at in ((above, 0), (below, HALO + rows)):
            plane_ref[f, 0, at : at + HALO, :] = load(f * HALO, HALO)
            edge = pltpu.roll(load(FIELDS * HALO, HALO), (0 - (2 * f + 1) * HALO) % 128, 1)
            plane_ref[f, 1, at : at + HALO, :] = jnp.where((band < HALO) | (band >= 128 - HALO), edge, 0.0)

    def strided(f, h, v):
        return plane_ref[f, h, pl.ds(v, STRIPS, stride=groups), :]

    def beside(pair):
        a, b = pair
        ra, rb = pltpu.roll(a, 1, 1), pltpu.roll(b, 1, 1)
        before = (jnp.where(first_lane, rb, ra), jnp.where(first_lane, ra, rb))
        ra, rb = pltpu.roll(a, 127, 1), pltpu.roll(b, 127, 1)
        after = (jnp.where(last_lane, rb, ra), jnp.where(last_lane, ra, rb))
        return before, pair, after

    def row(load, v):
        if v < 0:
            return beside(tuple(pltpu.roll(load(h, groups - 1), 1, 0) for h in range(2)))
        if v == groups:
            return beside(tuple(pltpu.roll(load(h, 0), STRIPS - 1, 0) for h in range(2)))
        return beside(tuple(load(h, v) for h in range(2)))

    strip = lax.broadcasted_iota(jnp.int32, (8, 128), 0)
    col_in = [
        None,
        ((lane < HALO) & (t < n_tile - 1)) | ((lane >= 128 - HALO) & (t > 0)),
    ]
    load_visc = functools.partial(strided, 2)
    prev, cur = row(load_visc, -1), row(load_visc, 0)
    for v in range(groups):
        nxt = row(load_visc, v + 1)
        place = g * rows - HALO + strip * groups + v
        row_in = (place >= 0) & (place < n_grp * rows)
        at = pl.ds(v * 8, 8)
        for h in range(2):
            centre = cur[1][h]
            east = 0.5 * (centre + nxt[1][h])
            west = 0.5 * (centre + prev[1][h])
            north = 0.5 * (centre + cur[2][h])
            south = 0.5 * (centre + cur[0][h])
            node_pp = 0.25 * (centre + nxt[1][h] + cur[2][h] + nxt[2][h])
            node_mm = 0.25 * (centre + prev[1][h] + cur[0][h] + prev[0][h])
            node_pm = 0.25 * (centre + nxt[1][h] + cur[0][h] + nxt[0][h])
            node_mp = 0.25 * (centre + prev[1][h] + cur[2][h] + prev[2][h])
            fric = strided(3, h, v)
            diag_x = fric + 2.0 * (east + west) + (north + south)
            diag_y = fric + (east + west) + 2.0 * (north + south)
            inside = row_in if col_in[h] is None else row_in & col_in[h]
            inv_x = jnp.where(inside, RELAX / jnp.where(inside, diag_x, 1.0), 0.0)
            inv_y = jnp.where(inside, RELAX / jnp.where(inside, diag_y, 1.0), 0.0)
            cols = pl.ds(h * 128, 128)
            for i, plane in enumerate(
                (east, west, north, south, 0.25 * node_pp, 0.25 * node_mm, 0.25 * node_pm, 0.25 * node_mp, inv_x, inv_y)
            ):
                coef_ref[i, at, cols] = plane
            src_ref[0, at, cols] = inv_x * strided(0, h, v)
            src_ref[1, at, cols] = inv_y * strided(1, h, v)
        prev, cur = cur, nxt

    def natural(h, v):
        return (h, pl.ds(v, STRIPS, stride=groups), slice(None))

    def relax():
        w_ref[0] = src_ref[...]

        def sweep(now, later, start):
            rows_seen = {}

            def both(v):
                if v not in rows_seen:
                    rows_seen[v] = tuple(
                        row(lambda h, u, c=c: now[c, pl.ds(u * 8, 8), pl.ds(h * 128, 128)], v) for c in range(2)
                    )
                return rows_seen[v]

            for p in range(groups):
                v = (p + start) % groups
                prev, cur, nxt = both(v - 1), both(v), both(v + 1)
                at = pl.ds(v * 8, 8)
                for h in range(2):
                    cols = pl.ds(h * 128, 128)
                    east, west, north, south, pp, mm, pm, mp, inv_x, inv_y = (
                        coef_ref[i, at, cols] for i in range(10)
                    )

                    def along(c):
                        return (
                            east * nxt[c][1][h] + west * prev[c][1][h],
                            north * cur[c][2][h] + south * cur[c][0][h],
                        )

                    def cross(c):
                        return (
                            pp * nxt[c][2][h] + mm * prev[c][0][h] - pm * nxt[c][0][h] - mp * prev[c][2][h]
                        )

                    one, two = along(0)
                    sum_x = 2.0 * one + two + cross(1)
                    one, two = along(1)
                    sum_y = one + 2.0 * two + cross(0)
                    for c, new in ((0, inv_x * sum_x), (1, inv_y * sum_y)):
                        new = (1.0 - RELAX) * cur[c][1][h] + src_ref[c, at, cols] + new
                        if later is None:
                            nat_ref[(c,) + natural(h, v)] = new
                        else:
                            later[c, at, cols] = new

        def three_sweeps(_, carry):
            for k in range(3):
                sweep(w_ref.at[k], w_ref.at[(k + 1) % 3], k)
            return carry

        lax.fori_loop(0, (SWEEPS - 2) // 3, three_sweeps, 0)
        sweep(w_ref.at[0], None, 0)

    def solve(phase, carry):
        relax()

        @pl.when(phase == 0)
        def _():
            for c in range(2):
                inc_ref[c] = nat_ref[c, 0, HALO : HALO + rows, :]
            pltpu.make_async_copy(inc_ref, inc_hbm, inc_sem).start()
            misfit()

        return carry

    def misfit():
        n_near, n_all = n_tile // 2, 3 * n_tile // 2
        low = lanes((n_tile, 128)) < CAP
        spans = ((0, HALO, rows), (-1, HALO - EDGE, EDGE), (1, HALO + rows, EDGE))

        def exact(h, delta):
            return h == 0 and delta == 0

        jobs = []
        for delta, first, size in spans:
            if delta == 0:
                values = pix_ref[...]
            else:
                base = (FIELDS + 1) * HALO
                values = (above if delta < 0 else below)(base, 4 * n_all)
            los_x, los_y, r, c = (values[q * n_all : (q + 1) * n_all] for q in range(4))
            if delta < 0:
                r = r - (rows - EDGE)
            in_rim = c[n_near:] + jnp.where(low, float(EDGE) - 128.0, float(EDGE))
            for h, begin, count, lane_of in ((0, 0, n_near, c[0:n_near]), (1, n_near, n_tile, in_rim)):
                parts = []
                for comp in range(2):
                    part = nat_ref[comp, h, first : first + size, :]
                    parts.append(part if h == 0 else pltpu.roll(part, EDGE, 1))
                field = jnp.concatenate(parts, axis=0)
                stacked = field.astype(BF16)
                if exact(h, delta):
                    rest = (field - stacked.astype(F32)).astype(BF16)
                    stacked = jnp.concatenate([stacked, rest], axis=1)
                jobs.append((exact(h, delta), h, first, size, begin, count, lane_of, los_x, los_y, r, stacked))

        nat_ref[...] = jnp.zeros_like(nat_ref)
        for two_parts, h, first, size, begin, count, lane_of, los_x, los_y, r, stacked in jobs:
            chunk = 4
            depth = 128 if h == 0 else 2 * EDGE
            wide = chunk * 128
            row_id = lax.broadcasted_iota(jnp.int32, (size, wide), 0).astype(F32)
            lane_id = lax.broadcasted_iota(jnp.int32, (depth, wide), 0).astype(F32)
            total = jnp.zeros(((4 if two_parts else 2) * size, 128), F32)
            for j in range(0, count, chunk):

                def line(table, offset):
                    return jnp.concatenate([table[offset + i : offset + i + 1] for i in range(j, j + chunk)], axis=1)

                line_x, line_y = line(los_x, begin), line(los_y, begin)
                hot = jnp.where(lane_id == line(lane_of, 0), 1.0, 0.0).astype(BF16)
                here = row_id == line(r, begin)
                if h == 1:
                    hot = jnp.concatenate([hot, jnp.zeros((128 - depth, wide), BF16)], axis=0)
                twice = jnp.concatenate([hot, hot], axis=0) if two_parts else hot
                got = jnp.dot(stacked, twice, preferred_element_type=F32)
                got_x = jnp.sum(jnp.where(here, got[0:size], 0.0), axis=0, keepdims=True)
                got_y = jnp.sum(jnp.where(here, got[size:], 0.0), axis=0, keepdims=True)
                amount = line_x * got_x + line_y * got_y
                terms = [amount * line_x, amount * line_y]
                if two_parts:
                    highs = [p.astype(BF16).astype(F32) for p in terms]
                    terms = highs + [p - q for p, q in zip(terms, highs)]
                spread = jnp.concatenate([jnp.where(here, p, 0.0) for p in terms], axis=0).astype(BF16)
                total = total + lax.dot_general(spread, hot, (((1,), (1,)), ((), ())), preferred_element_type=F32)
            if two_parts:
                total = total[0 : 2 * size] + total[2 * size :]
            if h == 1:
                total = pltpu.roll(total, 128 - EDGE, 1)
            for c in range(2):
                nat_ref[c, h, first : first + size, :] = total[c * size : (c + 1) * size]

        for v in range(groups):
            at = pl.ds(v * 8, 8)
            for h in range(2):
                cols = pl.ds(h * 128, 128)
                for c in range(2):
                    src_ref[c, at, cols] = coef_ref[8 + c, at, cols] * nat_ref[(c,) + natural(h, v)]

    lax.fori_loop(0, 2, solve, 0)
    for copy in copies:
        copy.wait()
    pltpu.make_async_copy(inc_ref, inc_hbm, inc_sem).wait()
    hess = -(bv_ref[0] * nat_ref[0, 0, HALO : HALO + rows, :] + bv_ref[1] * nat_ref[1, 0, HALO : HALO + rows, :])
    hess_ref[...] = hess
    low_ref[...] = hess.astype(BF16)


def distances(n_grp):
    return [0] + list(range(2, n_grp)) + [1]


def project_block(panels_ref, probe_ref, k, distance):
    count, n_grp, rows, columns = panels_ref.shape
    product = panels_ref[k, lax.axis_index("grp") ^ distance].astype(F32) * probe_ref[...].astype(F32)
    return jnp.sum(product.reshape(-1, 8, columns), axis=0)


def project_kernel(panels_ref, hess_ref, *refs):
    blocks, (sums_ref, hess_hbm, sem) = refs[:-3], refs[-3:]
    copy = pltpu.make_async_copy(hess_ref, hess_hbm, sem)
    copy.start()
    order = distances(panels_ref.shape[1])
    for k in range(panels_ref.shape[0]):
        sums_ref[k] = sum(project_block(panels_ref, block, k, i) for i, block in zip(order, blocks))
    copy.wait()


def project_last_kernel(panels_ref, block_ref, sums_ref, out_ref):
    count, n_grp = panels_ref.shape[:2]
    sums = []
    for k in range(count):
        total = sums_ref[k] + project_block(panels_ref, block_ref, k, distances(n_grp)[-1])
        sums.append(jnp.sum(total, axis=0, keepdims=True))
    sums.append(jnp.zeros((128 - count, 128), F32))
    table = jnp.concatenate(sums, axis=0)
    high = table.astype(BF16)
    parts = jnp.concatenate([high, (table - high.astype(F32)).astype(BF16)], axis=1)
    line = lax.dot_general(
        jnp.ones((16, 256), BF16), parts, (((1,), (1,)), ((), ())), preferred_element_type=F32
    )
    line = pltpu.roll(line, lax.axis_index("grp") * count, 1)[0:1]
    out_ref[...] = jnp.broadcast_to(line[None], out_ref.shape)


def add_lines_kernel(lines_ref, out_ref):
    out_ref[...] = jnp.sum(lines_ref[...], axis=0)


def vmem(n):
    return [pl.BlockSpec(memory_space=pltpu.VMEM)] * n


def on_device(
    base_velocity, viscosity, friction, friction_probe, pixel_los, pixel_weight, pixel_cell, pixel_count, panels
):
    n_grp, n_tile = lax.axis_size("grp"), lax.axis_size("tile")
    rows, columns = viscosity.shape
    half = rows // 2
    span = rows + 2 * HALO
    params = pltpu.CompilerParams(vmem_limit_bytes=32 * 2**20)

    inputs = [
        pltpu.with_memory_space_constraint(x, pltpu.HBM)
        for x in (
            base_velocity, viscosity, friction, friction_probe, pixel_los, pixel_weight, pixel_cell, pixel_count
        )
    ]
    slots, fields = pl.pallas_call(
        functools.partial(pack_tiles_kernel, n_tile),
        out_shape=(
            jax.ShapeDtypeStruct((n_tile, half + 16, 128), BF16),
            jax.ShapeDtypeStruct((FIELDS, rows, columns), F32),
        ),
        in_specs=[pl.BlockSpec(memory_space=pltpu.HBM)] * len(inputs),
        out_specs=tuple(vmem(2)),
        scratch_shapes=[pltpu.VMEM(x.shape, x.dtype) for x in inputs] + [pltpu.SemaphoreType.DMA((len(inputs),))],
        compiler_params=params,
        name="pack_tiles",
    )(*inputs)
    got = lax.all_to_all(slots, "tile", split_axis=0, concat_axis=0, tiled=True)

    packet = (FIELDS + 1) * HALO + 6 * n_tile
    ext, pix, even, odd = pl.pallas_call(
        functools.partial(pack_rows_kernel, n_tile),
        out_shape=(
            jax.ShapeDtypeStruct((FIELDS, rows, 256), F32),
            jax.ShapeDtypeStruct((6 * n_tile, 128), F32),
            jax.ShapeDtypeStruct((packet, 128), BF16),
            jax.ShapeDtypeStruct((packet, 128), BF16),
        ),
        in_specs=vmem(2),
        out_specs=tuple(vmem(4)),
        compiler_params=params,
        name="pack_rows",
    )(fields, got)
    even = lax.ppermute(even, "grp", [(i, i ^ 1) for i in range(n_grp)])
    odd = lax.ppermute(odd, "grp", [(i, (i - 1 + 2 * (i % 2)) % n_grp) for i in range(n_grp)])

    increment, hess, probe_low, panels_near = pl.pallas_call(
        functools.partial(solve_kernel, n_grp, n_tile),
        out_shape=(
            jax.ShapeDtypeStruct((2, rows, columns), F32),
            jax.ShapeDtypeStruct((rows, columns), F32),
            jax.ShapeDtypeStruct((rows, columns), BF16),
            jax.ShapeDtypeStruct((panels.shape[0], n_grp, rows, columns), BF16),
        ),
        in_specs=vmem(4) + [pl.BlockSpec(memory_space=pltpu.HBM)] * 2,
        out_specs=tuple([pl.BlockSpec(memory_space=pltpu.HBM)] + vmem(3)),
        scratch_shapes=[
            pltpu.VMEM((FIELDS, 2, span, 128), F32),
            pltpu.VMEM((10, span, 256), F32),
            pltpu.VMEM((2, span, 256), F32),
            pltpu.VMEM((3, 2, span, 256), F32),
            pltpu.VMEM((2, 2, span, 128), F32),
            pltpu.VMEM(base_velocity.shape, F32),
            pltpu.VMEM(base_velocity.shape, F32),
            pltpu.SemaphoreType.DMA((1 + n_grp,)),
            pltpu.SemaphoreType.DMA,
        ],
        compiler_params=params,
        name="solve",
    )(ext, pix, odd, even, inputs[0], pltpu.with_memory_space_constraint(panels, pltpu.HBM))

    column = [probe_low] + [
        lax.ppermute(probe_low, "grp", [(i, i ^ k) for i in range(n_grp)]) for k in distances(n_grp)[1:]
    ]
    sums, hessian_probe = pl.pallas_call(
        project_kernel,
        out_shape=(
            jax.ShapeDtypeStruct((panels.shape[0], 8, 128), F32),
            jax.ShapeDtypeStruct((rows, columns), F32),
        ),
        in_specs=vmem(1 + n_grp),
        out_specs=(pl.BlockSpec(memory_space=pltpu.VMEM), pl.BlockSpec(memory_space=pltpu.HBM)),
        scratch_shapes=[pltpu.SemaphoreType.DMA],
        compiler_params=params,
        cost_estimate=pl.CostEstimate(
            flops=2 * panels.size * (n_grp - 1) // n_grp, bytes_accessed=2 * panels.size, transcendentals=0
        ),
        name="project",
    )(panels_near, hess, *column[:-1])
    partial = pl.pallas_call(
        project_last_kernel,
        out_shape=jax.ShapeDtypeStruct((n_grp * n_tile, 1, 128), F32),
        in_specs=vmem(3),
        out_specs=pl.BlockSpec(memory_space=pltpu.VMEM),
        compiler_params=params,
        name="project_last",
    )(panels_near, column[-1], sums)
    everyone = lax.all_to_all(partial, ("grp", "tile"), split_axis=0, concat_axis=0, tiled=True)
    coefficients = pl.pallas_call(
        add_lines_kernel,
        out_shape=jax.ShapeDtypeStruct((1, 128), F32),
        in_specs=vmem(1),
        out_specs=pl.BlockSpec(memory_space=pltpu.VMEM),
        compiler_params=params,
        name="add_lines",
    )(everyone)
    return increment, hessian_probe, coefficients.reshape(128)


def solution(mesh):
    in_specs = (
        P(None, "grp", "tile"),
        P("grp", "tile"),
        P("grp", "tile"),
        P("grp", "tile"),
        P("grp", "tile", None, None),
        P("grp", "tile", None, None),
        P("grp", "tile", None, None),
        P("grp", "tile", None, None),
        P("grp", None, "tile"),
    )
    out_specs = (P(None, "grp", "tile"), P("grp", "tile"), P())
    return jax.shard_map(
        on_device, mesh=mesh, in_specs=in_specs, out_specs=out_specs, check_vma=False
    )
```
